256 devices in a mesh: dp: 4 (over y), gx: 16 (over z, x_hi), gy: 4 (over x_lo, core).
Axes of the slice: x: 4 (x_hi: 2, x_lo: 2; x = x_hi * 2 + x_lo), y: 4, z: 8, core: 2. Of those that a mesh axis runs over, the one named last changes fastest.
Arguments:
- tokens: bfloat16 [4, 32, 32, 32, 256], P('dp', 'gx', 'gy'), may hold values from -120 to 120
- attn: bfloat16 [4, 32, 32, 32, 256], P('dp', 'gx', 'gy'), may hold values from -6 to 6
- cotangent: bfloat16 [4, 32, 32, 32, 256], P('dp', 'gx', 'gy'), may hold values from -6 to 6
- gain: float32 [256], replicated, may hold values from 0.25 to 1.75
- w_qkv: bfloat16 [256, 768], replicated, may hold values from -0.26796875 to 0.26796875
- w_out: bfloat16 [256, 256], replicated, may hold values from -0.375 to 0.375
Outputs:
- d_tokens: bfloat16 [4, 32, 32, 32, 256], P('dp', 'gx', 'gy')
- d_w_qkv: float32 [256, 768], replicated
- d_w_out: float32 [256, 256], replicated
- d_gain: float32 [256], replicated
The draws below stay inside these ranges and needn't reach their ends.
All inputs are finite; a program needn't handle non-finite values.
Results may differ from the reference program's by a relative error of at most 0.012.
The reference program's roundings to bfloat16 on the way count: a program that leaves them out, or rounds other values in their place, can miss the bound.
Values may be sent and summed in bfloat16 or wider, within the bound.
No kernel may reach another device: no remote copies, remote signals or barrier semaphores. Data moves between devices by JAX's collectives and lax.ppermute only.
A program may use at most 64 MiB of HBM per device.

```python
import math
import jax
import jax.numpy as jnp
from jax import lax

C = 256
HEADS = 8
Z = 32
VOLS = 4
X = 32
Y = 32


def draw_tokens(key, part):
    key = jax.random.fold_in(key, 1)
    keys = jax.random.split(key, 3)
    shape = (VOLS, X, Y, Z, C)
    lead = (VOLS, X, Y, Z, 1)
    rows = jnp.exp(jax.random.uniform(keys[0], lead, jnp.float32, 0.0, math.log(10.0)))
    chans = jnp.exp(jax.random.uniform(keys[1], (C,), jnp.float32, math.log(0.5), math.log(2.0)))
    base = jnp.clip(jax.random.normal(keys[2], shape, jnp.float32), -5.0, 5.0)
    values = base * chans * rows
    return values.astype(jnp.bfloat16)


def draw_w_qkv(key, part):
    key = jax.random.fold_in(key, 2)
    base = jnp.clip(jax.random.normal(key, (C, 3 * C), jnp.float32), -3.0, 3.0) * C ** (-0.5)
    values = base
    return values.astype(jnp.bfloat16)


def steps_of(key, extent, pieces, low, top_value):
    level, own = 1.0, jax.random.fold_in(key, 6)
    for axis_at, blocks in pieces:
        heights = jnp.exp(jax.random.uniform(jax.random.fold_in(own, axis_at), (blocks,), jnp.float32, low / len(pieces), top_value / len(pieces)))
        level = level * jnp.repeat(heights, extent[axis_at] // blocks).reshape([-1 if axis == axis_at else 1 for axis in range(len(extent))])
    return level


def gaussian(key, dims, scale, bound, cuts=(), held_as=jnp.bfloat16):
    values = scale * jax.random.normal(key, dims, jnp.float32)
    if cuts:
        values = values * steps_of(key, dims, cuts, -0.22, 0.18)
    return jnp.clip(values, -bound, bound).astype(held_as)


def setup_inputs(seed: int = 0) -> dict:
    streams_of = jax.random.split(jax.random.key(seed), 7)
    return {
        "tokens": draw_tokens(jax.random.fold_in(streams_of[6], 71), 0),
        "attn": gaussian(streams_of[1], (VOLS, X, Y, Z, C), 1.0, 6.0, ((0, 4), (1, 16), (2, 4))),
        "cotangent": gaussian(streams_of[2], (VOLS, X, Y, Z, C), 1.0, 6.0, ((0, 4), (1, 16), (2, 4))),
        "gain": jnp.clip(1.0 + 0.15 * jax.random.normal(streams_of[3], (C,), jnp.float32), 0.25, 1.75),
        "w_qkv": draw_w_qkv(jax.random.fold_in(streams_of[6], 71), 0),
        "w_out": gaussian(streams_of[5], (C, C), C ** -0.5, 0.375),
    }


EPSILON = 1e-06

def pencil_grads(linear, grad_attn):
    batch, length, width = grad_attn.shape
    head_size = width // HEADS
    factor = 1.0 / math.sqrt(head_size)
    query = linear[..., :width].astype(jnp.float32).reshape(batch, length, HEADS, head_size)
    keys_h = linear[..., width:2 * width].astype(jnp.float32).reshape(batch, length, HEADS, head_size)
    values_h = linear[..., 2 * width:].astype(jnp.float32).reshape(batch, length, HEADS, head_size)
    grad_h = grad_attn.astype(jnp.float32).reshape(batch, length, HEADS, head_size)
    high = lax.Precision.HIGHEST
    scores = jnp.einsum('blhd,bmhd->bhlm', query, keys_h, precision=high) * factor
    probs = jax.nn.softmax(scores, axis=-1)
    probs_low = lax.optimization_barrier(probs.astype(jnp.bfloat16)).astype(jnp.float32)
    grad_values = jnp.einsum('bhlm,blhd->bmhd', probs_low, grad_h, precision=high)
    grad_probs = jnp.einsum('blhd,bmhd->bhlm', grad_h, values_h, precision=high)
    grad_scores = probs * (grad_probs - lax.optimization_barrier(jnp.sum(probs * grad_probs, axis=-1, keepdims=True)))
    scores_low = lax.optimization_barrier(grad_scores.astype(jnp.bfloat16)).astype(jnp.float32)
    grad_query = jnp.einsum('bhlm,bmhd->blhd', scores_low, keys_h, precision=high) * factor
    grad_keys = jnp.einsum('bhlm,blhd->bmhd', scores_low, query, precision=high) * factor
    joined = jnp.concatenate([grad_query.reshape(batch, length, width), grad_keys.reshape(batch, length, width), grad_values.reshape(batch, length, width)], axis=-1)
    return joined.astype(jnp.bfloat16)

def mapped_grads(linear, grad_attn):
    return lax.map(lambda pair: pencil_grads(pair[0], pair[1]), (linear, grad_attn))

def volume_grads(volume, saved, upstream, gain, w_qkv, w_out):
    tokens_f = volume.astype(jnp.float32)
    root = jnp.sqrt(lax.optimization_barrier(jnp.mean(tokens_f * tokens_f, axis=-1, keepdims=True)) + EPSILON)
    normed = (tokens_f / root * gain).astype(jnp.bfloat16)
    flat_normed = normed.reshape(-1, C)
    qkv = jnp.dot(flat_normed, w_qkv, preferred_element_type=jnp.float32).astype(jnp.bfloat16).reshape(X, Y, Z, 3 * C)
    flat_up = upstream.reshape(-1, C)
    grad_attn = jnp.dot(flat_up, w_out.T, preferred_element_type=jnp.float32).astype(jnp.bfloat16).reshape(X, Y, Z, C)
    grad_third = mapped_grads(qkv, grad_attn)
    first_qkv = qkv.transpose(1, 2, 0, 3)
    first_grad = grad_attn.transpose(1, 2, 0, 3)
    grad_first = mapped_grads(first_qkv, first_grad).transpose(2, 0, 1, 3)
    second_qkv = qkv.transpose(0, 2, 1, 3)
    second_grad = grad_attn.transpose(0, 2, 1, 3)
    grad_second = mapped_grads(second_qkv, second_grad).transpose(0, 2, 1, 3)
    part_qkv = jnp.zeros((C, 3 * C), jnp.float32)
    grad_normed = jnp.zeros((X * Y * Z, C), jnp.float32)
    for each in (grad_third, grad_first, grad_second):
        flat_grad = each.reshape(-1, 3 * C)
        part_qkv = part_qkv + jnp.dot(flat_normed.T, flat_grad, preferred_element_type=jnp.float32)
        grad_normed = grad_normed + jnp.dot(flat_grad, w_qkv.T, preferred_element_type=jnp.float32)
    part_out = jnp.dot(saved.reshape(-1, C).T, flat_up, preferred_element_type=jnp.float32)
    flat_tokens = tokens_f.reshape(-1, C)
    flat_root = root.reshape(-1, 1)
    part_gain = lax.optimization_barrier(jnp.sum(grad_normed * flat_tokens / flat_root, axis=0))
    gained = gain * grad_normed
    inner = lax.optimization_barrier(jnp.sum(gained * flat_tokens, axis=-1, keepdims=True))
    result = gained / flat_root - flat_tokens * inner / (C * flat_root ** 3)
    return (result.astype(jnp.bfloat16).reshape(X, Y, Z, C), part_qkv, part_out, part_gain)

def reference(tokens, attn, cotangent, gain, w_qkv, w_out):

    def one_volume(triple):
        return volume_grads(triple[0], triple[1], triple[2], gain, w_qkv, w_out)
    d_tokens, parts_qkv, parts_out, parts_gain = lax.map(one_volume, (tokens, attn, cotangent))
    scale = 1.0 / math.sqrt(VOLS * X * Y * Z)
    d_w_qkv = lax.optimization_barrier(jnp.sum(parts_qkv, axis=0)) * scale
    d_w_out = lax.optimization_barrier(jnp.sum(parts_out, axis=0)) * scale
    d_gain = lax.optimization_barrier(jnp.sum(parts_gain, axis=0)) * scale
    return (d_tokens, d_w_qkv, d_w_out, d_gain)
```

```python
import functools
import math

import jax
import jax.numpy as jnp
from jax import lax
from jax.experimental import pallas as pl
from jax.experimental.pallas import tpu as pltpu
from jax.sharding import Mesh
from jax.sharding import PartitionSpec as P

HEADS = 8
HEAD = 32
WIDTH = 256
TRIPLE = 3 * WIDTH
EPSILON = 1e-06
FACTOR = 1.0 / math.sqrt(HEAD)
TOKENS = 512
LENGTH = 32
PENCILS = 16
ROWS = 16
LANES = 128
TILES = 64
BF16 = jnp.bfloat16
F32 = jnp.float32
VMEM = pl.BlockSpec(memory_space=pltpu.VMEM)
SMEM = pl.BlockSpec(memory_space=pltpu.SMEM)
PLANE = ("y", "xh", "xl")
FIRST = ("z", "xh")
SECOND = ("xl", "c")


def params():
    return pltpu.CompilerParams(vmem_limit_bytes=48 * 2**20)


def cost(us):
    return pl.CostEstimate(
        flops=int(us * 8e8), bytes_accessed=int(us * 2e6), transcendentals=0
    )


def dot(left, right, left_dim, right_dim):
    return lax.dot_general(
        left, right, (((left_dim,), (right_dim,)), ((), ())), preferred_element_type=F32
    )


def wide(ref, first, rows):
    return jnp.concatenate([ref[first, rows, :], ref[first + 1, rows, :]], axis=1).astype(BF16)


def attention(proj, grads, rows_of, block, lane):
    q = [wide(proj, 0, rows) for rows in rows_of]
    k = [wide(proj, 2, rows) for rows in rows_of]
    v = [wide(proj, 4, rows) for rows in rows_of]
    g = [wide(proj, 6, rows) for rows in rows_of]
    lows = []
    for i, rows in enumerate(rows_of):
        q_block = jnp.concatenate([q[i]] * HEADS, axis=0) * block
        g_block = jnp.concatenate([g[i]] * HEADS, axis=0) * block
        scores = dot(k[i], q_block, 1, 1)
        grad_probs = dot(v[i], g_block, 1, 1)
        top = jnp.max(scores, axis=0, keepdims=True)
        powers = jnp.exp((scores - top) * FACTOR)
        probs = powers * (1.0 / jnp.sum(powers, axis=0, keepdims=True))
        inner = jnp.sum(probs * grad_probs, axis=0, keepdims=True)
        low = (probs * (grad_probs - inner)).astype(BF16)
        grad_v = dot(probs.astype(BF16), g_block, 1, 0)
        grad_k = dot(low, q_block, 1, 0) * FACTOR
        for half in range(2):
            cols = slice(half * LANES, (half + 1) * LANES)
            grads[2 + half, rows, :] = grad_k[:, cols]
            grads[4 + half, rows, :] = grad_v[:, cols]
        lows.append(low)
    stacked = jnp.concatenate(lows, axis=0)
    for half in range(2):
        cols = slice(half * LANES, (half + 1) * LANES)
        turned = stacked[:, cols].T
        for i, rows in enumerate(rows_of):
            every = dot(turned[:, i * LENGTH : (i + 1) * LENGTH], k[i][:, cols], 1, 0)
            picked = every[96:128]
            for head in (2, 1, 0):
                picked = jnp.where(
                    lane < HEAD * (head + 1), every[head * 32 : head * 32 + 32], picked
                )
            grads[half, rows, :] = picked * FACTOR


def axis_grads(tokens, cotangent, gain, w_qkv, w_out, proj, grads, strided):
    tokens_f = tokens.astype(F32)
    root = jnp.sqrt(jnp.mean(tokens_f * tokens_f, axis=-1, keepdims=True) + EPSILON)
    unit = tokens_f / root
    normed = (unit * gain).astype(BF16)
    qkv = dot(normed, w_qkv, 1, 0)
    for col in range(6):
        proj[col] = qkv[:, col * LANES : (col + 1) * LANES]
    grad_attn = dot(cotangent, w_out, 1, 1)
    for col in range(2):
        proj[6 + col] = grad_attn[:, col * LANES : (col + 1) * LANES]
    shape = (WIDTH, WIDTH)
    block = (
        lax.broadcasted_iota(jnp.int32, shape, 0) // HEAD
        == lax.broadcasted_iota(jnp.int32, shape, 1) // HEAD
    )
    block = block.astype(F32).astype(BF16)
    lane = lax.broadcasted_iota(jnp.int32, (LENGTH, LANES), 1)
    for base in range(0, PENCILS, 4):
        if strided:
            rows_of = [pl.ds(base + i, LENGTH, stride=PENCILS) for i in range(4)]
        else:
            rows_of = [pl.ds((base + i) * LENGTH, LENGTH) for i in range(4)]
        attention(proj, grads, rows_of, block, lane)
    joined = jnp.concatenate([grads[col].astype(BF16) for col in range(6)], axis=1)
    grad_normed = dot(joined, w_qkv, 1, 1)
    part_qkv = dot(normed, joined, 0, 0)
    part_gain = jnp.sum(grad_normed * unit, axis=0, keepdims=True)
    return grad_normed, part_qkv, part_gain


SCRATCH = [
    pltpu.VMEM((8, TOKENS, LANES), F32),
    pltpu.VMEM((6, TOKENS, LANES), F32),
]


def prepare_kernel(tokens, cotangent, to_first, to_second):
    for kind, ref in enumerate((tokens, cotangent)):
        for x in range(2):
            for y in range(8):
                for z in range(2):
                    rows = ref[x, y, z * ROWS : (z + 1) * ROWS, :]
                    to_first[y * 2 + z, kind, x] = rows
                    to_second[x * 2 + z, kind, y] = rows


def third_kernel(
    tokens, cotangent, attn, gain, w_qkv, w_out, normed_out, qkv_out, out_out, gain_out, proj, grads
):
    cot = cotangent[...]
    grad_normed, part_qkv, part_gain = axis_grads(
        tokens[...], cot, gain[...], w_qkv[...], w_out[...], proj, grads, False
    )
    normed_out[...] = grad_normed
    qkv_out[...] = part_qkv
    gain_out[...] = part_gain
    out_out[...] = dot(attn[...], cot, 0, 0)


def second_kernel(
    pieces, gain, w_qkv, w_out, qkv_in, gain_in, back, qkv_out, gain_out, proj, grads
):
    tokens = pieces[:, 0].reshape(TOKENS, WIDTH)
    cot = pieces[:, 1].reshape(TOKENS, WIDTH)
    grad_normed, part_qkv, part_gain = axis_grads(
        tokens, cot, gain[...], w_qkv[...], w_out[...], proj, grads, True
    )
    back[...] = grad_normed.astype(BF16).reshape(back.shape)
    qkv_out[...] = qkv_in[...] + part_qkv
    gain_out[...] = gain_in[...] + part_gain


def first_kernel(
    core,
    pieces,
    gain,
    w_qkv,
    w_out,
    qkv_in,
    out_in,
    gain_in,
    back,
    own,
    other,
    proj,
    grads,
    halves,
):
    tokens = pieces[:, 0].reshape(TOKENS, WIDTH)
    cot = pieces[:, 1].reshape(TOKENS, WIDTH)
    grad_normed, part_qkv, part_gain = axis_grads(
        tokens, cot, gain[...], w_qkv[...], w_out[...], proj, grads, True
    )
    back[...] = grad_normed.astype(BF16).reshape(back.shape)
    total = qkv_in[...] + part_qkv
    for at in range(2 * TILES):
        half, tile = divmod(at, TILES)
        if at < 96:
            row, col = divmod(at, 6)
            halves[half, tile] = total[row * 16 : row * 16 + 16, col * LANES : (col + 1) * LANES]
        else:
            row, col = divmod(at - 96, 2)
            halves[half, tile] = out_in[row * 16 : row * 16 + 16, col * LANES : (col + 1) * LANES]
    mine = core[0]
    own[0:TILES] = halves[mine]
    other[0:TILES] = halves[1 - mine]
    part_gain = gain_in[...] + part_gain
    gains = jnp.concatenate(
        [part_gain[:, :LANES], part_gain[:, LANES:], jnp.zeros((14, LANES), F32)], axis=0
    )
    own[TILES] = gains
    other[TILES] = gains


def pair_kernel(own, received, pieces):
    for peer in range(16):
        tiles = slice(peer * 4, peer * 4 + 4)
        pieces[peer, 0:4] = (own[tiles] + received[tiles]).astype(BF16)
    gains = (own[TILES] + received[TILES]).astype(BF16)
    for peer in range(16):
        pieces[peer, 4] = gains


def plane_kernel(received, pieces):
    total = jnp.sum(received[...].astype(F32), axis=0).astype(BF16)
    for peer in range(8):
        pieces[peer] = total


def line_kernel(scale, received, pieces, gain_out):
    total = jnp.sum(received[...].astype(F32), axis=0) * scale
    low = total[0:4].astype(BF16)
    for peer in range(16):
        pieces[peer] = low
    gain_out[...] = jnp.concatenate([total[4, 0:1], total[4, 1:2]], axis=1)


def assemble_kernel(core, mine, theirs, w_qkv_out, w_out_out, halves):
    at_core = core[0]
    halves[at_core] = mine[...]
    halves[1 - at_core] = theirs[...]
    for at in range(2 * TILES):
        half, tile = divmod(at, TILES)
        rows = halves[half, tile].astype(F32)
        if at < 96:
            row, col = divmod(at, 6)
            w_qkv_out[row * 16 : row * 16 + 16, col * LANES : (col + 1) * LANES] = rows
        else:
            row, col = divmod(at - 96, 2)
            w_out_out[row * 16 : row * 16 + 16, col * LANES : (col + 1) * LANES] = rows


def tokens_kernel(tokens, gain, third, from_first, from_second, out):
    for x in range(2):
        for y in range(8):
            tokens_f = tokens[x, y].astype(F32)
            first = jnp.concatenate([from_first[y * 2, x], from_first[y * 2 + 1, x]], axis=0)
            second = jnp.concatenate([from_second[x * 2, y], from_second[x * 2 + 1, y]], axis=0)
            grad_normed = third[x, y] + first.astype(F32) + second.astype(F32)
            square = jnp.mean(tokens_f * tokens_f, axis=-1, keepdims=True) + EPSILON
            root = jnp.sqrt(square)
            gained = gain[...] * grad_normed
            inner = jnp.sum(gained * tokens_f, axis=-1, keepdims=True)
            result = gained / root - tokens_f * (inner / (WIDTH * root * square))
            out[x, y] = result.astype(BF16)


def shape(dims, dtype):
    return jax.ShapeDtypeStruct(dims, dtype)


def kernel_call(body, outs, operands, us, scratch=(), scalars=0):
    return pl.pallas_call(
        body,
        out_shape=outs,
        in_specs=[SMEM] * scalars + [VMEM] * (len(operands) - scalars),
        out_specs=jax.tree.map(lambda _: VMEM, outs),
        scratch_shapes=list(scratch),
        compiler_params=params(),
        cost_estimate=cost(us),
    )(*operands)


def exchange(pieces, axes):
    return lax.all_to_all(pieces, axes, split_axis=0, concat_axis=0, tiled=True)


def on_device(count, tokens, attn, cotangent, gain, w_qkv, w_out):
    core = lax.axis_index("c").astype(jnp.int32).reshape(1)
    gain_row = gain.reshape(1, WIDTH)
    local = tokens[0]
    upstream = cotangent[0]
    to_first, to_second = kernel_call(
        prepare_kernel,
        (shape((16, 2, 2, ROWS, WIDTH), BF16), shape((4, 2, 8, ROWS, WIDTH), BF16)),
        (local, upstream),
        2,
    )
    at_first = exchange(to_first, FIRST)
    at_second = exchange(to_second, SECOND)
    flat = (TOKENS, WIDTH)
    third, part_qkv, part_out, part_gain = kernel_call(
        third_kernel,
        (
            shape(flat, F32),
            shape((WIDTH, TRIPLE), F32),
            shape((WIDTH, WIDTH), F32),
            shape((1, WIDTH), F32),
        ),
        (local.reshape(flat), upstream.reshape(flat), attn.reshape(flat), gain_row, w_qkv, w_out),
        7,
        SCRATCH,
    )
    back_second, part_qkv, part_gain = kernel_call(
        second_kernel,
        (
            shape((4, 8, ROWS, WIDTH), BF16),
            shape((WIDTH, TRIPLE), F32),
            shape((1, WIDTH), F32),
        ),
        (at_second, gain_row, w_qkv, w_out, part_qkv, part_gain),
        7,
        SCRATCH,
    )
    from_second = exchange(back_second, SECOND)
    tile = (16, LANES)
    back_first, own, other = kernel_call(
        first_kernel,
        (
            shape((16, 2, ROWS, WIDTH), BF16),
            shape((TILES + 1, *tile), F32),
            shape((TILES + 1, *tile), F32),
        ),
        (core, at_first, gain_row, w_qkv, w_out, part_qkv, part_out, part_gain),
        7,
        SCRATCH + [pltpu.VMEM((2, TILES, *tile), F32)],
        1,
    )
    swap = [(0, 1), (1, 0)]
    received = lax.ppermute(other, "c", swap)
    pieces = kernel_call(pair_kernel, shape((16, 5, *tile), BF16), (own, received), 1)
    summed = exchange(pieces, PLANE)
    from_first = exchange(back_first, FIRST)
    pieces = kernel_call(plane_kernel, shape((8, 5, *tile), BF16), (summed,), 1)
    summed = exchange(pieces, "z")
    pieces, d_gain = kernel_call(
        functools.partial(line_kernel, 1.0 / math.sqrt(count)),
        (shape((16, 4, *tile), BF16), shape((1, WIDTH), F32)),
        (summed,),
        1,
    )
    mine = exchange(pieces, PLANE).reshape(TILES, *tile)
    theirs = lax.ppermute(mine, "c", swap)
    d_w_qkv, d_w_out = kernel_call(
        assemble_kernel,
        (shape((WIDTH, TRIPLE), F32), shape((WIDTH, WIDTH), F32)),
        (core, mine, theirs),
        1,
        [pltpu.VMEM((2, TILES, *tile), BF16)],
        1,
    )
    d_tokens = kernel_call(
        tokens_kernel,
        shape(local.shape, BF16),
        (local, gain_row, third.reshape(local.shape), from_first, from_second),
        2,
    )
    return (d_tokens[None], d_w_qkv, d_w_out, d_gain.reshape(WIDTH))


def solution(mesh):
    fine = Mesh(mesh.devices.reshape(4, 8, 2, 2, 2), ("y", "z", "xh", "xl", "c"))
    split = P("y", FIRST, SECOND, None, None)
    count = 4 * 32 * 32 * 32
    return jax.shard_map(
        functools.partial(on_device, count),
        mesh=fine,
        in_specs=(split, split, split, P(), P(), P()),
        out_specs=(split, P(), P(), P()),
        check_vma=False,
    )
```

```python
import functools
import math

import jax
import jax.numpy as jnp
from jax import lax
from jax.experimental import pallas as pl
from jax.experimental.pallas import tpu as pltpu
from jax.sharding import Mesh
from jax.sharding import PartitionSpec as P

HEADS = 8
HEAD = 32
WIDTH = 256
TRIPLE = 3 * WIDTH
EPSILON = 1e-06
FACTOR = 1.0 / math.sqrt(HEAD)
TOKENS = 512
LENGTH = 32
PENCILS = 16
ROWS = 16
LANES = 128
TILES = 64
BF16 = jnp.bfloat16
F32 = jnp.float32
VMEM = pl.BlockSpec(memory_space=pltpu.VMEM)
ANY = pl.BlockSpec(memory_space=pl.ANY)
SMEM = pl.BlockSpec(memory_space=pltpu.SMEM)
PLANE = ("y", "xh", "xl")
FIRST = ("z", "xh")
SECOND = ("xl", "c")


def params():
    return pltpu.CompilerParams(vmem_limit_bytes=48 * 2**20)


def cost(us):
    return pl.CostEstimate(
        flops=int(us * 8e8), bytes_accessed=int(us * 2e6), transcendentals=0
    )


def dot(left, right, left_dim, right_dim):
    return lax.dot_general(
        left, right, (((left_dim,), (right_dim,)), ((), ())), preferred_element_type=F32
    )


def wide(ref, first, rows):
    return jnp.concatenate([ref[first, rows, :], ref[first + 1, rows, :]], axis=1).astype(BF16)


def attention(proj, grads, rows_of, block, lane):
    q = [wide(proj, 0, rows) for rows in rows_of]
    k = [wide(proj, 2, rows) for rows in rows_of]
    v = [wide(proj, 4, rows) for rows in rows_of]
    g = [wide(proj, 6, rows) for rows in rows_of]
    lows = []
    for i, rows in enumerate(rows_of):
        q_block = jnp.concatenate([q[i]] * HEADS, axis=0) * block
        g_block = jnp.concatenate([g[i]] * HEADS, axis=0) * block
        scores = dot(k[i], q_block, 1, 1)
        grad_probs = dot(v[i], g_block, 1, 1)
        top = jnp.max(scores, axis=0, keepdims=True)
        powers = jnp.exp((scores - top) * FACTOR)
        probs = powers * (1.0 / jnp.sum(powers, axis=0, keepdims=True))
        inner = jnp.sum(probs * grad_probs, axis=0, keepdims=True)
        low = (probs * (grad_probs - inner)).astype(BF16)
        grad_v = dot(probs.astype(BF16), g_block, 1, 0)
        grad_k = dot(low, q_block, 1, 0) * FACTOR
        for half in range(2):
            cols = slice(half * LANES, (half + 1) * LANES)
            grads[2 + half, rows, :] = grad_k[:, cols]
            grads[4 + half, rows, :] = grad_v[:, cols]
        lows.append(low)
    stacked = jnp.concatenate(lows, axis=0)
    for half in range(2):
        cols = slice(half * LANES, (half + 1) * LANES)
        turned = stacked[:, cols].T
        for i, rows in enumerate(rows_of):
            every = dot(turned[:, i * LENGTH : (i + 1) * LENGTH], k[i][:, cols], 1, 0)
            picked = every[96:128]
            for head in (2, 1, 0):
                picked = jnp.where(
                    lane < HEAD * (head + 1), every[head * 32 : head * 32 + 32], picked
                )
            grads[half, rows, :] = picked * FACTOR


def axis_grads(tokens, cotangent, gain, w_qkv, w_out, proj, grads, strided):
    tokens_f = tokens.astype(F32)
    root = jnp.sqrt(jnp.mean(tokens_f * tokens_f, axis=-1, keepdims=True) + EPSILON)
    unit = tokens_f / root
    normed = (unit * gain).astype(BF16)
    qkv = dot(normed, w_qkv, 1, 0)
    for col in range(6):
        proj[col] = qkv[:, col * LANES : (col + 1) * LANES]
    grad_attn = dot(cotangent, w_out, 1, 1)
    for col in range(2):
        proj[6 + col] = grad_attn[:, col * LANES : (col + 1) * LANES]
    shape = (WIDTH, WIDTH)
    block = (
        lax.broadcasted_iota(jnp.int32, shape, 0) // HEAD
        == lax.broadcasted_iota(jnp.int32, shape, 1) // HEAD
    )
    block = block.astype(F32).astype(BF16)
    lane = lax.broadcasted_iota(jnp.int32, (LENGTH, LANES), 1)
    for base in range(0, PENCILS, 4):
        if strided:
            rows_of = [pl.ds(base + i, LENGTH, stride=PENCILS) for i in range(4)]
        else:
            rows_of = [pl.ds((base + i) * LENGTH, LENGTH) for i in range(4)]
        attention(proj, grads, rows_of, block, lane)
    joined = jnp.concatenate([grads[col].astype(BF16) for col in range(6)], axis=1)
    grad_normed = dot(joined, w_qkv, 1, 1)
    part_qkv = dot(normed, joined, 0, 0)
    part_gain = jnp.sum(grad_normed * unit, axis=0, keepdims=True)
    return grad_normed, part_qkv, part_gain


BITS = (2, 8, 1, 4)
SWAPS = (("z", 1, 8), ("z", 4, 8), ("xh", 1, 2), ("z", 2, 8))


def sources_before(stage):
    masks = [0]
    for bit in BITS[:stage]:
        masks += [mask ^ bit for mask in masks]
    return masks


def span_masks(count):
    masks = [0]
    for bit in reversed(BITS[4 - count :]):
        masks += [mask ^ bit for mask in masks]
    return masks


SPANS = [span_masks(count) for count in range(4)]

SCRATCH = [
    pltpu.VMEM((8, TOKENS, LANES), F32),
    pltpu.VMEM((6, TOKENS, LANES), F32),
]


def first_pieces_kernel(tokens, cotangent, pieces, sem):
    copies = []
    for kind, ref in enumerate((tokens, cotangent)):
        for x in range(2):
            for z in range(2):
                copies.append(
                    pltpu.make_async_copy(
                        ref.at[x, :, pl.ds(z * ROWS, ROWS), :],
                        pieces.at[:, z, kind, x],
                        sem.at[len(copies)],
                    )
                )
    for copy in copies:
        copy.start()
    for copy in copies:
        copy.wait()


def second_pieces_kernel(place, tokens, cotangent, *rest):
    pieces, sem = rest[:4], rest[4]
    copies = []
    for mask, out in enumerate(pieces):
        peer = place[1] ^ mask
        rows = pl.ds(pl.multiple_of((peer & 1) * ROWS, ROWS), ROWS)
        for kind, ref in enumerate((tokens, cotangent)):
            copies.append(
                pltpu.make_async_copy(
                    ref.at[peer >> 1, :, rows, :], out.at[kind], sem.at[len(copies)]
                )
            )
    for copy in copies:
        copy.start()
    for copy in copies:
        copy.wait()


def third_kernel(
    tokens, cotangent, attn, gain, w_qkv, w_out, normed_out, qkv_out, out_out, gain_out, proj, grads
):
    cot = cotangent[...]
    grad_normed, part_qkv, part_gain = axis_grads(
        tokens[...], cot, gain[...], w_qkv[...], w_out[...], proj, grads, False
    )
    normed_out[...] = grad_normed
    qkv_out[...] = part_qkv
    gain_out[...] = part_gain
    out_out[...] = dot(attn[...], cot, 0, 0)


def second_kernel(*refs):
    pieces, (gain, w_qkv, w_out, qkv_in, gain_in) = refs[:4], refs[4:9]
    back, (qkv_out, gain_out, proj, grads) = refs[9:13], refs[13:]
    tokens = jnp.concatenate([piece[0].reshape(-1, WIDTH) for piece in pieces], axis=0)
    cot = jnp.concatenate([piece[1].reshape(-1, WIDTH) for piece in pieces], axis=0)
    grad_normed, part_qkv, part_gain = axis_grads(
        tokens, cot, gain[...], w_qkv[...], w_out[...], proj, grads, True
    )
    returned = grad_normed.astype(BF16)
    rows = TOKENS // 4
    for mask, out in enumerate(back):
        out[...] = returned[mask * rows : (mask + 1) * rows].reshape(out.shape)
    qkv_out[...] = qkv_in[...] + part_qkv
    gain_out[...] = gain_in[...] + part_gain


def first_kernel(
    place,
    pieces,
    gain,
    w_qkv,
    w_out,
    qkv_in,
    out_in,
    gain_in,
    stay,
    leave,
    own,
    other,
    proj,
    grads,
    halves,
    returned,
):
    tokens = pieces[:, 0].reshape(TOKENS, WIDTH)
    cot = pieces[:, 1].reshape(TOKENS, WIDTH)
    grad_normed, part_qkv, part_gain = axis_grads(
        tokens, cot, gain[...], w_qkv[...], w_out[...], proj, grads, True
    )
    returned[...] = grad_normed.astype(BF16).reshape(returned.shape)
    here = place[2]
    for at, mask in enumerate(SPANS[3]):
        stay[at] = returned[here ^ mask]
        leave[at] = returned[here ^ mask ^ BITS[0]]
    total = qkv_in[...] + part_qkv
    for at in range(2 * TILES):
        half, tile = divmod(at, TILES)
        if at < 96:
            row, col = divmod(at, 6)
            halves[half, tile] = total[row * 16 : row * 16 + 16, col * LANES : (col + 1) * LANES]
        else:
            row, col = divmod(at - 96, 2)
            halves[half, tile] = out_in[row * 16 : row * 16 + 16, col * LANES : (col + 1) * LANES]
    mine = place[0]
    own[0:TILES] = halves[mine]
    other[0:TILES] = halves[1 - mine]
    part_gain = gain_in[...] + part_gain
    gains = jnp.concatenate(
        [part_gain[:, :LANES], part_gain[:, LANES:], jnp.zeros((14, LANES), F32)], axis=0
    )
    own[TILES] = gains
    other[TILES] = gains


def stage_kernel(*refs):
    groups, out = refs[:-1], refs[-1]
    left = 16 >> (len(groups) - 1)
    at = 0
    for order, ref in enumerate(groups):
        span = 8 >> max(order - 1, 0)
        for base in range(0, 8, span):
            for block in range(left // 2, left):
                out[at] = ref[base + block]
                at += 1


def pair_kernel(own, received, pieces):
    for peer in range(16):
        tiles = slice(peer * 4, peer * 4 + 4)
        pieces[peer, 0:4] = (own[tiles] + received[tiles]).astype(BF16)
    gains = (own[TILES] + received[TILES]).astype(BF16)
    for peer in range(16):
        pieces[peer, 4] = gains


def plane_kernel(received, pieces):
    total = jnp.sum(received[...].astype(F32), axis=0).astype(BF16)
    for peer in range(8):
        pieces[peer] = total


def line_kernel(scale, received, pieces, gain_out):
    total = jnp.sum(received[...].astype(F32), axis=0) * scale
    low = total[0:4].astype(BF16)
    for peer in range(16):
        pieces[peer] = low
    gain_out[...] = jnp.concatenate([total[4, 0:1], total[4, 1:2]], axis=1)


def assemble_kernel(place, mine, theirs, w_qkv_out, w_out_out, halves):
    at_core = place[0]
    halves[at_core] = mine[...]
    halves[1 - at_core] = theirs[...]
    for at in range(2 * TILES):
        half, tile = divmod(at, TILES)
        rows = halves[half, tile].astype(F32)
        if at < 96:
            row, col = divmod(at, 6)
            w_qkv_out[row * 16 : row * 16 + 16, col * LANES : (col + 1) * LANES] = rows
        else:
            row, col = divmod(at - 96, 2)
            w_out_out[row * 16 : row * 16 + 16, col * LANES : (col + 1) * LANES] = rows


def tokens_kernel(place, tokens, gain, third, *rest):
    groups, seconds = rest[:5], rest[5:9]
    out, from_first, from_second = rest[9:]
    here = place[2]
    from_first[here] = groups[0][0]
    for stage in range(4):
        span = 8 >> stage
        for at, mask in enumerate(sources_before(stage)):
            from_first[here ^ (mask ^ BITS[stage])] = groups[stage + 1][at * span]
    for mask, ref in enumerate(seconds):
        from_second[place[1] ^ mask] = ref[...]
    for x in range(2):
        for y in range(8):
            tokens_f = tokens[x, y].astype(F32)
            first = jnp.concatenate([from_first[y * 2, x], from_first[y * 2 + 1, x]], axis=0)
            second = jnp.concatenate([from_second[x * 2, y], from_second[x * 2 + 1, y]], axis=0)
            grad_normed = third[x, y] + first.astype(F32) + second.astype(F32)
            square = jnp.mean(tokens_f * tokens_f, axis=-1, keepdims=True) + EPSILON
            root = jnp.sqrt(square)
            gained = gain[...] * grad_normed
            inner = jnp.sum(gained * tokens_f, axis=-1, keepdims=True)
            result = gained / root - tokens_f * (inner / (WIDTH * root * square))
            out[x, y] = result.astype(BF16)


def shape(dims, dtype):
    return jax.ShapeDtypeStruct(dims, dtype)


def kernel_call(body, outs, operands, us, scratch=(), scalars=0, space=VMEM):
    return pl.pallas_call(
        body,
        out_shape=outs,
        in_specs=[SMEM] * scalars + [space] * (len(operands) - scalars),
        out_specs=jax.tree.map(lambda _: space, outs),
        scratch_shapes=list(scratch),
        compiler_params=params(),
        cost_estimate=cost(us),
    )(*operands)


def swap(array, axis, mask, size):
    return lax.ppermute(array, axis, [(i, i ^ mask) for i in range(size)])


def exchange(pieces, axes):
    return lax.all_to_all(pieces, axes, split_axis=0, concat_axis=0, tiled=True)


def on_device(count, tokens, attn, cotangent, gain, w_qkv, w_out):
    core = lax.axis_index("c")
    along_second = lax.axis_index("xl") * 2 + core
    along_first = lax.axis_index("z") * 2 + lax.axis_index("xh")
    place = jnp.stack([core, along_second, along_first]).astype(jnp.int32)
    gain_row = gain.reshape(1, WIDTH)
    local = tokens[0]
    upstream = cotangent[0]
    flat = (TOKENS, WIDTH)
    tile = (16, LANES)
    to_first = kernel_call(
        first_pieces_kernel,
        shape((8, 2, 2, 2, ROWS, WIDTH), BF16),
        (local, upstream),
        2,
        [pltpu.SemaphoreType.DMA((8,))],
        space=ANY,
    )
    at_first = exchange(to_first.reshape(16, 2, 2, ROWS, WIDTH), FIRST)
    to_second = kernel_call(
        second_pieces_kernel,
        (shape((2, 8, ROWS, WIDTH), BF16),) * 4,
        (place, local, upstream),
        2,
        [pltpu.SemaphoreType.DMA((8,))],
        1,
        ANY,
    )
    at_second = [to_second[0]] + [swap(to_second[m], SECOND, m, 4) for m in (1, 2, 3)]
    third, part_qkv, part_out, part_gain = kernel_call(
        third_kernel,
        (
            shape(flat, F32),
            shape((WIDTH, TRIPLE), F32),
            shape((WIDTH, WIDTH), F32),
            shape((1, WIDTH), F32),
        ),
        (local.reshape(flat), upstream.reshape(flat), attn.reshape(flat), gain_row, w_qkv, w_out),
        7,
        SCRATCH,
    )
    *back, part_qkv, part_gain = kernel_call(
        second_kernel,
        (shape((8, ROWS, WIDTH), BF16),) * 4
        + (shape((WIDTH, TRIPLE), F32), shape((1, WIDTH), F32)),
        (*at_second, gain_row, w_qkv, w_out, part_qkv, part_gain),
        7,
        SCRATCH,
    )
    from_second = [back[0]] + [swap(back[m], SECOND, m, 4) for m in (1, 2, 3)]
    block = (2, ROWS, WIDTH)
    stay, leave, own, other = kernel_call(
        first_kernel,
        (
            shape((8, *block), BF16),
            shape((8, *block), BF16),
            shape((TILES + 1, *tile), F32),
            shape((TILES + 1, *tile), F32),
        ),
        (place, at_first, gain_row, w_qkv, w_out, part_qkv, part_out, part_gain),
        7,
        SCRATCH + [pltpu.VMEM((2, TILES, *tile), F32), pltpu.VMEM((16, *block), BF16)],
        1,
    )
    received = swap(other, "c", 1, 2)
    groups = [stay, swap(leave, *SWAPS[0])]
    pieces = kernel_call(pair_kernel, shape((16, 5, *tile), BF16), (own, received), 1)
    summed = exchange(pieces, PLANE)
    for stage in (1, 2, 3):
        leave = kernel_call(stage_kernel, shape((8, *block), BF16), groups, 1)
        groups.append(swap(leave, *SWAPS[stage]))
    pieces = kernel_call(plane_kernel, shape((8, 5, *tile), BF16), (summed,), 1)
    summed = exchange(pieces, "z")
    pieces, d_gain = kernel_call(
        functools.partial(line_kernel, 1.0 / math.sqrt(count)),
        (shape((16, 4, *tile), BF16), shape((1, WIDTH), F32)),
        (summed,),
        1,
    )
    mine = exchange(pieces, PLANE).reshape(TILES, *tile)
    theirs = swap(mine, "c", 1, 2)
    d_w_qkv, d_w_out = kernel_call(
        assemble_kernel,
        (shape((WIDTH, TRIPLE), F32), shape((WIDTH, WIDTH), F32)),
        (place, mine, theirs),
        1,
        [pltpu.VMEM((2, TILES, *tile), BF16)],
        1,
    )
    d_tokens = kernel_call(
        tokens_kernel,
        shape(local.shape, BF16),
        (place, local, gain_row, third.reshape(local.shape), *groups, *from_second),
        2,
        [pltpu.VMEM((16, *block), BF16), pltpu.VMEM((4, 8, ROWS, WIDTH), BF16)],
        1,
    )
    return (d_tokens[None], d_w_qkv, d_w_out, d_gain.reshape(WIDTH))


def solution(mesh):
    fine = Mesh(mesh.devices.reshape(4, 8, 2, 2, 2), ("y", "z", "xh", "xl", "c"))
    split = P("y", FIRST, SECOND, None, None)
    count = 4 * 32 * 32 * 32
    return jax.shard_map(
        functools.partial(on_device, count),
        mesh=fine,
        in_specs=(split, split, split, P(), P(), P()),
        out_specs=(split, P(), P(), P()),
        check_vma=False,
    )
```

```python
import functools
import math

import jax
import jax.numpy as jnp
from jax import lax
from jax.experimental import pallas as pl
from jax.experimental.pallas import tpu as pltpu
from jax.sharding import Mesh
from jax.sharding import PartitionSpec as P

HEADS = 8
HEAD = 32
WIDTH = 256
TRIPLE = 3 * WIDTH
EPSILON = 1e-06
FACTOR = 1.0 / math.sqrt(HEAD)
TOKENS = 512
LENGTH = 32
GROUP = 8
PENCILS = 16
ROWS = 16
LANES = 128
TILES = 64
BF16 = jnp.bfloat16
F32 = jnp.float32
VMEM = pl.BlockSpec(memory_space=pltpu.VMEM)
HBM = pl.BlockSpec(memory_space=pltpu.HBM)
SMEM = pl.BlockSpec(memory_space=pltpu.SMEM)
PLANE = ("y", "xh", "xl")
FIRST = ("z", "xh")
SECOND = ("xl", "c")


def params(mib):
    return pltpu.CompilerParams(vmem_limit_bytes=mib * 2**20)


def cost(us):
    return pl.CostEstimate(
        flops=int(us * 8e8), bytes_accessed=int(us * 2e6), transcendentals=0
    )


def dot(left, right, left_dim, right_dim):
    return lax.dot_general(
        left, right, (((left_dim,), (right_dim,)), ((), ())), preferred_element_type=F32
    )


def attention(qkv, grad_attn, block, lane, count):
    spans = [slice(i * LENGTH, (i + 1) * LENGTH) for i in range(count)]
    k = [qkv[span, WIDTH : 2 * WIDTH] for span in spans]
    v = [qkv[span, 2 * WIDTH :] for span in spans]
    q_block = [jnp.concatenate([qkv[span, :WIDTH]] * HEADS, axis=0) * block for span in spans]
    g_block = [jnp.concatenate([grad_attn[span]] * HEADS, axis=0) * block for span in spans]
    scores = [dot(k[i], q_block[i], 1, 1) for i in range(count)]
    grad_probs = [dot(v[i], g_block[i], 1, 1) for i in range(count)]
    probs_low = []
    scores_low = []
    for i in range(count):
        top = jnp.max(scores[i], axis=0, keepdims=True)
        powers = jnp.exp((scores[i] - top) * FACTOR)
        probs = powers * (1.0 / jnp.sum(powers, axis=0, keepdims=True))
        inner = jnp.sum(probs * grad_probs[i], axis=0, keepdims=True)
        scores_low.append((probs * (grad_probs[i] - inner)).astype(BF16))
        probs_low.append(probs.astype(BF16))
    grad_v = [dot(probs_low[i], g_block[i], 1, 0) for i in range(count)]
    grad_k = [dot(scores_low[i], q_block[i], 1, 0) * FACTOR for i in range(count)]
    grad_q = [[] for _ in range(count)]
    for half in range(2):
        cols = slice(half * LANES, (half + 1) * LANES)
        for base in range(0, count, 4):
            turned = jnp.concatenate([low[:, cols] for low in scores_low[base : base + 4]], axis=0)
            turned = turned.T
            for i in range(4):
                every = dot(turned[:, spans[i]], k[base + i][:, cols], 1, 0)
                picked = every[96:128]
                for head in (2, 1, 0):
                    picked = jnp.where(
                        lane < HEAD * (head + 1), every[head * HEAD : (head + 1) * HEAD], picked
                    )
                grad_q[base + i].append(picked * FACTOR)
    joined = [
        jnp.concatenate([*grad_q[i], grad_k[i], grad_v[i]], axis=1).astype(BF16)
        for i in range(count)
    ]
    return jnp.concatenate(joined, axis=0)


def axis_grads(tokens, cotangent, gain, w_qkv, w_out, scratch, strided):
    tokens_cols, cot_cols, grad_cols, joined_rows, normed_rows = scratch
    if strided:
        tokens_f, cot_f = tokens.astype(F32), cotangent.astype(F32)
        for col in range(2):
            tokens_cols[col] = tokens_f[:, col * LANES : (col + 1) * LANES]
            cot_cols[col] = cot_f[:, col * LANES : (col + 1) * LANES]
    dims = (WIDTH, WIDTH)
    block = (
        lax.broadcasted_iota(jnp.int32, dims, 0) // HEAD
        == lax.broadcasted_iota(jnp.int32, dims, 1) // HEAD
    )
    block = block.astype(F32).astype(BF16)
    lane = lax.broadcasted_iota(jnp.int32, (LENGTH, LANES), 1)
    part_gain = jnp.zeros((1, WIDTH), F32)
    for base in range(0, PENCILS, GROUP):
        group = slice(base * LENGTH, (base + GROUP) * LENGTH)
        if strided:
            rows_of = [pl.ds(base + i, LENGTH, stride=PENCILS) for i in range(GROUP)]

            def gathered(ref):
                cols = [
                    jnp.concatenate([ref[col, rows, :] for rows in rows_of], axis=0)
                    for col in range(2)
                ]
                return jnp.concatenate(cols, axis=1)

            tokens_f = gathered(tokens_cols)
            cot = gathered(cot_cols).astype(BF16)
        else:
            rows_of = [pl.ds((base + i) * LENGTH, LENGTH) for i in range(GROUP)]
            tokens_f = tokens[group].astype(F32)
            cot = cotangent[group]
        square = jnp.mean(tokens_f * tokens_f, axis=-1, keepdims=True) + EPSILON
        unit = tokens_f * lax.rsqrt(square)
        normed = (unit * gain).astype(BF16)
        normed_rows[group] = normed
        qkv = dot(normed, w_qkv, 1, 0).astype(BF16)
        grad_attn = dot(cot, w_out, 1, 1).astype(BF16)
        joined = attention(qkv, grad_attn, block, lane, GROUP)
        joined_rows[group] = joined
        grad_normed = dot(joined, w_qkv, 1, 1)
        part_gain = part_gain + jnp.sum(grad_normed * unit, axis=0, keepdims=True)
        for i, rows in enumerate(rows_of):
            for col in range(2):
                grad_cols[col, rows, :] = grad_normed[spans_of(i), col * LANES : (col + 1) * LANES]
    part_qkv = dot(normed_rows[...], joined_rows[...], 0, 0)
    return jnp.concatenate([grad_cols[0], grad_cols[1]], axis=1), part_qkv, part_gain


def spans_of(i):
    return slice(i * LENGTH, (i + 1) * LENGTH)


BITS = (2, 8, 1, 4)
SWAPS = (("z", 1, 8), ("z", 4, 8), ("xh", 1, 2), ("z", 2, 8))


def sources_before(stage):
    masks = [0]
    for bit in BITS[:stage]:
        masks += [mask ^ bit for mask in masks]
    return masks


def span_masks(count):
    masks = [0]
    for bit in reversed(BITS[4 - count :]):
        masks += [mask ^ bit for mask in masks]
    return masks


SPANS = [span_masks(count) for count in range(4)]

SCRATCH = [pltpu.VMEM((2, TOKENS, LANES), F32)] * 3 + [
    pltpu.VMEM((TOKENS, TRIPLE), BF16),
    pltpu.VMEM((TOKENS, WIDTH), BF16),
]


def first_pieces_kernel(tokens, cotangent, pieces, sem):
    copies = []
    for kind, ref in enumerate((tokens, cotangent)):
        for x in range(2):
            for z in range(2):
                copies.append(
                    pltpu.make_async_copy(
                        ref.at[x, :, pl.ds(z * ROWS, ROWS), :],
                        pieces.at[:, z, kind, x],
                        sem.at[len(copies)],
                    )
                )
    for copy in copies:
        copy.start()
    for copy in copies:
        copy.wait()


def second_pieces_kernel(place, tokens, cotangent, *rest):
    pieces, sem = rest[:4], rest[4]
    copies = []
    for mask, out in enumerate(pieces):
        peer = place[1] ^ mask
        rows = pl.ds(pl.multiple_of((peer & 1) * ROWS, ROWS), ROWS)
        for kind, ref in enumerate((tokens, cotangent)):
            copies.append(
                pltpu.make_async_copy(
                    ref.at[peer >> 1, :, rows, :], out.at[kind], sem.at[len(copies)]
                )
            )
    for copy in copies:
        copy.start()
    for copy in copies:
        copy.wait()


def third_kernel(
    tokens, cotangent, attn, gain, w_qkv, w_out, normed_out, qkv_out, out_out, gain_out, *scratch
):
    cot = cotangent[...]
    grad_normed, part_qkv, part_gain = axis_grads(
        tokens[...], cot, gain[...], w_qkv[...], w_out[...], scratch, False
    )
    normed_out[...] = grad_normed
    qkv_out[...] = part_qkv
    gain_out[...] = part_gain
    out_out[...] = dot(attn[...], cot, 0, 0)


def first_kernel(
    place, pieces, gain, w_qkv, w_out, qkv_in, gain_in, stay, leave, qkv_out, gain_out, *scratch
):
    returned = scratch[-1]
    tokens = pieces[:, 0].reshape(TOKENS, WIDTH)
    cot = pieces[:, 1].reshape(TOKENS, WIDTH)
    grad_normed, part_qkv, part_gain = axis_grads(
        tokens, cot, gain[...], w_qkv[...], w_out[...], scratch[:-1], True
    )
    returned[...] = grad_normed.astype(BF16).reshape(returned.shape)
    here = place[2]
    for at, mask in enumerate(SPANS[3]):
        stay[at] = returned[here ^ mask]
        leave[at] = returned[here ^ mask ^ BITS[0]]
    qkv_out[...] = qkv_in[...] + part_qkv
    gain_out[...] = gain_in[...] + part_gain


def second_kernel(place, *refs):
    pieces, (gain, w_qkv, w_out, qkv_in, out_in, gain_in) = refs[:4], refs[4:10]
    back, (own, other), scratch, halves = refs[10:14], refs[14:16], refs[16:-1], refs[-1]
    tokens = jnp.concatenate([piece[0].reshape(-1, WIDTH) for piece in pieces], axis=0)
    cot = jnp.concatenate([piece[1].reshape(-1, WIDTH) for piece in pieces], axis=0)
    grad_normed, part_qkv, part_gain = axis_grads(
        tokens, cot, gain[...], w_qkv[...], w_out[...], scratch, True
    )
    returned = grad_normed.astype(BF16)
    rows = TOKENS // 4
    for mask, out in enumerate(back):
        out[...] = returned[mask * rows : (mask + 1) * rows].reshape(out.shape)
    total = qkv_in[...] + part_qkv
    for at in range(2 * TILES):
        half, tile = divmod(at, TILES)
        if at < 96:
            row, col = divmod(at, 6)
            halves[half, tile] = total[row * 16 : row * 16 + 16, col * LANES : (col + 1) * LANES]
        else:
            row, col = divmod(at - 96, 2)
            halves[half, tile] = out_in[row * 16 : row * 16 + 16, col * LANES : (col + 1) * LANES]
    mine = place[0]
    own[0:TILES] = halves[mine]
    other[0:TILES] = halves[1 - mine]
    part_gain = gain_in[...] + part_gain
    gains = jnp.concatenate(
        [part_gain[:, :LANES], part_gain[:, LANES:], jnp.zeros((14, LANES), F32)], axis=0
    )
    own[TILES] = gains
    other[TILES] = gains


def stage_kernel(*refs):
    groups, out = refs[:-1], refs[-1]
    left = 16 >> (len(groups) - 1)
    at = 0
    for order, ref in enumerate(groups):
        span = 8 >> max(order - 1, 0)
        for base in range(0, 8, span):
            for block in range(left // 2, left):
                out[at] = ref[base + block]
                at += 1


def pair_kernel(own, received, pieces):
    for peer in range(16):
        tiles = slice(peer * 4, peer * 4 + 4)
        pieces[peer, 0:4] = (own[tiles] + received[tiles]).astype(BF16)
    gains = (own[TILES] + received[TILES]).astype(BF16)
    for peer in range(16):
        pieces[peer, 4] = gains


def plane_kernel(received, pieces):
    total = jnp.sum(received[...].astype(F32), axis=0).astype(BF16)
    for peer in range(8):
        pieces[peer] = total


def line_kernel(scale, received, pieces, gain_out):
    total = jnp.sum(received[...].astype(F32), axis=0) * scale
    low = total[0:4].astype(BF16)
    for peer in range(16):
        pieces[peer] = low
    gain_out[...] = jnp.concatenate([total[4, 0:1], total[4, 1:2]], axis=1)


def assemble_kernel(place, mine, theirs, w_qkv_out, w_out_out, halves):
    at_core = place[0]
    halves[at_core] = mine[...]
    halves[1 - at_core] = theirs[...]
    for at in range(2 * TILES):
        half, tile = divmod(at, TILES)
        rows = halves[half, tile].astype(F32)
        if at < 96:
            row, col = divmod(at, 6)
            w_qkv_out[row * 16 : row * 16 + 16, col * LANES : (col + 1) * LANES] = rows
        else:
            row, col = divmod(at - 96, 2)
            w_out_out[row * 16 : row * 16 + 16, col * LANES : (col + 1) * LANES] = rows


def tokens_kernel(place, tokens, gain, third, *rest):
    groups, seconds = rest[:5], rest[5:9]
    out, from_first, from_second = rest[9:]
    here = place[2]
    from_first[here] = groups[0][0]
    for stage in range(4):
        span = 8 >> stage
        for at, mask in enumerate(sources_before(stage)):
            from_first[here ^ (mask ^ BITS[stage])] = groups[stage + 1][at * span]
    for mask, ref in enumerate(seconds):
        from_second[place[1] ^ mask] = ref[...]
    for x in range(2):
        for y in range(8):
            tokens_f = tokens[x, y].astype(F32)
            first = jnp.concatenate([from_first[y * 2, x], from_first[y * 2 + 1, x]], axis=0)
            second = jnp.concatenate([from_second[x * 2, y], from_second[x * 2 + 1, y]], axis=0)
            grad_normed = third[x, y] + first.astype(F32) + second.astype(F32)
            square = jnp.mean(tokens_f * tokens_f, axis=-1, keepdims=True) + EPSILON
            root = jnp.sqrt(square)
            gained = gain[...] * grad_normed
            inner = jnp.sum(gained * tokens_f, axis=-1, keepdims=True)
            result = gained / root - tokens_f * (inner / (WIDTH * root * square))
            out[x, y] = result.astype(BF16)


def shape(dims, dtype):
    return jax.ShapeDtypeStruct(dims, dtype)


def kernel_call(body, outs, operands, us, scratch=(), scalars=0, space=VMEM):
    return pl.pallas_call(
        body,
        out_shape=outs,
        in_specs=[SMEM] * scalars + [space] * (len(operands) - scalars),
        out_specs=jax.tree.map(lambda _: space, outs),
        scratch_shapes=list(scratch),
        compiler_params=params(62 if space is HBM else 48),
        cost_estimate=cost(us),
    )(*operands)


def swap(array, axis, mask, size):
    return lax.ppermute(array, axis, [(i, i ^ mask) for i in range(size)])


def exchange(pieces, axes):
    return lax.all_to_all(pieces, axes, split_axis=0, concat_axis=0, tiled=True)


def on_device(count, tokens, attn, cotangent, gain, w_qkv, w_out):
    core = lax.axis_index("c")
    along_second = lax.axis_index("xl") * 2 + core
    along_first = lax.axis_index("z") * 2 + lax.axis_index("xh")
    place = jnp.stack([core, along_second, along_first]).astype(jnp.int32)
    gain_row = gain.reshape(1, WIDTH)
    local = tokens[0]
    upstream = cotangent[0]
    flat = (TOKENS, WIDTH)
    tile = (16, LANES)
    to_first = kernel_call(
        first_pieces_kernel,
        shape((8, 2, 2, 2, ROWS, WIDTH), BF16),
        (local, upstream),
        2,
        [pltpu.SemaphoreType.DMA((8,))],
        space=HBM,
    )
    at_first = exchange(to_first.reshape(16, 2, 2, ROWS, WIDTH), FIRST)
    to_second = kernel_call(
        second_pieces_kernel,
        (shape((2, 8, ROWS, WIDTH), BF16),) * 4,
        (place, local, upstream),
        2,
        [pltpu.SemaphoreType.DMA((8,))],
        1,
        HBM,
    )
    at_second = [to_second[0]] + [swap(to_second[m], SECOND, m, 4) for m in (1, 2, 3)]
    third, part_qkv, part_out, part_gain = kernel_call(
        third_kernel,
        (
            shape(flat, F32),
            shape((WIDTH, TRIPLE), F32),
            shape((WIDTH, WIDTH), F32),
            shape((1, WIDTH), F32),
        ),
        (local.reshape(flat), upstream.reshape(flat), attn.reshape(flat), gain_row, w_qkv, w_out),
        5,
        SCRATCH,
    )
    block = (2, ROWS, WIDTH)
    stay, leave, part_qkv, part_gain = kernel_call(
        first_kernel,
        (
            shape((8, *block), BF16),
            shape((8, *block), BF16),
            shape((WIDTH, TRIPLE), F32),
            shape((1, WIDTH), F32),
        ),
        (place, at_first, gain_row, w_qkv, w_out, part_qkv, part_gain),
        5,
        SCRATCH + [pltpu.VMEM((16, *block), BF16)],
        1,
    )
    groups = [stay, swap(leave, *SWAPS[0])]
    *back, own, other = kernel_call(
        second_kernel,
        (shape((8, ROWS, WIDTH), BF16),) * 4 + (shape((TILES + 1, *tile), F32),) * 2,
        (place, *at_second, gain_row, w_qkv, w_out, part_qkv, part_out, part_gain),
        5,
        SCRATCH + [pltpu.VMEM((2, TILES, *tile), F32)],
        1,
    )
    received = swap(other, "c", 1, 2)
    pieces = kernel_call(pair_kernel, shape((16, 5, *tile), BF16), (own, received), 1)
    leave = kernel_call(stage_kernel, shape((8, *block), BF16), groups, 1)
    pieces, leave, *back = lax.optimization_barrier((pieces, leave, *back))
    summed = exchange(pieces, PLANE)
    from_second = [back[0]] + [swap(back[m], SECOND, m, 4) for m in (1, 2, 3)]
    groups.append(swap(leave, *SWAPS[1]))
    summed, groups, from_second = lax.optimization_barrier((summed, groups, from_second))
    pieces = kernel_call(plane_kernel, shape((8, 5, *tile), BF16), (summed,), 1)
    leave = kernel_call(stage_kernel, shape((8, *block), BF16), groups, 1)
    pieces, leave = lax.optimization_barrier((pieces, leave))
    summed = exchange(pieces, "z")
    groups.append(swap(leave, *SWAPS[2]))
    summed, groups = lax.optimization_barrier((summed, groups))
    pieces, d_gain = kernel_call(
        functools.partial(line_kernel, 1.0 / math.sqrt(count)),
        (shape((16, 4, *tile), BF16), shape((1, WIDTH), F32)),
        (summed,),
        1,
    )
    leave = kernel_call(stage_kernel, shape((8, *block), BF16), groups, 1)
    pieces, leave = lax.optimization_barrier((pieces, leave))
    mine = exchange(pieces, PLANE)
    groups.append(swap(leave, *SWAPS[3]))
    mine, groups = lax.optimization_barrier((mine, groups))
    mine = mine.reshape(TILES, *tile)
    theirs = swap(mine, "c", 1, 2)
    d_w_qkv, d_w_out = kernel_call(
        assemble_kernel,
        (shape((WIDTH, TRIPLE), F32), shape((WIDTH, WIDTH), F32)),
        (place, mine, theirs),
        1,
        [pltpu.VMEM((2, TILES, *tile), BF16)],
        1,
    )
    d_tokens = kernel_call(
        tokens_kernel,
        shape(local.shape, BF16),
        (place, local, gain_row, third.reshape(local.shape), *groups, *from_second),
        2,
        [pltpu.VMEM((16, *block), BF16), pltpu.VMEM((4, 8, ROWS, WIDTH), BF16)],
        1,
    )
    return (d_tokens[None], d_w_qkv, d_w_out, d_gain.reshape(WIDTH))


def solution(mesh):
    fine = Mesh(mesh.devices.reshape(4, 8, 2, 2, 2), ("y", "z", "xh", "xl", "c"))
    split = P("y", FIRST, SECOND, None, None)
    count = 4 * 32 * 32 * 32
    return jax.shard_map(
        functools.partial(on_device, count),
        mesh=fine,
        in_specs=(split, split, split, P(), P(), P()),
        out_specs=(split, P(), P(), P()),
        check_vma=False,
    )
```

```python
import functools
import math

import jax
import jax.numpy as jnp
from jax import lax
from jax.experimental import pallas as pl
from jax.experimental.pallas import tpu as pltpu
from jax.sharding import Mesh
from jax.sharding import PartitionSpec as P

HEADS = 8
HEAD = 32
WIDTH = 256
TRIPLE = 3 * WIDTH
EPSILON = 1e-06
FACTOR = 1.0 / math.sqrt(HEAD)
TOKENS = 512
LENGTH = 32
GROUP = 8
PENCILS = 16
ROWS = 16
LANES = 128
HALF = 32
TILES = 64
BF16 = jnp.bfloat16
F32 = jnp.float32
VMEM = pl.BlockSpec(memory_space=pltpu.VMEM)
HBM = pl.BlockSpec(memory_space=pltpu.HBM)
PLANE = ("y", "xh", "xl")
FIRST = ("z", "xh")
SECOND = ("xl", "c")


def params(mib):
    return pltpu.CompilerParams(vmem_limit_bytes=mib * 2**20)


def cost(us):
    return pl.CostEstimate(
        flops=int(us * 8e8), bytes_accessed=int(us * 2e6), transcendentals=0
    )


def dot(left, right, left_dim, right_dim):
    return lax.dot_general(
        left, right, (((left_dim,), (right_dim,)), ((), ())), preferred_element_type=F32
    )


def attention(qkv, grad_attn, block, lane, count):
    spans = [slice(i * LENGTH, (i + 1) * LENGTH) for i in range(count)]
    k = [qkv[span, WIDTH : 2 * WIDTH] for span in spans]
    v = [qkv[span, 2 * WIDTH :] for span in spans]
    q_block = [jnp.concatenate([qkv[span, :WIDTH]] * HEADS, axis=0) * block for span in spans]
    g_block = [jnp.concatenate([grad_attn[span]] * HEADS, axis=0) * block for span in spans]
    scores = [dot(k[i], q_block[i], 1, 1) for i in range(count)]
    grad_probs = [dot(v[i], g_block[i], 1, 1) for i in range(count)]
    probs_low = []
    scores_low = []
    for i in range(count):
        top = jnp.max(scores[i], axis=0, keepdims=True)
        powers = jnp.exp((scores[i] - top) * FACTOR)
        probs = powers * (1.0 / jnp.sum(powers, axis=0, keepdims=True))
        inner = jnp.sum(probs * grad_probs[i], axis=0, keepdims=True)
        scores_low.append((probs * (grad_probs[i] - inner)).astype(BF16))
        probs_low.append(probs.astype(BF16))
    grad_v = [dot(probs_low[i], g_block[i], 1, 0) for i in range(count)]
    grad_k = [dot(scores_low[i], q_block[i], 1, 0) * FACTOR for i in range(count)]
    grad_q = [[] for _ in range(count)]
    for half in range(2):
        cols = slice(half * LANES, (half + 1) * LANES)
        for base in range(0, count, 4):
            turned = jnp.concatenate([low[:, cols] for low in scores_low[base : base + 4]], axis=0)
            turned = turned.T
            for i in range(4):
                every = dot(turned[:, spans[i]], k[base + i][:, cols], 1, 0)
                picked = every[96:128]
                for head in (2, 1, 0):
                    picked = jnp.where(
                        lane < HEAD * (head + 1), every[head * HEAD : (head + 1) * HEAD], picked
                    )
                grad_q[base + i].append(picked * FACTOR)
    joined = [
        jnp.concatenate([*grad_q[i], grad_k[i], grad_v[i]], axis=1).astype(BF16)
        for i in range(count)
    ]
    return jnp.concatenate(joined, axis=0)


def axis_grads(tokens, cotangent, gain, w_qkv, w_out, scratch, strided):
    tokens_cols, cot_cols, grad_cols, joined_rows, normed_rows = scratch
    if strided:
        tokens_f, cot_f = tokens.astype(F32), cotangent.astype(F32)
        for col in range(2):
            tokens_cols[col] = tokens_f[:, col * LANES : (col + 1) * LANES]
            cot_cols[col] = cot_f[:, col * LANES : (col + 1) * LANES]
    dims = (WIDTH, WIDTH)
    block = (
        lax.broadcasted_iota(jnp.int32, dims, 0) // HEAD
        == lax.broadcasted_iota(jnp.int32, dims, 1) // HEAD
    )
    block = block.astype(F32).astype(BF16)
    lane = lax.broadcasted_iota(jnp.int32, (LENGTH, LANES), 1)
    part_gain = jnp.zeros((1, WIDTH), F32)
    for base in range(0, PENCILS, GROUP):
        group = slice(base * LENGTH, (base + GROUP) * LENGTH)
        if strided:
            rows_of = [pl.ds(base + i, LENGTH, stride=PENCILS) for i in range(GROUP)]

            def gathered(ref):
                cols = [
                    jnp.concatenate([ref[col, rows, :] for rows in rows_of], axis=0)
                    for col in range(2)
                ]
                return jnp.concatenate(cols, axis=1)

            tokens_f = gathered(tokens_cols)
            cot = gathered(cot_cols).astype(BF16)
        else:
            rows_of = [pl.ds((base + i) * LENGTH, LENGTH) for i in range(GROUP)]
            tokens_f = tokens[group].astype(F32)
            cot = cotangent[group]
        square = jnp.mean(tokens_f * tokens_f, axis=-1, keepdims=True) + EPSILON
        unit = tokens_f * lax.rsqrt(square)
        normed = (unit * gain).astype(BF16)
        normed_rows[group] = normed
        qkv = dot(normed, w_qkv, 1, 0).astype(BF16)
        grad_attn = dot(cot, w_out, 1, 1).astype(BF16)
        joined = attention(qkv, grad_attn, block, lane, GROUP)
        joined_rows[group] = joined
        grad_normed = dot(joined, w_qkv, 1, 1)
        part_gain = part_gain + jnp.sum(grad_normed * unit, axis=0, keepdims=True)
        for i, rows in enumerate(rows_of):
            for col in range(2):
                grad_cols[col, rows, :] = grad_normed[spans_of(i), col * LANES : (col + 1) * LANES]
    part_qkv = dot(normed_rows[...], joined_rows[...], 0, 0)
    return jnp.concatenate([grad_cols[0], grad_cols[1]], axis=1), part_qkv, part_gain


def spans_of(i):
    return slice(i * LENGTH, (i + 1) * LENGTH)


BITS = (2, 8, 1, 4)
SWAPS = (("z", 1, 8), ("z", 4, 8), ("xh", 1, 2), ("z", 2, 8))


def sources_before(stage):
    masks = [0]
    for bit in BITS[:stage]:
        masks += [mask ^ bit for mask in masks]
    return masks


def span_masks(count):
    masks = [0]
    for bit in reversed(BITS[4 - count :]):
        masks += [mask ^ bit for mask in masks]
    return masks


SPANS = [span_masks(count) for count in range(4)]

SCRATCH = [pltpu.VMEM((2, TOKENS, LANES), F32)] * 3 + [
    pltpu.VMEM((TOKENS, TRIPLE), BF16),
    pltpu.VMEM((TOKENS, WIDTH), BF16),
]


def along_second():
    return lax.axis_index("xl") * 2 + lax.axis_index("c")


def along_first():
    return lax.axis_index("z") * 2 + lax.axis_index("xh")


def pieces_kernel(tokens, cotangent, to_first, *rest):
    to_second, (held, sem) = rest[:4], rest[4:]
    loads, firsts, seconds = [], [], []
    for kind, ref in enumerate((tokens, cotangent)):
        at = kind * 9
        loads.append(pltpu.make_async_copy(ref, held.at[kind], sem.at[at]))
        for x in range(2):
            for z in range(2):
                source = held.at[kind, x, :, pl.ds(z * ROWS, ROWS), :]
                target = to_first.at[:, z, kind, x]
                firsts.append(
                    (kind, pltpu.make_async_copy(source, target, sem.at[at + 1 + x * 2 + z]))
                )
        for mask, out in enumerate(to_second):
            peer = along_second() ^ mask
            rows = pl.ds(pl.multiple_of((peer & 1) * ROWS, ROWS), ROWS)
            source = held.at[kind, peer >> 1, :, rows, :]
            seconds.append(
                (kind, pltpu.make_async_copy(source, out.at[kind], sem.at[at + 5 + mask]))
            )
    for load in loads:
        load.start()
    for now, load in enumerate(loads):
        load.wait()
        for kind, store in firsts + seconds:
            if kind == now:
                store.start()
    for _, store in firsts + seconds:
        store.wait()


def third_kernel(
    tokens, cotangent, attn, gain, w_qkv, w_out, normed_out, qkv_out, out_out, gain_out, *scratch
):
    cot = cotangent[...]
    grad_normed, part_qkv, part_gain = axis_grads(
        tokens[...], cot, gain[...], w_qkv[...], w_out[...], scratch, False
    )
    normed_out[...] = grad_normed
    qkv_out[...] = part_qkv
    gain_out[...] = part_gain
    out_out[...] = dot(attn[...], cot, 0, 0)


def pack(total, part_out, part_gain, halves, own, low, high):
    for at in range(2 * TILES):
        half, tile = divmod(at, TILES)
        if at < 96:
            row, col = divmod(at, 6)
            halves[half, tile] = total[row * 16 : row * 16 + 16, col * LANES : (col + 1) * LANES]
        elif part_out is None:
            halves[half, tile] = jnp.zeros((16, LANES), F32)
        else:
            row, col = divmod(at - 96, 2)
            halves[half, tile] = part_out[row * 16 : row * 16 + 16, col * LANES : (col + 1) * LANES]
    mine = lax.axis_index("c")
    own[0:TILES] = halves[mine]
    low[0:HALF] = halves[1 - mine, 0:HALF].astype(BF16)
    high[0:HALF] = halves[1 - mine, HALF:TILES].astype(BF16)
    gains = jnp.concatenate(
        [part_gain[:, :LANES], part_gain[:, LANES:], jnp.zeros((14, LANES), F32)], axis=0
    )
    own[TILES] = gains
    high[HALF] = gains.astype(BF16)


def second_kernel(*refs):
    pieces, (gain, w_qkv, w_out), parts = refs[:4], refs[4:7], refs[7:10]
    back, packed, scratch, halves = refs[10:14], refs[14:17], refs[17:-1], refs[-1]
    tokens = jnp.concatenate([piece[0].reshape(-1, WIDTH) for piece in pieces], axis=0)
    cot = jnp.concatenate([piece[1].reshape(-1, WIDTH) for piece in pieces], axis=0)
    grad_normed, part_qkv, part_gain = axis_grads(
        tokens, cot, gain[...], w_qkv[...], w_out[...], scratch, True
    )
    returned = grad_normed.astype(BF16)
    rows = TOKENS // 4
    for mask, out in enumerate(back):
        out[...] = returned[mask * rows : (mask + 1) * rows].reshape(out.shape)
    third_qkv, part_out, third_gain = parts
    pack(third_qkv[...] + part_qkv, part_out, third_gain[...] + part_gain, halves, *packed)


def first_kernel(pieces, gain, w_qkv, w_out, *refs):
    (stay, leave), packed, scratch, (returned, halves) = refs[:2], refs[2:5], refs[5:-2], refs[-2:]
    tokens = pieces[:, 0].reshape(TOKENS, WIDTH)
    cot = pieces[:, 1].reshape(TOKENS, WIDTH)
    grad_normed, part_qkv, part_gain = axis_grads(
        tokens, cot, gain[...], w_qkv[...], w_out[...], scratch, True
    )
    returned[...] = grad_normed.astype(BF16).reshape(returned.shape)
    here = along_first()
    for at, mask in enumerate(SPANS[3]):
        stay[at] = returned[here ^ mask]
        leave[at] = returned[here ^ mask ^ BITS[0]]
    pack(part_qkv, None, part_gain, halves, *packed)


def stage_kernel(*refs):
    groups, out = refs[:-1], refs[-1]
    left = 16 >> (len(groups) - 1)
    at = 0
    for order, ref in enumerate(groups):
        span = 8 >> max(order - 1, 0)
        for base in range(0, 8, span):
            for block in range(left // 2, left):
                out[at] = ref[base + block]
                at += 1


def pair_kernel(*refs):
    sources, pieces = (refs[0:3], refs[3:6]), refs[6]

    def summed(tiles):
        half, at = divmod(tiles.start, HALF)
        if tiles.start == TILES:
            half, at = 1, HALF
        total = None
        for own, low, high in sources:
            mine = own[tiles]
            if tiles.start == TILES:
                mine = mine.astype(BF16).astype(F32)
            part = mine + (low, high)[half][at : at + tiles.stop - tiles.start].astype(F32)
            total = part if total is None else total + part
        return total.astype(BF16)

    gains = summed(slice(TILES, TILES + 1))
    for peer in range(16):
        pieces[peer, 0:4] = summed(slice(peer * 4, peer * 4 + 4))
        pieces[peer, 4:5] = gains


def plane_kernel(received, pieces):
    total = jnp.sum(received[...].astype(F32), axis=0).astype(BF16)
    for peer in range(8):
        pieces[peer] = total


def line_kernel(scale, received, pieces, gain_out):
    total = jnp.sum(received[...].astype(F32), axis=0) * scale
    low = total[0:4].astype(BF16)
    for peer in range(16):
        pieces[peer] = low
    gain_out[...] = jnp.concatenate([total[4, 0:1], total[4, 1:2]], axis=1)


def assemble_kernel(mine, theirs, w_qkv_out, w_out_out, halves):
    at_core = lax.axis_index("c")
    halves[at_core] = mine[...]
    halves[1 - at_core] = theirs[...]
    for at in range(2 * TILES):
        half, tile = divmod(at, TILES)
        rows = halves[half, tile].astype(F32)
        if at < 96:
            row, col = divmod(at, 6)
            w_qkv_out[row * 16 : row * 16 + 16, col * LANES : (col + 1) * LANES] = rows
        else:
            row, col = divmod(at - 96, 2)
            w_out_out[row * 16 : row * 16 + 16, col * LANES : (col + 1) * LANES] = rows


def tokens_kernel(tokens, gain, third, *rest):
    groups, seconds = rest[:5], rest[5:9]
    out, from_first, from_second = rest[9:]
    here = along_first()
    from_first[here] = groups[0][0]
    for stage in range(4):
        span = 8 >> stage
        for at, mask in enumerate(sources_before(stage)):
            from_first[here ^ (mask ^ BITS[stage])] = groups[stage + 1][at * span]
    for mask, ref in enumerate(seconds):
        from_second[along_second() ^ mask] = ref[...]
    for x in range(2):
        for y in range(8):
            tokens_f = tokens[x, y].astype(F32)
            first = jnp.concatenate([from_first[y * 2, x], from_first[y * 2 + 1, x]], axis=0)
            second = jnp.concatenate([from_second[x * 2, y], from_second[x * 2 + 1, y]], axis=0)
            grad_normed = third[x, y] + first.astype(F32) + second.astype(F32)
            square = jnp.mean(tokens_f * tokens_f, axis=-1, keepdims=True) + EPSILON
            inverse = lax.rsqrt(square)
            gained = gain[...] * grad_normed
            inner = jnp.sum(gained * tokens_f, axis=-1, keepdims=True)
            result = gained * inverse - tokens_f * (inner * inverse / (WIDTH * square))
            out[x, y] = result.astype(BF16)


def shape(dims, dtype):
    return jax.ShapeDtypeStruct(dims, dtype)


def kernel_call(body, outs, operands, us, scratch=(), space=VMEM):
    return pl.pallas_call(
        body,
        out_shape=outs,
        in_specs=[space] * len(operands),
        out_specs=jax.tree.map(lambda _: space, outs),
        scratch_shapes=list(scratch),
        compiler_params=params(62 if space is HBM else 48),
        cost_estimate=cost(us),
    )(*operands)


def swap(array, axis, mask, size):
    return lax.ppermute(array, axis, [(i, i ^ mask) for i in range(size)])


def exchange(pieces, axes):
    return lax.all_to_all(pieces, axes, split_axis=0, concat_axis=0, tiled=True)


def on_device(count, tokens, attn, cotangent, gain, w_qkv, w_out):
    gain_row = gain.reshape(1, WIDTH)
    local = tokens[0]
    upstream = cotangent[0]
    flat = (TOKENS, WIDTH)
    tile = (16, LANES)
    to_first, *to_second = kernel_call(
        pieces_kernel,
        (shape((8, 2, 2, 2, ROWS, WIDTH), BF16),) + (shape((2, 8, ROWS, WIDTH), BF16),) * 4,
        (local, upstream),
        2,
        [pltpu.VMEM((2, *local.shape), BF16), pltpu.SemaphoreType.DMA((18,))],
        space=HBM,
    )
    at_first = exchange(to_first.reshape(16, 2, 2, ROWS, WIDTH), FIRST)
    at_second = [to_second[0]] + [swap(to_second[m], SECOND, m, 4) for m in (1, 2, 3)]
    third, third_qkv, part_out, third_gain = kernel_call(
        third_kernel,
        (
            shape(flat, F32),
            shape((WIDTH, TRIPLE), F32),
            shape((WIDTH, WIDTH), F32),
            shape((1, WIDTH), F32),
        ),
        (local.reshape(flat), upstream.reshape(flat), attn.reshape(flat), gain_row, w_qkv, w_out),
        5,
        SCRATCH,
    )
    packed = (
        shape((TILES + 1, *tile), F32),
        shape((HALF, *tile), BF16),
        shape((HALF + 1, *tile), BF16),
    )
    halves = pltpu.VMEM((2, TILES, *tile), F32)
    *back, own, low, high = kernel_call(
        second_kernel,
        (shape((8, ROWS, WIDTH), BF16),) * 4 + packed,
        (*at_second, gain_row, w_qkv, w_out, third_qkv, part_out, third_gain),
        5,
        SCRATCH + [halves],
    )
    from_second = [back[0]] + [swap(back[m], SECOND, m, 4) for m in (1, 2, 3)]
    early = [own, swap(low, "c", 1, 2), swap(high, "c", 1, 2)]
    block = (2, ROWS, WIDTH)
    stay, leave, own, low, high = kernel_call(
        first_kernel,
        (shape((8, *block), BF16),) * 2 + packed,
        (at_first, gain_row, w_qkv, w_out),
        5,
        SCRATCH + [pltpu.VMEM((16, *block), BF16), halves],
    )
    low, high, early, from_second = lax.optimization_barrier((low, high, early, from_second))
    late = [own, swap(low, "c", 1, 2), swap(high, "c", 1, 2)]
    groups = [stay, swap(leave, *SWAPS[0])]
    for stage in (1, 2, 3):
        leave = kernel_call(stage_kernel, shape((8, *block), BF16), groups, 20)
        groups.append(swap(leave, *SWAPS[stage]))
    pieces = kernel_call(pair_kernel, shape((16, 5, *tile), BF16), (*early, *late), 1)
    summed = exchange(pieces, PLANE)
    pieces = kernel_call(plane_kernel, shape((8, 5, *tile), BF16), (summed,), 1)
    summed = exchange(pieces, "z")
    pieces, d_gain = kernel_call(
        functools.partial(line_kernel, 1.0 / math.sqrt(count)),
        (shape((16, 4, *tile), BF16), shape((1, WIDTH), F32)),
        (summed,),
        1,
    )
    mine = exchange(pieces, PLANE)
    mine = mine.reshape(TILES, *tile)
    theirs = swap(mine, "c", 1, 2)
    d_w_qkv, d_w_out = kernel_call(
        assemble_kernel,
        (shape((WIDTH, TRIPLE), F32), shape((WIDTH, WIDTH), F32)),
        (mine, theirs),
        1,
        [pltpu.VMEM((2, TILES, *tile), BF16)],
    )
    d_tokens = kernel_call(
        tokens_kernel,
        shape(local.shape, BF16),
        (local, gain_row, third.reshape(local.shape), *groups, *from_second),
        2,
        [pltpu.VMEM((16, *block), BF16), pltpu.VMEM((4, 8, ROWS, WIDTH), BF16)],
    )
    return (d_tokens[None], d_w_qkv, d_w_out, d_gain.reshape(WIDTH))


def solution(mesh):
    fine = Mesh(mesh.devices.reshape(4, 8, 2, 2, 2), ("y", "z", "xh", "xl", "c"))
    split = P("y", FIRST, SECOND, None, None)
    count = 4 * 32 * 32 * 32
    return jax.shard_map(
        functools.partial(on_device, count),
        mesh=fine,
        in_specs=(split, split, split, P(), P(), P()),
        out_specs=(split, P(), P(), P()),
        check_vma=False,
    )
```

```python
import functools
import math

import jax
import jax.numpy as jnp
from jax import lax
from jax.experimental import pallas as pl
from jax.experimental.pallas import tpu as pltpu
from jax.sharding import Mesh
from jax.sharding import PartitionSpec as P

HEADS = 8
HEAD = 32
WIDTH = 256
TRIPLE = 3 * WIDTH
EPSILON = 1e-06
FACTOR = 1.0 / math.sqrt(HEAD)
TOKENS = 512
LENGTH = 32
GROUP = 8
PENCILS = 16
ROWS = 16
LANES = 128
HALF = 32
TILES = 64
BF16 = jnp.bfloat16
F32 = jnp.float32
VMEM = pl.BlockSpec(memory_space=pltpu.VMEM)
HBM = pl.BlockSpec(memory_space=pltpu.HBM)
PLANE = ("y", "xh", "xl")
FIRST = ("z", "xh")
SECOND = ("xl", "c")


def params(mib):
    return pltpu.CompilerParams(vmem_limit_bytes=mib * 2**20)


def cost(us):
    return pl.CostEstimate(
        flops=int(us * 8e8), bytes_accessed=int(us * 2e6), transcendentals=0
    )


def dot(left, right, left_dim, right_dim):
    return lax.dot_general(
        left, right, (((left_dim,), (right_dim,)), ((), ())), preferred_element_type=F32
    )


def attention(qkv, grad_attn, block, lane, count):
    spans = [slice(i * LENGTH, (i + 1) * LENGTH) for i in range(count)]
    k = [qkv[span, WIDTH : 2 * WIDTH] for span in spans]
    v = [qkv[span, 2 * WIDTH :] for span in spans]
    q_block = [jnp.concatenate([qkv[span, :WIDTH]] * HEADS, axis=0) * block for span in spans]
    g_block = [jnp.concatenate([grad_attn[span]] * HEADS, axis=0) * block for span in spans]
    scores = [dot(k[i], q_block[i], 1, 1) for i in range(count)]
    grad_probs = [dot(v[i], g_block[i], 1, 1) for i in range(count)]
    probs_low = []
    scores_low = []
    for i in range(count):
        top = jnp.max(scores[i], axis=0, keepdims=True)
        powers = jnp.exp((scores[i] - top) * FACTOR)
        probs = powers * (1.0 / jnp.sum(powers, axis=0, keepdims=True))
        inner = jnp.sum(probs * grad_probs[i], axis=0, keepdims=True)
        scores_low.append((probs * (grad_probs[i] - inner)).astype(BF16))
        probs_low.append(probs.astype(BF16))
    grad_v = [dot(probs_low[i], g_block[i], 1, 0) for i in range(count)]
    grad_k = [dot(scores_low[i], q_block[i], 1, 0) * FACTOR for i in range(count)]
    grad_q = [[] for _ in range(count)]
    for half in range(2):
        cols = slice(half * LANES, (half + 1) * LANES)
        for base in range(0, count, 4):
            turned = jnp.concatenate([low[:, cols] for low in scores_low[base : base + 4]], axis=0)
            turned = turned.T
            for i in range(4):
                every = dot(turned[:, spans[i]], k[base + i][:, cols], 1, 0)
                picked = every[96:128]
                for head in (2, 1, 0):
                    picked = jnp.where(
                        lane < HEAD * (head + 1), every[head * HEAD : (head + 1) * HEAD], picked
                    )
                grad_q[base + i].append(picked * FACTOR)
    joined = [
        jnp.concatenate([*grad_q[i], grad_k[i], grad_v[i]], axis=1).astype(BF16)
        for i in range(count)
    ]
    return jnp.concatenate(joined, axis=0)


def axis_grads(tokens, cotangent, gain, w_qkv, w_out, scratch, strided):
    tokens_cols, cot_cols, grad_cols, joined_rows, normed_rows = scratch
    if strided:
        tokens_f, cot_f = tokens.astype(F32), cotangent.astype(F32)
        for col in range(2):
            tokens_cols[col] = tokens_f[:, col * LANES : (col + 1) * LANES]
            cot_cols[col] = cot_f[:, col * LANES : (col + 1) * LANES]
    dims = (WIDTH, WIDTH)
    block = (
        lax.broadcasted_iota(jnp.int32, dims, 0) // HEAD
        == lax.broadcasted_iota(jnp.int32, dims, 1) // HEAD
    )
    block = block.astype(F32).astype(BF16)
    lane = lax.broadcasted_iota(jnp.int32, (LENGTH, LANES), 1)
    part_gain = jnp.zeros((1, WIDTH), F32)
    for base in range(0, PENCILS, GROUP):
        group = slice(base * LENGTH, (base + GROUP) * LENGTH)
        if strided:
            rows_of = [pl.ds(base + i, LENGTH, stride=PENCILS) for i in range(GROUP)]

            def gathered(ref):
                cols = [
                    jnp.concatenate([ref[col, rows, :] for rows in rows_of], axis=0)
                    for col in range(2)
                ]
                return jnp.concatenate(cols, axis=1)

            tokens_f = gathered(tokens_cols)
            cot = gathered(cot_cols).astype(BF16)
        else:
            rows_of = [pl.ds((base + i) * LENGTH, LENGTH) for i in range(GROUP)]
            tokens_f = tokens[group].astype(F32)
            cot = cotangent[group]
        square = jnp.mean(tokens_f * tokens_f, axis=-1, keepdims=True) + EPSILON
        unit = tokens_f * lax.rsqrt(square)
        normed = (unit * gain).astype(BF16)
        normed_rows[group] = normed
        qkv = dot(normed, w_qkv, 1, 0).astype(BF16)
        grad_attn = dot(cot, w_out, 1, 1).astype(BF16)
        joined = attention(qkv, grad_attn, block, lane, GROUP)
        joined_rows[group] = joined
        grad_normed = dot(joined, w_qkv, 1, 1)
        part_gain = part_gain + jnp.sum(grad_normed * unit, axis=0, keepdims=True)
        for i, rows in enumerate(rows_of):
            for col in range(2):
                grad_cols[col, rows, :] = grad_normed[spans_of(i), col * LANES : (col + 1) * LANES]
    part_qkv = dot(normed_rows[...], joined_rows[...], 0, 0)
    return jnp.concatenate([grad_cols[0], grad_cols[1]], axis=1), part_qkv, part_gain


def spans_of(i):
    return slice(i * LENGTH, (i + 1) * LENGTH)


BITS = (2, 8, 1, 4)
SWAPS = (("z", 1, 8), ("z", 4, 8), ("xh", 1, 2), ("z", 2, 8))


def sources_before(stage):
    masks = [0]
    for bit in BITS[:stage]:
        masks += [mask ^ bit for mask in masks]
    return masks


def span_masks(count):
    masks = [0]
    for bit in reversed(BITS[4 - count :]):
        masks += [mask ^ bit for mask in masks]
    return masks


SPANS = [span_masks(count) for count in range(4)]

SCRATCH = [pltpu.VMEM((2, TOKENS, LANES), F32)] * 3 + [
    pltpu.VMEM((TOKENS, TRIPLE), BF16),
    pltpu.VMEM((TOKENS, WIDTH), BF16),
]


def along_second():
    return lax.axis_index("xl") * 2 + lax.axis_index("c")


def along_first():
    return lax.axis_index("z") * 2 + lax.axis_index("xh")


def pieces_kernel(tokens, cotangent, to_first, *rest):
    to_second, (held, sem) = rest[:4], rest[4:]
    loads, firsts, seconds = [], [], []
    for kind, ref in enumerate((tokens, cotangent)):
        at = kind * 9
        loads.append(pltpu.make_async_copy(ref, held.at[kind], sem.at[at]))
        for x in range(2):
            for z in range(2):
                source = held.at[kind, x, :, pl.ds(z * ROWS, ROWS), :]
                target = to_first.at[:, z, kind, x]
                firsts.append(
                    (kind, pltpu.make_async_copy(source, target, sem.at[at + 1 + x * 2 + z]))
                )
        for mask, out in enumerate(to_second):
            peer = along_second() ^ mask
            rows = pl.ds(pl.multiple_of((peer & 1) * ROWS, ROWS), ROWS)
            source = held.at[kind, peer >> 1, :, rows, :]
            seconds.append(
                (kind, pltpu.make_async_copy(source, out.at[kind], sem.at[at + 5 + mask]))
            )
    for load in loads:
        load.start()
    for now, load in enumerate(loads):
        load.wait()
        for kind, store in firsts + seconds:
            if kind == now:
                store.start()
    for _, store in firsts + seconds:
        store.wait()


def third_kernel(
    tokens, cotangent, attn, gain, w_qkv, w_out, normed_out, qkv_out, out_out, gain_out, *scratch
):
    cot = cotangent[...]
    grad_normed, part_qkv, part_gain = axis_grads(
        tokens[...], cot, gain[...], w_qkv[...], w_out[...], scratch, False
    )
    normed_out[...] = grad_normed
    qkv_out[...] = part_qkv
    gain_out[...] = part_gain
    out_out[...] = dot(attn[...], cot, 0, 0)


def pack(total, part_out, part_gain, halves, own, low, high):
    for at in range(2 * TILES):
        half, tile = divmod(at, TILES)
        if at < 96:
            row, col = divmod(at, 6)
            halves[half, tile] = total[row * 16 : row * 16 + 16, col * LANES : (col + 1) * LANES]
        elif part_out is None:
            halves[half, tile] = jnp.zeros((16, LANES), F32)
        else:
            row, col = divmod(at - 96, 2)
            halves[half, tile] = part_out[row * 16 : row * 16 + 16, col * LANES : (col + 1) * LANES]
    mine = lax.axis_index("c")
    own[0:TILES] = halves[mine].astype(own.dtype)
    low[0:HALF] = halves[1 - mine, 0:HALF].astype(BF16)
    high[0:HALF] = halves[1 - mine, HALF:TILES].astype(BF16)
    gains = jnp.concatenate(
        [part_gain[:, :LANES], part_gain[:, LANES:], jnp.zeros((14, LANES), F32)], axis=0
    )
    own[TILES] = gains.astype(own.dtype)
    high[HALF] = gains.astype(BF16)


def second_kernel(*refs):
    pieces, (gain, w_qkv, w_out), parts = refs[:4], refs[4:7], refs[7:10]
    back, packed, scratch, halves = refs[10:14], refs[14:17], refs[17:-1], refs[-1]
    tokens = jnp.concatenate([piece[0].reshape(-1, WIDTH) for piece in pieces], axis=0)
    cot = jnp.concatenate([piece[1].reshape(-1, WIDTH) for piece in pieces], axis=0)
    grad_normed, part_qkv, part_gain = axis_grads(
        tokens, cot, gain[...], w_qkv[...], w_out[...], scratch, True
    )
    returned = grad_normed.astype(BF16)
    rows = TOKENS // 4
    for mask, out in enumerate(back):
        out[...] = returned[mask * rows : (mask + 1) * rows].reshape(out.shape)
    third_qkv, part_out, third_gain = parts
    pack(third_qkv[...] + part_qkv, part_out, third_gain[...] + part_gain, halves, *packed)


def first_kernel(pieces, early_own, early_low, early_high, gain, w_qkv, w_out, *refs):
    (stay, leave), packed, scratch, rest = refs[:2], refs[2:5], refs[5:-6], refs[-6:]
    returned, halves, held_own, held_low, held_high, sem = rest
    held = (held_own, held_low, held_high)
    copies = [
        pltpu.make_async_copy(source, target, sem.at[at])
        for at, (source, target) in enumerate(zip((early_own, early_low, early_high), held))
    ]
    for copy in copies:
        copy.start()
    tokens = pieces[:, 0].reshape(TOKENS, WIDTH)
    cot = pieces[:, 1].reshape(TOKENS, WIDTH)
    grad_normed, part_qkv, part_gain = axis_grads(
        tokens, cot, gain[...], w_qkv[...], w_out[...], scratch, True
    )
    returned[...] = grad_normed.astype(BF16).reshape(returned.shape)
    here = along_first()
    for at, mask in enumerate(SPANS[3]):
        stay[at] = returned[here ^ mask]
        leave[at] = returned[here ^ mask ^ BITS[0]]
    pack(part_qkv, None, part_gain, halves, *packed)
    for copy in copies:
        copy.wait()
    own = packed[0]
    own[0:HALF] += held_own[0:HALF].astype(F32) + held_low[...].astype(F32)
    own[HALF:TILES] += held_own[HALF:TILES].astype(F32) + held_high[0:HALF].astype(F32)
    own[TILES + 1] = both(held_own[TILES], held_high[HALF])


def both(mine, theirs):
    return mine.astype(BF16).astype(F32) + theirs.astype(F32)


def stage_kernel(*refs):
    groups, out = refs[:-1], refs[-1]
    left = 16 >> (len(groups) - 1)
    at = 0
    for order, ref in enumerate(groups):
        span = 8 >> max(order - 1, 0)
        for base in range(0, 8, span):
            for block in range(left // 2, left):
                out[at] = ref[base + block]
                at += 1


def pair_kernel(own, low, high, pieces):
    gains = (both(own[TILES], high[HALF]) + own[TILES + 1]).astype(BF16)
    for peer in range(16):
        half, at = divmod(peer * 4, HALF)
        received = (low, high)[half][at : at + 4].astype(F32)
        pieces[peer, 0:4] = (own[peer * 4 : peer * 4 + 4] + received).astype(BF16)
        pieces[peer, 4] = gains


def plane_kernel(received, pieces):
    total = jnp.sum(received[...].astype(F32), axis=0).astype(BF16)
    for peer in range(8):
        pieces[peer] = total


def line_kernel(scale, received, pieces, gain_out):
    total = jnp.sum(received[...].astype(F32), axis=0) * scale
    low = total[0:4].astype(BF16)
    for peer in range(16):
        pieces[peer] = low
    gain_out[...] = jnp.concatenate([total[4, 0:1], total[4, 1:2]], axis=1)


def assemble_kernel(mine, theirs, w_qkv_out, w_out_out, halves):
    at_core = lax.axis_index("c")
    halves[at_core] = mine[...]
    halves[1 - at_core] = theirs[...]
    for at in range(2 * TILES):
        half, tile = divmod(at, TILES)
        rows = halves[half, tile].astype(F32)
        if at < 96:
            row, col = divmod(at, 6)
            w_qkv_out[row * 16 : row * 16 + 16, col * LANES : (col + 1) * LANES] = rows
        else:
            row, col = divmod(at - 96, 2)
            w_out_out[row * 16 : row * 16 + 16, col * LANES : (col + 1) * LANES] = rows


def tokens_kernel(tokens, gain, third, *rest):
    groups, seconds = rest[:5], rest[5:9]
    out, from_first, from_second = rest[9:]
    here = along_first()
    from_first[here] = groups[0][0]
    for stage in range(4):
        span = 8 >> stage
        for at, mask in enumerate(sources_before(stage)):
            from_first[here ^ (mask ^ BITS[stage])] = groups[stage + 1][at * span]
    for mask, ref in enumerate(seconds):
        from_second[along_second() ^ mask] = ref[...]
    for x in range(2):
        for y in range(8):
            tokens_f = tokens[x, y].astype(F32)
            first = jnp.concatenate([from_first[y * 2, x], from_first[y * 2 + 1, x]], axis=0)
            second = jnp.concatenate([from_second[x * 2, y], from_second[x * 2 + 1, y]], axis=0)
            grad_normed = third[x, y] + first.astype(F32) + second.astype(F32)
            square = jnp.mean(tokens_f * tokens_f, axis=-1, keepdims=True) + EPSILON
            inverse = lax.rsqrt(square)
            gained = gain[...] * grad_normed
            inner = jnp.sum(gained * tokens_f, axis=-1, keepdims=True)
            result = gained * inverse - tokens_f * (inner * inverse / (WIDTH * square))
            out[x, y] = result.astype(BF16)


def shape(dims, dtype):
    return jax.ShapeDtypeStruct(dims, dtype)


def kernel_call(body, outs, operands, us, scratch=(), space=VMEM, spaces=None):
    return pl.pallas_call(
        body,
        out_shape=outs,
        in_specs=spaces or [space] * len(operands),
        out_specs=jax.tree.map(lambda _: space, outs),
        scratch_shapes=list(scratch),
        compiler_params=params(62 if space is HBM else 48),
        cost_estimate=cost(us),
    )(*operands)


def swap(array, axis, mask, size):
    return lax.ppermute(array, axis, [(i, i ^ mask) for i in range(size)])


def exchange(pieces, axes):
    return lax.all_to_all(pieces, axes, split_axis=0, concat_axis=0, tiled=True)


def on_device(count, tokens, attn, cotangent, gain, w_qkv, w_out):
    gain_row = gain.reshape(1, WIDTH)
    local = tokens[0]
    upstream = cotangent[0]
    flat = (TOKENS, WIDTH)
    tile = (16, LANES)
    to_first, *to_second = kernel_call(
        pieces_kernel,
        (shape((8, 2, 2, 2, ROWS, WIDTH), BF16),) + (shape((2, 8, ROWS, WIDTH), BF16),) * 4,
        (local, upstream),
        2,
        [pltpu.VMEM((2, *local.shape), BF16), pltpu.SemaphoreType.DMA((18,))],
        space=HBM,
    )
    at_first = exchange(to_first.reshape(16, 2, 2, ROWS, WIDTH), FIRST)
    at_second = [to_second[0]] + [swap(to_second[m], SECOND, m, 4) for m in (1, 2, 3)]
    third, third_qkv, part_out, third_gain = kernel_call(
        third_kernel,
        (
            shape(flat, F32),
            shape((WIDTH, TRIPLE), F32),
            shape((WIDTH, WIDTH), F32),
            shape((1, WIDTH), F32),
        ),
        (local.reshape(flat), upstream.reshape(flat), attn.reshape(flat), gain_row, w_qkv, w_out),
        0.1,
        SCRATCH,
    )
    packed = (
        shape((TILES + 1, *tile), BF16),
        shape((HALF, *tile), BF16),
        shape((HALF + 1, *tile), BF16),
    )
    halves = pltpu.VMEM((2, TILES, *tile), F32)
    *back, own, low, high = kernel_call(
        second_kernel,
        (shape((8, ROWS, WIDTH), BF16),) * 4 + packed,
        (*at_second, gain_row, w_qkv, w_out, third_qkv, part_out, third_gain),
        50,
        SCRATCH + [halves],
    )
    from_second = [back[0]] + [swap(back[m], SECOND, m, 4) for m in (1, 2, 3)]
    early = [own, swap(low, "c", 1, 2), swap(high, "c", 1, 2)]
    block = (2, ROWS, WIDTH)
    stay, leave, own, low, high = kernel_call(
        first_kernel,
        (
            shape((8, *block), BF16),
            shape((8, *block), BF16),
            shape((TILES + 2, *tile), F32),
            *packed[1:],
        ),
        (at_first, *early, gain_row, w_qkv, w_out),
        5,
        SCRATCH
        + [
            pltpu.VMEM((16, *block), BF16),
            halves,
            *[pltpu.VMEM(part.shape, part.dtype) for part in packed],
            pltpu.SemaphoreType.DMA((3,)),
        ],
        spaces=[VMEM] + [HBM] * 3 + [VMEM] * 3,
    )
    low, high, from_second = lax.optimization_barrier((low, high, from_second))
    late = [own, swap(low, "c", 1, 2), swap(high, "c", 1, 2)]
    groups = [stay, swap(leave, *SWAPS[0])]
    for stage in (1, 2, 3):
        leave = kernel_call(stage_kernel, shape((8, *block), BF16), groups, 20)
        groups.append(swap(leave, *SWAPS[stage]))
    pieces = kernel_call(pair_kernel, shape((16, 5, *tile), BF16), late, 1)
    summed = exchange(pieces, PLANE)
    pieces = kernel_call(plane_kernel, shape((8, 5, *tile), BF16), (summed,), 1)
    summed = exchange(pieces, "z")
    pieces, d_gain = kernel_call(
        functools.partial(line_kernel, 1.0 / math.sqrt(count)),
        (shape((16, 4, *tile), BF16), shape((1, WIDTH), F32)),
        (summed,),
        1,
    )
    mine = exchange(pieces, PLANE)
    mine = mine.reshape(TILES, *tile)
    theirs = swap(mine, "c", 1, 2)
    d_w_qkv, d_w_out = kernel_call(
        assemble_kernel,
        (shape((WIDTH, TRIPLE), F32), shape((WIDTH, WIDTH), F32)),
        (mine, theirs),
        1,
        [pltpu.VMEM((2, TILES, *tile), BF16)],
    )
    d_tokens = kernel_call(
        tokens_kernel,
        shape(local.shape, BF16),
        (local, gain_row, third.reshape(local.shape), *groups, *from_second),
        2,
        [pltpu.VMEM((16, *block), BF16), pltpu.VMEM((4, 8, ROWS, WIDTH), BF16)],
    )
    return (d_tokens[None], d_w_qkv, d_w_out, d_gain.reshape(WIDTH))


def solution(mesh):
    fine = Mesh(mesh.devices.reshape(4, 8, 2, 2, 2), ("y", "z", "xh", "xl", "c"))
    split = P("y", FIRST, SECOND, None, None)
    count = 4 * 32 * 32 * 32
    return jax.shard_map(
        functools.partial(on_device, count),
        mesh=fine,
        in_specs=(split, split, split, P(), P(), P()),
        out_specs=(split, P(), P(), P()),
        check_vma=False,
    )
```

```python
import functools
import math

import jax
import jax.numpy as jnp
from jax import lax
from jax.experimental import pallas as pl
from jax.experimental.pallas import tpu as pltpu
from jax.sharding import Mesh
from jax.sharding import PartitionSpec as P

HEADS = 8
HEAD = 32
WIDTH = 256
TRIPLE = 3 * WIDTH
EPSILON = 1e-06
FACTOR = 1.0 / math.sqrt(HEAD)
TOKENS = 512
LENGTH = 32
GROUP = 8
PENCILS = 16
ROWS = 16
LANES = 128
HALF = 32
TILES = 64
BF16 = jnp.bfloat16
F32 = jnp.float32
VMEM = pl.BlockSpec(memory_space=pltpu.VMEM)
HBM = pl.BlockSpec(memory_space=pltpu.HBM)
PLANE = ("y", "xh", "xl")
FIRST = ("z", "xh")
SECOND = ("xl", "c")


def params(mib):
    return pltpu.CompilerParams(vmem_limit_bytes=mib * 2**20)


def cost(us):
    return pl.CostEstimate(
        flops=int(us * 8e8), bytes_accessed=int(us * 2e6), transcendentals=0
    )


def dot(left, right, left_dim, right_dim):
    return lax.dot_general(
        left, right, (((left_dim,), (right_dim,)), ((), ())), preferred_element_type=F32
    )


def attention(qkv, grad_attn, block, lane, count):
    spans = [slice(i * LENGTH, (i + 1) * LENGTH) for i in range(count)]
    k = [qkv[span, WIDTH : 2 * WIDTH] for span in spans]
    v = [qkv[span, 2 * WIDTH :] for span in spans]
    q_block = [jnp.concatenate([qkv[span, :WIDTH]] * HEADS, axis=0) * block for span in spans]
    g_block = [jnp.concatenate([grad_attn[span]] * HEADS, axis=0) * block for span in spans]
    scores = [dot(k[i], q_block[i], 1, 1) for i in range(count)]
    grad_probs = [dot(v[i], g_block[i], 1, 1) for i in range(count)]
    probs_low = []
    scores_low = []
    for i in range(count):
        top = jnp.max(scores[i], axis=0, keepdims=True)
        powers = jnp.exp((scores[i] - top) * FACTOR)
        probs = powers * (1.0 / jnp.sum(powers, axis=0, keepdims=True))
        inner = jnp.sum(probs * grad_probs[i], axis=0, keepdims=True)
        scores_low.append((probs * (grad_probs[i] - inner)).astype(BF16))
        probs_low.append(probs.astype(BF16))
    grad_v = [dot(probs_low[i], g_block[i], 1, 0) for i in range(count)]
    grad_k = [dot(scores_low[i], q_block[i], 1, 0) * FACTOR for i in range(count)]
    grad_q = [[] for _ in range(count)]
    for half in range(2):
        cols = slice(half * LANES, (half + 1) * LANES)
        for base in range(0, count, 4):
            turned = jnp.concatenate([low[:, cols] for low in scores_low[base : base + 4]], axis=0)
            turned = turned.T
            for i in range(4):
                every = dot(turned[:, spans[i]], k[base + i][:, cols], 1, 0)
                picked = every[96:128]
                for head in (2, 1, 0):
                    picked = jnp.where(
                        lane < HEAD * (head + 1), every[head * HEAD : (head + 1) * HEAD], picked
                    )
                grad_q[base + i].append(picked * FACTOR)
    joined = [
        jnp.concatenate([*grad_q[i], grad_k[i], grad_v[i]], axis=1).astype(BF16)
        for i in range(count)
    ]
    return jnp.concatenate(joined, axis=0)


def axis_grads(tokens, cotangent, gain, w_qkv, w_out, scratch, strided):
    tokens_cols, cot_cols, grad_cols, joined_rows, normed_rows = scratch
    if strided:
        tokens_f, cot_f = tokens.astype(F32), cotangent.astype(F32)
        for col in range(2):
            tokens_cols[col] = tokens_f[:, col * LANES : (col + 1) * LANES]
            cot_cols[col] = cot_f[:, col * LANES : (col + 1) * LANES]
    dims = (WIDTH, WIDTH)
    block = (
        lax.broadcasted_iota(jnp.int32, dims, 0) // HEAD
        == lax.broadcasted_iota(jnp.int32, dims, 1) // HEAD
    )
    block = block.astype(F32).astype(BF16)
    lane = lax.broadcasted_iota(jnp.int32, (LENGTH, LANES), 1)
    part_gain = jnp.zeros((1, WIDTH), F32)
    for base in range(0, PENCILS, GROUP):
        group = slice(base * LENGTH, (base + GROUP) * LENGTH)
        if strided:
            rows_of = [pl.ds(base + i, LENGTH, stride=PENCILS) for i in range(GROUP)]

            def gathered(ref):
                cols = [
                    jnp.concatenate([ref[col, rows, :] for rows in rows_of], axis=0)
                    for col in range(2)
                ]
                return jnp.concatenate(cols, axis=1)

            tokens_f = gathered(tokens_cols)
            cot = gathered(cot_cols).astype(BF16)
        else:
            rows_of = [pl.ds((base + i) * LENGTH, LENGTH) for i in range(GROUP)]
            tokens_f = tokens[group].astype(F32)
            cot = cotangent[group]
        square = jnp.mean(tokens_f * tokens_f, axis=-1, keepdims=True) + EPSILON
        unit = tokens_f * lax.rsqrt(square)
        normed = (unit * gain).astype(BF16)
        normed_rows[group] = normed
        qkv = dot(normed, w_qkv, 1, 0).astype(BF16)
        grad_attn = dot(cot, w_out, 1, 1).astype(BF16)
        joined = attention(qkv, grad_attn, block, lane, GROUP)
        joined_rows[group] = joined
        grad_normed = dot(joined, w_qkv, 1, 1)
        part_gain = part_gain + jnp.sum(grad_normed * unit, axis=0, keepdims=True)
        for i, rows in enumerate(rows_of):
            for col in range(2):
                grad_cols[col, rows, :] = grad_normed[spans_of(i), col * LANES : (col + 1) * LANES]
    part_qkv = dot(normed_rows[...], joined_rows[...], 0, 0)
    return jnp.concatenate([grad_cols[0], grad_cols[1]], axis=1), part_qkv, part_gain


def spans_of(i):
    return slice(i * LENGTH, (i + 1) * LENGTH)


BITS = (2, 8, 1, 4)
SWAPS = (("z", 1, 8), ("z", 4, 8), ("xh", 1, 2), ("z", 2, 8))


def sources_before(stage):
    masks = [0]
    for bit in BITS[:stage]:
        masks += [mask ^ bit for mask in masks]
    return masks


def span_masks(count):
    masks = [0]
    for bit in reversed(BITS[4 - count :]):
        masks += [mask ^ bit for mask in masks]
    return masks


SPANS = [span_masks(count) for count in range(4)]

SCRATCH = [pltpu.VMEM((2, TOKENS, LANES), F32)] * 3 + [
    pltpu.VMEM((TOKENS, TRIPLE), BF16),
    pltpu.VMEM((TOKENS, WIDTH), BF16),
]


def along_second():
    return lax.axis_index("xl") * 2 + lax.axis_index("c")


def along_first():
    return lax.axis_index("z") * 2 + lax.axis_index("xh")


def pieces_kernel(tokens, cotangent, to_first, near, mate, far, held, sem):
    core, chip = lax.axis_index("c"), lax.axis_index("xl")
    loads, stores = [], []
    for kind, ref in enumerate((tokens, cotangent)):
        for x in range(2):
            at = len(loads) * 5
            source = held.at[kind, x]
            loads.append(pltpu.make_async_copy(ref.at[x], source, sem.at[at]))
            targets = [(z, to_first.at[:, z, kind, x]) for z in range(2)]
            copies = [
                pltpu.make_async_copy(
                    source.at[:, pl.ds(z * ROWS, ROWS), :], target, sem.at[at + 1 + z]
                )
                for z, target in targets
            ]
            stores.append(copies)
    for load in loads:
        load.start()
    for load, copies in zip(loads, stores):
        load.wait()
        for copy in copies:
            copy.start()
    late = []
    for kind in range(2):
        for other in range(2):
            z = core ^ other
            rows = pl.ds(pl.multiple_of(z * ROWS, ROWS), ROWS)
            for target, x in (((near, mate)[other].at[kind], chip), (far.at[other, kind], 1 - chip)):
                late.append(
                    pltpu.make_async_copy(
                        held.at[kind, x, :, rows, :], target, sem.at[20 + len(late)]
                    )
                )
                late[-1].start()
    for copies in stores + [late]:
        for copy in copies:
            copy.wait()


def third_kernel(
    tokens, cotangent, attn, gain, w_qkv, w_out, normed_out, qkv_out, out_out, gain_out, *scratch
):
    cot = cotangent[...]
    grad_normed, part_qkv, part_gain = axis_grads(
        tokens[...], cot, gain[...], w_qkv[...], w_out[...], scratch, False
    )
    normed_out[...] = grad_normed
    qkv_out[...] = part_qkv
    gain_out[...] = part_gain
    out_out[...] = dot(attn[...], cot, 0, 0)


def pack(total, part_out, part_gain, halves, own, low, high):
    for at in range(2 * TILES):
        half, tile = divmod(at, TILES)
        if at < 96:
            row, col = divmod(at, 6)
            halves[half, tile] = total[row * 16 : row * 16 + 16, col * LANES : (col + 1) * LANES]
        elif part_out is None:
            halves[half, tile] = jnp.zeros((16, LANES), F32)
        else:
            row, col = divmod(at - 96, 2)
            halves[half, tile] = part_out[row * 16 : row * 16 + 16, col * LANES : (col + 1) * LANES]
    mine = lax.axis_index("c")
    own[0:TILES] = halves[mine].astype(own.dtype)
    low[0:HALF] = halves[1 - mine, 0:HALF].astype(BF16)
    high[0:HALF] = halves[1 - mine, HALF:TILES].astype(BF16)
    gains = jnp.concatenate(
        [part_gain[:, :LANES], part_gain[:, LANES:], jnp.zeros((14, LANES), F32)], axis=0
    )
    own[TILES] = gains.astype(own.dtype)
    high[HALF] = gains.astype(BF16)


def second_kernel(*refs):
    pieces, (gain, w_qkv, w_out), parts = refs[:4], refs[4:7], refs[7:10]
    back, packed, scratch, halves = refs[10:14], refs[14:17], refs[17:-1], refs[-1]
    near, mate, far, passed = pieces
    pieces = (near, mate, far.at[0], passed.at[1])
    tokens = jnp.concatenate([piece[0].reshape(-1, WIDTH) for piece in pieces], axis=0)
    cot = jnp.concatenate([piece[1].reshape(-1, WIDTH) for piece in pieces], axis=0)
    grad_normed, part_qkv, part_gain = axis_grads(
        tokens, cot, gain[...], w_qkv[...], w_out[...], scratch, True
    )
    returned = grad_normed.astype(BF16)
    rows = TOKENS // 4
    for mask, out in enumerate(back):
        out[...] = returned[mask * rows : (mask + 1) * rows].reshape(out.shape)
    third_qkv, part_out, third_gain = parts
    pack(third_qkv[...] + part_qkv, part_out, third_gain[...] + part_gain, halves, *packed)


def first_kernel(pieces, early_own, early_low, early_high, gain, w_qkv, w_out, *refs):
    (stay, leave), packed, scratch, rest = refs[:2], refs[2:5], refs[5:-6], refs[-6:]
    returned, halves, held_own, held_low, held_high, sem = rest
    held = (held_own, held_low, held_high)
    copies = [
        pltpu.make_async_copy(source, target, sem.at[at])
        for at, (source, target) in enumerate(zip((early_own, early_low, early_high), held))
    ]
    for copy in copies:
        copy.start()
    tokens = pieces[:, 0].reshape(TOKENS, WIDTH)
    cot = pieces[:, 1].reshape(TOKENS, WIDTH)
    grad_normed, part_qkv, part_gain = axis_grads(
        tokens, cot, gain[...], w_qkv[...], w_out[...], scratch, True
    )
    returned[...] = grad_normed.astype(BF16).reshape(returned.shape)
    here = along_first()
    for at, mask in enumerate(SPANS[3]):
        stay[at] = returned[here ^ mask]
        leave[at] = returned[here ^ mask ^ BITS[0]]
    pack(part_qkv, None, part_gain, halves, *packed)
    for copy in copies:
        copy.wait()
    own = packed[0]
    own[0:HALF] += held_own[0:HALF].astype(F32) + held_low[...].astype(F32)
    own[HALF:TILES] += held_own[HALF:TILES].astype(F32) + held_high[0:HALF].astype(F32)
    own[TILES + 1] = both(held_own[TILES], held_high[HALF])


def both(mine, theirs):
    return mine.astype(BF16).astype(F32) + theirs.astype(F32)


def stage_kernel(*refs):
    groups, out = refs[:-1], refs[-1]
    left = 16 >> (len(groups) - 1)
    at = 0
    for order, ref in enumerate(groups):
        span = 8 >> max(order - 1, 0)
        for base in range(0, 8, span):
            for block in range(left // 2, left):
                out[at] = ref[base + block]
                at += 1


def pair_kernel(own, low, high, pieces):
    gains = (both(own[TILES], high[HALF]) + own[TILES + 1]).astype(BF16)
    for peer in range(16):
        half, at = divmod(peer * 4, HALF)
        received = (low, high)[half][at : at + 4].astype(F32)
        pieces[peer, 0:4] = (own[peer * 4 : peer * 4 + 4] + received).astype(BF16)
        pieces[peer, 4] = gains


def plane_kernel(received, pieces):
    total = jnp.sum(received[...].astype(F32), axis=0).astype(BF16)
    for peer in range(8):
        pieces[peer] = total


def line_kernel(scale, received, pieces, gain_out):
    total = jnp.sum(received[...].astype(F32), axis=0) * scale
    low = total[0:4].astype(BF16)
    for peer in range(16):
        pieces[peer] = low
    gain_out[...] = jnp.concatenate([total[4, 0:1], total[4, 1:2]], axis=1)


def assemble_kernel(mine, theirs, w_qkv_out, w_out_out, halves):
    at_core = lax.axis_index("c")
    halves[at_core] = mine[...]
    halves[1 - at_core] = theirs[...]
    for at in range(2 * TILES):
        half, tile = divmod(at, TILES)
        rows = halves[half, tile].astype(F32)
        if at < 96:
            row, col = divmod(at, 6)
            w_qkv_out[row * 16 : row * 16 + 16, col * LANES : (col + 1) * LANES] = rows
        else:
            row, col = divmod(at - 96, 2)
            w_out_out[row * 16 : row * 16 + 16, col * LANES : (col + 1) * LANES] = rows


def tokens_kernel(tokens, gain, third, *rest):
    groups, seconds = rest[:5], rest[5:9]
    out, from_first, from_second = rest[9:]
    here = along_first()
    from_first[here] = groups[0][0]
    for stage in range(4):
        span = 8 >> stage
        for at, mask in enumerate(sources_before(stage)):
            from_first[here ^ (mask ^ BITS[stage])] = groups[stage + 1][at * span]
    for mask, ref in enumerate(seconds):
        from_second[along_second() ^ mask] = ref[...]
    for x in range(2):
        for y in range(8):
            tokens_f = tokens[x, y].astype(F32)
            first = jnp.concatenate([from_first[y * 2, x], from_first[y * 2 + 1, x]], axis=0)
            second = jnp.concatenate([from_second[x * 2, y], from_second[x * 2 + 1, y]], axis=0)
            grad_normed = third[x, y] + first.astype(F32) + second.astype(F32)
            square = jnp.mean(tokens_f * tokens_f, axis=-1, keepdims=True) + EPSILON
            inverse = lax.rsqrt(square)
            gained = gain[...] * grad_normed
            inner = jnp.sum(gained * tokens_f, axis=-1, keepdims=True)
            result = gained * inverse - tokens_f * (inner * inverse / (WIDTH * square))
            out[x, y] = result.astype(BF16)


def shape(dims, dtype):
    return jax.ShapeDtypeStruct(dims, dtype)


def kernel_call(body, outs, operands, us, scratch=(), space=VMEM, spaces=None):
    return pl.pallas_call(
        body,
        out_shape=outs,
        in_specs=spaces or [space] * len(operands),
        out_specs=jax.tree.map(lambda _: space, outs),
        scratch_shapes=list(scratch),
        compiler_params=params(62 if space is HBM else 48),
        cost_estimate=cost(us),
    )(*operands)


def swap(array, axis, mask, size):
    return lax.ppermute(array, axis, [(i, i ^ mask) for i in range(size)])


def exchange(pieces, axes):
    return lax.all_to_all(pieces, axes, split_axis=0, concat_axis=0, tiled=True)


def on_device(count, tokens, attn, cotangent, gain, w_qkv, w_out):
    gain_row = gain.reshape(1, WIDTH)
    local = tokens[0]
    upstream = cotangent[0]
    flat = (TOKENS, WIDTH)
    tile = (16, LANES)
    quarter = (2, 8, ROWS, WIDTH)
    to_first, near, mate, far = kernel_call(
        pieces_kernel,
        (
            shape((8, 2, 2, 2, ROWS, WIDTH), BF16),
            shape(quarter, BF16),
            shape(quarter, BF16),
            shape((2, *quarter), BF16),
        ),
        (local, upstream),
        2,
        [pltpu.VMEM((2, *local.shape), BF16), pltpu.SemaphoreType.DMA((28,))],
        space=HBM,
    )
    at_first = exchange(to_first.reshape(16, 2, 2, ROWS, WIDTH), FIRST)
    far = swap(far, "xl", 1, 2)
    at_second = [near, swap(mate, "c", 1, 2), far, swap(far, "c", 1, 2)]
    third, third_qkv, part_out, third_gain = kernel_call(
        third_kernel,
        (
            shape(flat, F32),
            shape((WIDTH, TRIPLE), F32),
            shape((WIDTH, WIDTH), F32),
            shape((1, WIDTH), F32),
        ),
        (local.reshape(flat), upstream.reshape(flat), attn.reshape(flat), gain_row, w_qkv, w_out),
        5,
        SCRATCH,
    )
    packed = (
        shape((TILES + 1, *tile), BF16),
        shape((HALF, *tile), BF16),
        shape((HALF + 1, *tile), BF16),
    )
    halves = pltpu.VMEM((2, TILES, *tile), F32)
    *back, own, low, high = kernel_call(
        second_kernel,
        (shape((8, ROWS, WIDTH), BF16),) * 4 + packed,
        (*at_second, gain_row, w_qkv, w_out, third_qkv, part_out, third_gain),
        5,
        SCRATCH + [halves],
    )
    from_second = [back[0]] + [swap(back[m], SECOND, m, 4) for m in (1, 2, 3)]
    early = [own, swap(low, "c", 1, 2), swap(high, "c", 1, 2)]
    block = (2, ROWS, WIDTH)
    stay, leave, own, low, high = kernel_call(
        first_kernel,
        (
            shape((8, *block), BF16),
            shape((8, *block), BF16),
            shape((TILES + 2, *tile), F32),
            *packed[1:],
        ),
        (at_first, *early, gain_row, w_qkv, w_out),
        5,
        SCRATCH
        + [
            pltpu.VMEM((16, *block), BF16),
            halves,
            *[pltpu.VMEM(part.shape, part.dtype) for part in packed],
            pltpu.SemaphoreType.DMA((3,)),
        ],
        spaces=[VMEM] + [HBM] * 3 + [VMEM] * 3,
    )
    low, high, from_second = lax.optimization_barrier((low, high, from_second))
    late = [own, swap(low, "c", 1, 2), swap(high, "c", 1, 2)]
    groups = [stay, swap(leave, *SWAPS[0])]
    for stage in (1, 2, 3):
        leave = kernel_call(stage_kernel, shape((8, *block), BF16), groups, 20)
        groups.append(swap(leave, *SWAPS[stage]))
    pieces = kernel_call(pair_kernel, shape((16, 5, *tile), BF16), late, 1)
    summed = exchange(pieces, PLANE)
    pieces = kernel_call(plane_kernel, shape((8, 5, *tile), BF16), (summed,), 1)
    summed = exchange(pieces, "z")
    pieces, d_gain = kernel_call(
        functools.partial(line_kernel, 1.0 / math.sqrt(count)),
        (shape((16, 4, *tile), BF16), shape((1, WIDTH), F32)),
        (summed,),
        1,
    )
    mine = exchange(pieces, PLANE)
    mine = mine.reshape(TILES, *tile)
    theirs = swap(mine, "c", 1, 2)
    d_w_qkv, d_w_out = kernel_call(
        assemble_kernel,
        (shape((WIDTH, TRIPLE), F32), shape((WIDTH, WIDTH), F32)),
        (mine, theirs),
        1,
        [pltpu.VMEM((2, TILES, *tile), BF16)],
    )
    d_tokens = kernel_call(
        tokens_kernel,
        shape(local.shape, BF16),
        (local, gain_row, third.reshape(local.shape), *groups, *from_second),
        2,
        [pltpu.VMEM((16, *block), BF16), pltpu.VMEM((4, 8, ROWS, WIDTH), BF16)],
    )
    return (d_tokens[None], d_w_qkv, d_w_out, d_gain.reshape(WIDTH))


def solution(mesh):
    fine = Mesh(mesh.devices.reshape(4, 8, 2, 2, 2), ("y", "z", "xh", "xl", "c"))
    split = P("y", FIRST, SECOND, None, None)
    count = 4 * 32 * 32 * 32
    return jax.shard_map(
        functools.partial(on_device, count),
        mesh=fine,
        in_specs=(split, split, split, P(), P(), P()),
        out_specs=(split, P(), P(), P()),
        check_vma=False,
    )
```

```python
import functools
import math

import jax
import jax.numpy as jnp
from jax import lax
from jax.experimental import pallas as pl
from jax.experimental.pallas import tpu as pltpu
from jax.sharding import Mesh
from jax.sharding import PartitionSpec as P

HEADS = 8
HEAD = 32
WIDTH = 256
TRIPLE = 3 * WIDTH
EPSILON = 1e-06
FACTOR = 1.0 / math.sqrt(HEAD)
TOKENS = 512
LENGTH = 32
GROUP = 8
PENCILS = 16
ROWS = 16
LANES = 128
HALF = 32
TILES = 64
BF16 = jnp.bfloat16
F32 = jnp.float32
VMEM = pl.BlockSpec(memory_space=pltpu.VMEM)
HBM = pl.BlockSpec(memory_space=pltpu.HBM)
PLANE = ("y", "xh", "xl")
FIRST = ("z", "xh")
SECOND = ("xl", "c")


def params(mib):
    return pltpu.CompilerParams(vmem_limit_bytes=mib * 2**20)


def cost(us):
    return pl.CostEstimate(
        flops=int(us * 8e8), bytes_accessed=int(us * 2e6), transcendentals=0
    )


def dot(left, right, left_dim, right_dim):
    return lax.dot_general(
        left, right, (((left_dim,), (right_dim,)), ((), ())), preferred_element_type=F32
    )


def attention(qkv, grad_attn, block, lane, count):
    spans = [slice(i * LENGTH, (i + 1) * LENGTH) for i in range(count)]
    k = [qkv[span, WIDTH : 2 * WIDTH] for span in spans]
    v = [qkv[span, 2 * WIDTH :] for span in spans]
    q_block = [jnp.concatenate([qkv[span, :WIDTH]] * HEADS, axis=0) * block for span in spans]
    g_block = [jnp.concatenate([grad_attn[span]] * HEADS, axis=0) * block for span in spans]
    scores = [dot(k[i], q_block[i], 1, 1) for i in range(count)]
    grad_probs = [dot(v[i], g_block[i], 1, 1) for i in range(count)]
    probs_low = []
    scores_low = []
    for i in range(count):
        top = jnp.max(scores[i], axis=0, keepdims=True)
        powers = jnp.exp((scores[i] - top) * FACTOR)
        probs = powers * (1.0 / jnp.sum(powers, axis=0, keepdims=True))
        inner = jnp.sum(probs * grad_probs[i], axis=0, keepdims=True)
        scores_low.append((probs * (grad_probs[i] - inner)).astype(BF16))
        probs_low.append(probs.astype(BF16))
    grad_v = [dot(probs_low[i], g_block[i], 1, 0) for i in range(count)]
    grad_k = [dot(scores_low[i], q_block[i], 1, 0) * FACTOR for i in range(count)]
    grad_q = [[] for _ in range(count)]
    for half in range(2):
        cols = slice(half * LANES, (half + 1) * LANES)
        for base in range(0, count, 4):
            turned = jnp.concatenate([low[:, cols] for low in scores_low[base : base + 4]], axis=0)
            turned = turned.T
            for i in range(4):
                every = dot(turned[:, spans[i]], k[base + i][:, cols], 1, 0)
                picked = every[96:128]
                for head in (2, 1, 0):
                    picked = jnp.where(
                        lane < HEAD * (head + 1), every[head * HEAD : (head + 1) * HEAD], picked
                    )
                grad_q[base + i].append(picked * FACTOR)
    joined = [
        jnp.concatenate([*grad_q[i], grad_k[i], grad_v[i]], axis=1).astype(BF16)
        for i in range(count)
    ]
    return jnp.concatenate(joined, axis=0)


def axis_grads(tokens, cotangent, gain, w_qkv, w_out, scratch, strided):
    tokens_cols, cot_cols, grad_cols, joined_rows, normed_rows = scratch
    if strided:
        tokens_f, cot_f = tokens.astype(F32), cotangent.astype(F32)
        for col in range(2):
            tokens_cols[col] = tokens_f[:, col * LANES : (col + 1) * LANES]
            cot_cols[col] = cot_f[:, col * LANES : (col + 1) * LANES]
    dims = (WIDTH, WIDTH)
    block = (
        lax.broadcasted_iota(jnp.int32, dims, 0) // HEAD
        == lax.broadcasted_iota(jnp.int32, dims, 1) // HEAD
    )
    block = block.astype(F32).astype(BF16)
    lane = lax.broadcasted_iota(jnp.int32, (LENGTH, LANES), 1)
    for base in range(0, PENCILS, GROUP):
        group = slice(base * LENGTH, (base + GROUP) * LENGTH)
        if strided:
            rows_of = [pl.ds(base + i, LENGTH, stride=PENCILS) for i in range(GROUP)]

            def gathered(ref):
                cols = [
                    jnp.concatenate([ref[col, rows, :] for rows in rows_of], axis=0)
                    for col in range(2)
                ]
                return jnp.concatenate(cols, axis=1)

            tokens_f = gathered(tokens_cols)
            cot = gathered(cot_cols).astype(BF16)
        else:
            rows_of = [pl.ds((base + i) * LENGTH, LENGTH) for i in range(GROUP)]
            tokens_f = tokens[group].astype(F32)
            cot = cotangent[group]
        square = jnp.mean(tokens_f * tokens_f, axis=-1, keepdims=True) + EPSILON
        normed = (tokens_f * lax.rsqrt(square) * gain).astype(BF16)
        normed_rows[group] = normed
        qkv = dot(normed, w_qkv, 1, 0).astype(BF16)
        grad_attn = dot(cot, w_out, 1, 1).astype(BF16)
        joined = attention(qkv, grad_attn, block, lane, GROUP)
        joined_rows[group] = joined
        grad_normed = dot(joined, w_qkv, 1, 1)
        for i, rows in enumerate(rows_of):
            for col in range(2):
                grad_cols[col, rows, :] = grad_normed[spans_of(i), col * LANES : (col + 1) * LANES]
    part_qkv = dot(normed_rows[...], joined_rows[...], 0, 0)
    return jnp.concatenate([grad_cols[0], grad_cols[1]], axis=1), part_qkv


def spans_of(i):
    return slice(i * LENGTH, (i + 1) * LENGTH)


BITS = (2, 8, 1, 4)
SWAPS = (("z", 1, 8), ("z", 4, 8), ("xh", 1, 2), ("z", 2, 8))


def sources_before(stage):
    masks = [0]
    for bit in BITS[:stage]:
        masks += [mask ^ bit for mask in masks]
    return masks


def span_masks(count):
    masks = [0]
    for bit in reversed(BITS[4 - count :]):
        masks += [mask ^ bit for mask in masks]
    return masks


SPANS = [span_masks(count) for count in range(4)]

SCRATCH = [pltpu.VMEM((2, TOKENS, LANES), F32)] * 3 + [
    pltpu.VMEM((TOKENS, TRIPLE), BF16),
    pltpu.VMEM((TOKENS, WIDTH), BF16),
]


def along_second():
    return lax.axis_index("xl") * 2 + lax.axis_index("c")


def along_first():
    return lax.axis_index("z") * 2 + lax.axis_index("xh")


def pieces_kernel(tokens, cotangent, to_first, far, held, sem):
    core, chip = lax.axis_index("c"), lax.axis_index("xl")
    loads, stores = [], []
    for kind, ref in enumerate((tokens, cotangent)):
        for x in range(2):
            at = len(loads) * 3
            source = held.at[kind, x]
            loads.append(pltpu.make_async_copy(ref.at[x], source, sem.at[at]))
            stores.append(
                [
                    pltpu.make_async_copy(
                        source.at[:, pl.ds(z * ROWS, ROWS), :],
                        to_first.at[:, z, kind, x],
                        sem.at[at + 1 + z],
                    )
                    for z in range(2)
                ]
            )
    for load in loads:
        load.start()
    for load, copies in zip(loads, stores):
        load.wait()
        for copy in copies:
            copy.start()
    late = []
    for kind in range(2):
        for other in range(2):
            rows = pl.ds(pl.multiple_of((core ^ other) * ROWS, ROWS), ROWS)
            late.append(
                pltpu.make_async_copy(
                    held.at[kind, 1 - chip, :, rows, :], far.at[other, kind], sem.at[12 + len(late)]
                )
            )
            late[-1].start()
    for copies in stores + [late]:
        for copy in copies:
            copy.wait()


def chip_pieces_kernel(tokens, cotangent, near, mate):
    core, chip = lax.axis_index("c"), lax.axis_index("xl")
    for other, out in enumerate((near, mate)):
        rows = pl.ds(pl.multiple_of((core ^ other) * ROWS, ROWS), ROWS)
        for kind, ref in enumerate((tokens, cotangent)):
            out[kind] = ref[chip, :, rows, :]


def third_kernel(
    tokens, cotangent, attn, gain, w_qkv, w_out, normed_out, qkv_out, out_out, *scratch
):
    cot = cotangent[...]
    grad_normed, part_qkv = axis_grads(
        tokens[...], cot, gain[...], w_qkv[...], w_out[...], scratch, False
    )
    normed_out[...] = grad_normed
    qkv_out[...] = part_qkv
    out_out[...] = dot(attn[...], cot, 0, 0)


def pack(total, part_out, halves, own, low, high):
    for at in range(2 * TILES):
        half, tile = divmod(at, TILES)
        if at < 96:
            row, col = divmod(at, 6)
            halves[half, tile] = total[row * 16 : row * 16 + 16, col * LANES : (col + 1) * LANES]
        elif part_out is None:
            halves[half, tile] = jnp.zeros((16, LANES), F32)
        else:
            row, col = divmod(at - 96, 2)
            halves[half, tile] = part_out[row * 16 : row * 16 + 16, col * LANES : (col + 1) * LANES]
    mine = lax.axis_index("c")
    own[0:TILES] = halves[mine].astype(own.dtype)
    low[0:HALF] = halves[1 - mine, 0:HALF].astype(BF16)
    high[0:HALF] = halves[1 - mine, HALF:TILES].astype(BF16)


def second_kernel(*refs):
    pieces, (gain, w_qkv, w_out), parts = refs[:4], refs[4:7], refs[7:9]
    back, packed, scratch, halves = refs[9:13], refs[13:16], refs[16:-1], refs[-1]
    near, mate, far, passed = pieces
    pieces = (near, mate, far.at[0], passed.at[1])
    tokens = jnp.concatenate([piece[0].reshape(-1, WIDTH) for piece in pieces], axis=0)
    cot = jnp.concatenate([piece[1].reshape(-1, WIDTH) for piece in pieces], axis=0)
    grad_normed, part_qkv = axis_grads(
        tokens, cot, gain[...], w_qkv[...], w_out[...], scratch, True
    )
    returned = grad_normed.astype(BF16)
    rows = TOKENS // 4
    for mask, out in enumerate(back):
        out[...] = returned[mask * rows : (mask + 1) * rows].reshape(out.shape)
    third_qkv, part_out = parts
    pack(third_qkv[...] + part_qkv, part_out, halves, *packed)


def first_kernel(pieces, early_own, early_low, early_high, gain, w_qkv, w_out, *refs):
    (stay, leave), packed, scratch, rest = refs[:2], refs[2:5], refs[5:-6], refs[-6:]
    returned, halves, held_own, held_low, held_high, sem = rest
    held = (held_own, held_low, held_high)
    copies = [
        pltpu.make_async_copy(source, target, sem.at[at])
        for at, (source, target) in enumerate(zip((early_own, early_low, early_high), held))
    ]
    for copy in copies:
        copy.start()
    tokens = pieces[:, 0].reshape(TOKENS, WIDTH)
    cot = pieces[:, 1].reshape(TOKENS, WIDTH)
    grad_normed, part_qkv = axis_grads(
        tokens, cot, gain[...], w_qkv[...], w_out[...], scratch, True
    )
    returned[...] = grad_normed.astype(BF16).reshape(returned.shape)
    here = along_first()
    for at, mask in enumerate(SPANS[3]):
        stay[at] = returned[here ^ mask]
        leave[at] = returned[here ^ mask ^ BITS[0]]
    pack(part_qkv, None, halves, *packed)
    for copy in copies:
        copy.wait()
    own = packed[0]
    own[0:HALF] += held_own[0:HALF].astype(F32) + held_low[...].astype(F32)
    own[HALF:TILES] += held_own[HALF:TILES].astype(F32) + held_high[...].astype(F32)


def stage_kernel(*refs):
    groups, out = refs[:-1], refs[-1]
    left = 16 >> (len(groups) - 1)
    at = 0
    for order, ref in enumerate(groups):
        span = 8 >> max(order - 1, 0)
        for base in range(0, 8, span):
            for block in range(left // 2, left):
                out[at] = ref[base + block]
                at += 1


def pair_kernel(own, low, high, pieces):
    for peer in range(16):
        half, at = divmod(peer * 4, HALF)
        received = (low, high)[half][at : at + 4].astype(F32)
        pieces[peer] = (own[peer * 4 : peer * 4 + 4] + received).astype(BF16)


def plane_kernel(received, pieces):
    total = jnp.sum(received[...].astype(F32), axis=0).astype(BF16)
    for peer in range(8):
        pieces[peer] = total


def line_kernel(scale, received, pieces):
    total = (jnp.sum(received[...].astype(F32), axis=0) * scale).astype(BF16)
    for peer in range(16):
        pieces[peer] = total


def assemble_kernel(mine, theirs, gain, w_qkv, w_qkv_out, w_out_out, gain_out, halves):
    at_core = lax.axis_index("c")
    halves[at_core] = mine[...]
    halves[1 - at_core] = theirs[...]
    for at in range(2 * TILES):
        half, tile = divmod(at, TILES)
        rows = halves[half, tile].astype(F32)
        if at < 96:
            row, col = divmod(at, 6)
            w_qkv_out[row * 16 : row * 16 + 16, col * LANES : (col + 1) * LANES] = rows
        else:
            row, col = divmod(at - 96, 2)
            w_out_out[row * 16 : row * 16 + 16, col * LANES : (col + 1) * LANES] = rows
    products = jnp.zeros((WIDTH, LANES), F32)
    for col in range(6):
        cols = slice(col * LANES, (col + 1) * LANES)
        products = products + w_qkv_out[:, cols] * w_qkv[:, cols].astype(F32)
    ones = jnp.ones((8, LANES), BF16)
    high = products.astype(BF16)
    low = (products - high.astype(F32)).astype(BF16)
    total = dot(ones, high, 1, 1) + dot(ones, low, 1, 1)
    gain_out[...] = total[0:1] / gain[...]


def tokens_kernel(tokens, gain, third, *rest):
    groups, seconds = rest[:5], rest[5:9]
    out, from_first, from_second = rest[9:]
    here = along_first()
    from_first[here] = groups[0][0]
    for stage in range(4):
        span = 8 >> stage
        for at, mask in enumerate(sources_before(stage)):
            from_first[here ^ (mask ^ BITS[stage])] = groups[stage + 1][at * span]
    for mask, ref in enumerate(seconds):
        from_second[along_second() ^ mask] = ref[...]
    for x in range(2):
        for y in range(8):
            tokens_f = tokens[x, y].astype(F32)
            first = jnp.concatenate([from_first[y * 2, x], from_first[y * 2 + 1, x]], axis=0)
            second = jnp.concatenate([from_second[x * 2, y], from_second[x * 2 + 1, y]], axis=0)
            grad_normed = third[x, y] + first.astype(F32) + second.astype(F32)
            square = jnp.mean(tokens_f * tokens_f, axis=-1, keepdims=True) + EPSILON
            inverse = lax.rsqrt(square)
            gained = gain[...] * grad_normed
            inner = jnp.sum(gained * tokens_f, axis=-1, keepdims=True)
            result = gained * inverse - tokens_f * (inner * inverse / (WIDTH * square))
            out[x, y] = result.astype(BF16)


def shape(dims, dtype):
    return jax.ShapeDtypeStruct(dims, dtype)


def kernel_call(body, outs, operands, us, scratch=(), space=VMEM, spaces=None):
    return pl.pallas_call(
        body,
        out_shape=outs,
        in_specs=spaces or [space] * len(operands),
        out_specs=jax.tree.map(lambda _: space, outs),
        scratch_shapes=list(scratch),
        compiler_params=params(62 if space is HBM else 48),
        cost_estimate=cost(us),
    )(*operands)


def swap(array, axis, mask, size):
    return lax.ppermute(array, axis, [(i, i ^ mask) for i in range(size)])


def exchange(pieces, axes):
    return lax.all_to_all(pieces, axes, split_axis=0, concat_axis=0, tiled=True)


def on_device(count, tokens, attn, cotangent, gain, w_qkv, w_out):
    gain_row = gain.reshape(1, WIDTH)
    local = tokens[0]
    upstream = cotangent[0]
    flat = (TOKENS, WIDTH)
    tile = (16, LANES)
    quarter = (2, 8, ROWS, WIDTH)
    to_first, far = kernel_call(
        pieces_kernel,
        (shape((8, 2, 2, 2, ROWS, WIDTH), BF16), shape((2, *quarter), BF16)),
        (local, upstream),
        2,
        [pltpu.VMEM((2, *local.shape), BF16), pltpu.SemaphoreType.DMA((16,))],
        space=HBM,
    )
    at_first = exchange(to_first.reshape(16, 2, 2, ROWS, WIDTH), FIRST)
    far = swap(far, "xl", 1, 2)
    near, mate = kernel_call(
        chip_pieces_kernel, (shape(quarter, BF16),) * 2, (local, upstream), 1
    )
    at_second = [near, swap(mate, "c", 1, 2), far, swap(far, "c", 1, 2)]
    third, third_qkv, part_out = kernel_call(
        third_kernel,
        (shape(flat, F32), shape((WIDTH, TRIPLE), F32), shape((WIDTH, WIDTH), F32)),
        (local.reshape(flat), upstream.reshape(flat), attn.reshape(flat), gain_row, w_qkv, w_out),
        5,
        SCRATCH,
    )
    packed = (
        shape((TILES, *tile), BF16),
        shape((HALF, *tile), BF16),
        shape((HALF, *tile), BF16),
    )
    halves = pltpu.VMEM((2, TILES, *tile), F32)
    *back, own, low, high = kernel_call(
        second_kernel,
        (shape((8, ROWS, WIDTH), BF16),) * 4 + packed,
        (*at_second, gain_row, w_qkv, w_out, third_qkv, part_out),
        5,
        SCRATCH + [halves],
    )
    from_second = [back[0]] + [swap(back[m], SECOND, m, 4) for m in (1, 2, 3)]
    early = [own, swap(low, "c", 1, 2), swap(high, "c", 1, 2)]
    block = (2, ROWS, WIDTH)
    stay, leave, own, low, high = kernel_call(
        first_kernel,
        (
            shape((8, *block), BF16),
            shape((8, *block), BF16),
            shape((TILES, *tile), F32),
            *packed[1:],
        ),
        (at_first, *early, gain_row, w_qkv, w_out),
        5,
        SCRATCH
        + [
            pltpu.VMEM((16, *block), BF16),
            halves,
            *[pltpu.VMEM(part.shape, part.dtype) for part in packed],
            pltpu.SemaphoreType.DMA((3,)),
        ],
        spaces=[VMEM] + [HBM] * 3 + [VMEM] * 3,
    )
    low, high, from_second = lax.optimization_barrier((low, high, from_second))
    late = [own, swap(low, "c", 1, 2), swap(high, "c", 1, 2)]
    groups = [stay, swap(leave, *SWAPS[0])]
    for stage in (1, 2, 3):
        leave = kernel_call(stage_kernel, shape((8, *block), BF16), groups, 20)
        groups.append(swap(leave, *SWAPS[stage]))
    pieces = kernel_call(pair_kernel, shape((16, 4, *tile), BF16), late, 1)
    summed = exchange(pieces, PLANE)
    pieces = kernel_call(plane_kernel, shape((8, 4, *tile), BF16), (summed,), 1)
    summed = exchange(pieces, "z")
    pieces = kernel_call(
        functools.partial(line_kernel, 1.0 / math.sqrt(count)),
        shape((16, 4, *tile), BF16),
        (summed,),
        1,
    )
    mine = exchange(pieces, PLANE)
    mine = mine.reshape(TILES, *tile)
    theirs = swap(mine, "c", 1, 2)
    d_w_qkv, d_w_out, d_gain = kernel_call(
        assemble_kernel,
        (
            shape((WIDTH, TRIPLE), F32),
            shape((WIDTH, WIDTH), F32),
            shape((1, WIDTH), F32),
        ),
        (mine, theirs, gain_row, w_qkv),
        1,
        [pltpu.VMEM((2, TILES, *tile), BF16)],
    )
    d_tokens = kernel_call(
        tokens_kernel,
        shape(local.shape, BF16),
        (local, gain_row, third.reshape(local.shape), *groups, *from_second),
        2,
        [pltpu.VMEM((16, *block), BF16), pltpu.VMEM((4, 8, ROWS, WIDTH), BF16)],
    )
    return (d_tokens[None], d_w_qkv, d_w_out, d_gain.reshape(WIDTH))


def solution(mesh):
    fine = Mesh(mesh.devices.reshape(4, 8, 2, 2, 2), ("y", "z", "xh", "xl", "c"))
    split = P("y", FIRST, SECOND, None, None)
    count = 4 * 32 * 32 * 32
    return jax.shard_map(
        functools.partial(on_device, count),
        mesh=fine,
        in_specs=(split, split, split, P(), P(), P()),
        out_specs=(split, P(), P(), P()),
        check_vma=False,
    )
```

```python
import functools
import math

import jax
import jax.numpy as jnp
from jax import lax
from jax.experimental import pallas as pl
from jax.experimental.pallas import tpu as pltpu
from jax.sharding import Mesh
from jax.sharding import PartitionSpec as P

HEADS = 8
HEAD = 32
WIDTH = 256
TRIPLE = 3 * WIDTH
EPSILON = 1e-06
FACTOR = 1.0 / math.sqrt(HEAD)
TOKENS = 512
LENGTH = 32
GROUP = 8
PENCILS = 16
ROWS = 16
LANES = 128
HALF = 32
TILES = 64
BF16 = jnp.bfloat16
F32 = jnp.float32
VMEM = pl.BlockSpec(memory_space=pltpu.VMEM)
HBM = pl.BlockSpec(memory_space=pltpu.HBM)
PLANE = ("xh", "xl", "y")
FIRST = ("xh", "z")
SECOND = ("xl", "c")


def params(mib):
    return pltpu.CompilerParams(vmem_limit_bytes=mib * 2**20)


def cost(us):
    return pl.CostEstimate(
        flops=int(us * 8e8), bytes_accessed=int(us * 2e6), transcendentals=0
    )


def dot(left, right, left_dim, right_dim):
    return lax.dot_general(
        left, right, (((left_dim,), (right_dim,)), ((), ())), preferred_element_type=F32
    )


def attention(qkv, grad_attn, block, lane, count):
    spans = [slice(i * LENGTH, (i + 1) * LENGTH) for i in range(count)]
    k = [qkv[span, WIDTH : 2 * WIDTH] for span in spans]
    v = [qkv[span, 2 * WIDTH :] for span in spans]
    q_block = [jnp.concatenate([qkv[span, :WIDTH]] * HEADS, axis=0) * block for span in spans]
    g_block = [jnp.concatenate([grad_attn[span]] * HEADS, axis=0) * block for span in spans]
    scores = [dot(k[i], q_block[i], 1, 1) for i in range(count)]
    grad_probs = [dot(v[i], g_block[i], 1, 1) for i in range(count)]
    probs_low = []
    scores_low = []
    for i in range(count):
        top = jnp.max(scores[i], axis=0, keepdims=True)
        powers = jnp.exp((scores[i] - top) * FACTOR)
        probs = powers * (1.0 / jnp.sum(powers, axis=0, keepdims=True))
        inner = jnp.sum(probs * grad_probs[i], axis=0, keepdims=True)
        scores_low.append((probs * (grad_probs[i] - inner)).astype(BF16))
        probs_low.append(probs.astype(BF16))
    grad_v = [dot(probs_low[i], g_block[i], 1, 0) for i in range(count)]
    grad_k = [dot(scores_low[i], q_block[i], 1, 0) * FACTOR for i in range(count)]
    grad_q = [[] for _ in range(count)]
    for half in range(2):
        cols = slice(half * LANES, (half + 1) * LANES)
        for base in range(0, count, 4):
            turned = jnp.concatenate([low[:, cols] for low in scores_low[base : base + 4]], axis=0)
            turned = turned.T
            for i in range(4):
                every = dot(turned[:, spans[i]], k[base + i][:, cols], 1, 0)
                picked = every[96:128]
                for head in (2, 1, 0):
                    picked = jnp.where(
                        lane < HEAD * (head + 1), every[head * HEAD : (head + 1) * HEAD], picked
                    )
                grad_q[base + i].append(picked * FACTOR)
    joined = [
        jnp.concatenate([*grad_q[i], grad_k[i], grad_v[i]], axis=1).astype(BF16)
        for i in range(count)
    ]
    return jnp.concatenate(joined, axis=0)


def axis_grads(tokens, cotangent, gain, w_qkv, w_out, scratch, strided):
    tokens_cols, cot_cols, grad_cols, joined_rows, normed_rows = scratch
    if strided:
        tokens_f, cot_f = tokens.astype(F32), cotangent.astype(F32)
        for col in range(2):
            tokens_cols[col] = tokens_f[:, col * LANES : (col + 1) * LANES]
            cot_cols[col] = cot_f[:, col * LANES : (col + 1) * LANES]
    dims = (WIDTH, WIDTH)
    block = (
        lax.broadcasted_iota(jnp.int32, dims, 0) // HEAD
        == lax.broadcasted_iota(jnp.int32, dims, 1) // HEAD
    )
    block = block.astype(F32).astype(BF16)
    lane = lax.broadcasted_iota(jnp.int32, (LENGTH, LANES), 1)
    for base in range(0, PENCILS, GROUP):
        group = slice(base * LENGTH, (base + GROUP) * LENGTH)
        if strided:
            rows_of = [pl.ds(base + i, LENGTH, stride=PENCILS) for i in range(GROUP)]

            def gathered(ref):
                cols = [
                    jnp.concatenate([ref[col, rows, :] for rows in rows_of], axis=0)
                    for col in range(2)
                ]
                return jnp.concatenate(cols, axis=1)

            tokens_f = gathered(tokens_cols)
            cot = gathered(cot_cols).astype(BF16)
        else:
            rows_of = [pl.ds((base + i) * LENGTH, LENGTH) for i in range(GROUP)]
            tokens_f = tokens[group].astype(F32)
            cot = cotangent[group]
        square = jnp.mean(tokens_f * tokens_f, axis=-1, keepdims=True) + EPSILON
        normed = (tokens_f * lax.rsqrt(square) * gain).astype(BF16)
        normed_rows[group] = normed
        qkv = dot(normed, w_qkv, 1, 0).astype(BF16)
        grad_attn = dot(cot, w_out, 1, 1).astype(BF16)
        joined = attention(qkv, grad_attn, block, lane, GROUP)
        joined_rows[group] = joined
        grad_normed = dot(joined, w_qkv, 1, 1)
        for i, rows in enumerate(rows_of):
            for col in range(2):
                grad_cols[col, rows, :] = grad_normed[spans_of(i), col * LANES : (col + 1) * LANES]
    part_qkv = dot(normed_rows[...], joined_rows[...], 0, 0)
    return jnp.concatenate([grad_cols[0], grad_cols[1]], axis=1), part_qkv


def spans_of(i):
    return slice(i * LENGTH, (i + 1) * LENGTH)


BITS = (1, 4, 8, 2)
SWAPS = (("z", 1, 8), ("z", 4, 8), ("xh", 1, 2), ("z", 2, 8))


def sources_before(stage):
    masks = [0]
    for bit in BITS[:stage]:
        masks += [mask ^ bit for mask in masks]
    return masks


def span_masks(count):
    masks = [0]
    for bit in reversed(BITS[4 - count :]):
        masks += [mask ^ bit for mask in masks]
    return masks


SPANS = [span_masks(count) for count in range(4)]

SCRATCH = [pltpu.VMEM((2, TOKENS, LANES), F32)] * 3 + [
    pltpu.VMEM((TOKENS, TRIPLE), BF16),
    pltpu.VMEM((TOKENS, WIDTH), BF16),
]


def along_second():
    return lax.axis_index("xl") * 2 + lax.axis_index("c")


def along_first():
    return lax.axis_index("xh") * 8 + lax.axis_index("z")


def pieces_kernel(tokens, cotangent, to_first, far, held, sem):
    core, chip = lax.axis_index("c"), lax.axis_index("xl")
    loads = [
        pltpu.make_async_copy(ref, held.at[kind], sem.at[kind])
        for kind, ref in enumerate((tokens, cotangent))
    ]
    for load in loads:
        load.start()
    for kind, load in enumerate(loads):
        load.wait()
        for x in range(2):
            for z in range(2):
                to_first[:, z, kind, x] = held[kind, x, :, z * ROWS : (z + 1) * ROWS, :]
        for other in range(2):
            rows = pl.ds(pl.multiple_of((core ^ other) * ROWS, ROWS), ROWS)
            far[other, kind] = held[kind, 1 - chip, :, rows, :]


def chip_pieces_kernel(tokens, cotangent, near, mate):
    core, chip = lax.axis_index("c"), lax.axis_index("xl")
    for other, out in enumerate((near, mate)):
        rows = pl.ds(pl.multiple_of((core ^ other) * ROWS, ROWS), ROWS)
        for kind, ref in enumerate((tokens, cotangent)):
            out[kind] = ref[chip, :, rows, :]


def third_kernel(
    tokens, cotangent, attn, gain, w_qkv, w_out, normed_out, qkv_out, out_out, *scratch
):
    cot = cotangent[...]
    grad_normed, part_qkv = axis_grads(
        tokens[...], cot, gain[...], w_qkv[...], w_out[...], scratch, False
    )
    normed_out[...] = grad_normed
    qkv_out[...] = part_qkv
    out_out[...] = dot(attn[...], cot, 0, 0)


def pack(total, part_out, halves, own, low, high):
    for at in range(2 * TILES):
        half, tile = divmod(at, TILES)
        if at < 96:
            row, col = divmod(at, 6)
            halves[half, tile] = total[row * 16 : row * 16 + 16, col * LANES : (col + 1) * LANES]
        elif part_out is None:
            halves[half, tile] = jnp.zeros((16, LANES), F32)
        else:
            row, col = divmod(at - 96, 2)
            halves[half, tile] = part_out[row * 16 : row * 16 + 16, col * LANES : (col + 1) * LANES]
    mine = lax.axis_index("c")
    own[0:TILES] = halves[mine].astype(own.dtype)
    low[0:HALF] = halves[1 - mine, 0:HALF].astype(BF16)
    high[0:HALF] = halves[1 - mine, HALF:TILES].astype(BF16)


def second_kernel(*refs):
    pieces, (gain, w_qkv, w_out), parts = refs[:4], refs[4:7], refs[7:9]
    back, packed, scratch, halves = refs[9:13], refs[13:16], refs[16:-1], refs[-1]
    near, mate, far, passed = pieces
    pieces = (near, mate, far.at[0], passed.at[1])
    tokens = jnp.concatenate([piece[0].reshape(-1, WIDTH) for piece in pieces], axis=0)
    cot = jnp.concatenate([piece[1].reshape(-1, WIDTH) for piece in pieces], axis=0)
    grad_normed, part_qkv = axis_grads(
        tokens, cot, gain[...], w_qkv[...], w_out[...], scratch, True
    )
    returned = grad_normed.astype(BF16)
    rows = TOKENS // 4
    for mask, out in enumerate(back):
        out[...] = returned[mask * rows : (mask + 1) * rows].reshape(out.shape)
    third_qkv, part_out = parts
    pack(third_qkv[...] + part_qkv, part_out, halves, *packed)


def first_kernel(pieces, early_own, early_low, early_high, gain, w_qkv, w_out, *refs):
    (stay, leave), packed, scratch, rest = refs[:2], refs[2:5], refs[5:-6], refs[-6:]
    returned, halves, held_own, held_low, held_high, sem = rest
    held = (held_own, held_low, held_high)
    copies = [
        pltpu.make_async_copy(source, target, sem.at[at])
        for at, (source, target) in enumerate(zip((early_own, early_low, early_high), held))
    ]
    for copy in copies:
        copy.start()
    tokens = pieces[:, 0].reshape(TOKENS, WIDTH)
    cot = pieces[:, 1].reshape(TOKENS, WIDTH)
    grad_normed, part_qkv = axis_grads(
        tokens, cot, gain[...], w_qkv[...], w_out[...], scratch, True
    )
    returned[...] = grad_normed.astype(BF16).reshape(returned.shape)
    here = along_first()
    for at, mask in enumerate(SPANS[3]):
        stay[at] = returned[here ^ mask]
        leave[at] = returned[here ^ mask ^ BITS[0]]
    pack(part_qkv, None, halves, *packed)
    for copy in copies:
        copy.wait()
    own = packed[0]
    own[0:HALF] += held_own[0:HALF].astype(F32) + held_low[...].astype(F32)
    own[HALF:TILES] += held_own[HALF:TILES].astype(F32) + held_high[...].astype(F32)


def stage_kernel(*refs):
    groups, out = refs[:-1], refs[-1]
    left = 16 >> (len(groups) - 1)
    at = 0
    for order, ref in enumerate(groups):
        span = 8 >> max(order - 1, 0)
        for base in range(0, 8, span):
            for block in range(left // 2, left):
                out[at] = ref[base + block]
                at += 1


def pair_kernel(own, low, high, pieces):
    for peer in range(16):
        half, at = divmod(peer * 4, HALF)
        received = (low, high)[half][at : at + 4].astype(F32)
        pieces[peer] = (own[peer * 4 : peer * 4 + 4] + received).astype(BF16)


def plane_kernel(received, pieces):
    total = jnp.sum(received[...].astype(F32), axis=0).astype(BF16)
    for peer in range(8):
        pieces[peer] = total


def line_kernel(scale, received, pieces):
    total = (jnp.sum(received[...].astype(F32), axis=0) * scale).astype(BF16)
    for peer in range(16):
        pieces[peer] = total


def assemble_kernel(mine, theirs, gain, w_qkv, w_qkv_out, w_out_out, gain_out, halves):
    at_core = lax.axis_index("c")
    halves[at_core] = mine[...]
    halves[1 - at_core] = theirs[...]
    for at in range(2 * TILES):
        half, tile = divmod(at, TILES)
        rows = halves[half, tile].astype(F32)
        if at < 96:
            row, col = divmod(at, 6)
            w_qkv_out[row * 16 : row * 16 + 16, col * LANES : (col + 1) * LANES] = rows
        else:
            row, col = divmod(at - 96, 2)
            w_out_out[row * 16 : row * 16 + 16, col * LANES : (col + 1) * LANES] = rows
    products = jnp.zeros((WIDTH, LANES), F32)
    for col in range(6):
        cols = slice(col * LANES, (col + 1) * LANES)
        products = products + w_qkv_out[:, cols] * w_qkv[:, cols].astype(F32)
    ones = jnp.ones((8, LANES), BF16)
    high = products.astype(BF16)
    low = (products - high.astype(F32)).astype(BF16)
    total = dot(ones, high, 1, 1) + dot(ones, low, 1, 1)
    gain_out[...] = total[0:1] / gain[...]


def tokens_kernel(tokens, gain, third, *rest):
    groups, seconds = rest[:5], rest[5:9]
    out, from_first, from_second = rest[9:]
    here = along_first()
    from_first[here] = groups[0][0]
    for stage in range(4):
        span = 8 >> stage
        for at, mask in enumerate(sources_before(stage)):
            from_first[here ^ (mask ^ BITS[stage])] = groups[stage + 1][at * span]
    for mask, ref in enumerate(seconds):
        from_second[along_second() ^ mask] = ref[...]
    for x in range(2):
        for y in range(8):
            tokens_f = tokens[x, y].astype(F32)
            first = jnp.concatenate([from_first[y * 2, x], from_first[y * 2 + 1, x]], axis=0)
            second = jnp.concatenate([from_second[x * 2, y], from_second[x * 2 + 1, y]], axis=0)
            grad_normed = third[x, y] + first.astype(F32) + second.astype(F32)
            square = jnp.mean(tokens_f * tokens_f, axis=-1, keepdims=True) + EPSILON
            inverse = lax.rsqrt(square)
            gained = gain[...] * grad_normed
            inner = jnp.sum(gained * tokens_f, axis=-1, keepdims=True)
            result = gained * inverse - tokens_f * (inner * inverse / (WIDTH * square))
            out[x, y] = result.astype(BF16)


def shape(dims, dtype):
    return jax.ShapeDtypeStruct(dims, dtype)


def kernel_call(body, outs, operands, us, scratch=(), space=VMEM, spaces=None, out_spaces=None):
    return pl.pallas_call(
        body,
        out_shape=outs,
        in_specs=spaces or [space] * len(operands),
        out_specs=out_spaces or jax.tree.map(lambda _: space, outs),
        scratch_shapes=list(scratch),
        compiler_params=params(62 if space is HBM else 48),
        cost_estimate=cost(us),
    )(*operands)


def swap(array, axis, mask, size):
    return lax.ppermute(array, axis, [(i, i ^ mask) for i in range(size)])


def exchange(pieces, axes):
    return lax.all_to_all(pieces, axes, split_axis=0, concat_axis=0, tiled=True)


def on_device(count, tokens, attn, cotangent, gain, w_qkv, w_out):
    gain_row = gain.reshape(1, WIDTH)
    local = tokens[0]
    upstream = cotangent[0]
    flat = (TOKENS, WIDTH)
    tile = (16, LANES)
    quarter = (2, 8, ROWS, WIDTH)
    to_first, far = kernel_call(
        pieces_kernel,
        (shape((8, 2, 2, 2, ROWS, WIDTH), BF16), shape((2, *quarter), BF16)),
        (local, upstream),
        2,
        [pltpu.VMEM((2, *local.shape), BF16), pltpu.SemaphoreType.DMA((2,))],
        space=HBM,
        out_spaces=(VMEM, VMEM),
    )
    at_first = exchange(to_first.reshape(16, 2, 2, ROWS, WIDTH), FIRST)
    far = swap(far, "xl", 1, 2)
    near, mate = kernel_call(
        chip_pieces_kernel, (shape(quarter, BF16),) * 2, (local, upstream), 1
    )
    at_second = [near, swap(mate, "c", 1, 2), far, swap(far, "c", 1, 2)]
    third, third_qkv, part_out = kernel_call(
        third_kernel,
        (shape(flat, F32), shape((WIDTH, TRIPLE), F32), shape((WIDTH, WIDTH), F32)),
        (local.reshape(flat), upstream.reshape(flat), attn.reshape(flat), gain_row, w_qkv, w_out),
        5,
        SCRATCH,
    )
    packed = (
        shape((TILES, *tile), BF16),
        shape((HALF, *tile), BF16),
        shape((HALF, *tile), BF16),
    )
    halves = pltpu.VMEM((2, TILES, *tile), F32)
    *back, own, low, high = kernel_call(
        second_kernel,
        (shape((8, ROWS, WIDTH), BF16),) * 4 + packed,
        (*at_second, gain_row, w_qkv, w_out, third_qkv, part_out),
        5,
        SCRATCH + [halves],
    )
    from_second = [back[0]] + [swap(back[m], SECOND, m, 4) for m in (1, 2, 3)]
    early = [own, swap(low, "c", 1, 2), swap(high, "c", 1, 2)]
    block = (2, ROWS, WIDTH)
    stay, leave, own, low, high = kernel_call(
        first_kernel,
        (
            shape((8, *block), BF16),
            shape((8, *block), BF16),
            shape((TILES, *tile), F32),
            *packed[1:],
        ),
        (at_first, *early, gain_row, w_qkv, w_out),
        5,
        SCRATCH
        + [
            pltpu.VMEM((16, *block), BF16),
            halves,
            *[pltpu.VMEM(part.shape, part.dtype) for part in packed],
            pltpu.SemaphoreType.DMA((3,)),
        ],
        spaces=[VMEM] + [HBM] * 3 + [VMEM] * 3,
    )
    low, high, from_second = lax.optimization_barrier((low, high, from_second))
    late = [own, swap(low, "c", 1, 2), swap(high, "c", 1, 2)]
    groups = [stay, swap(leave, *SWAPS[0])]
    for stage in (1, 2, 3):
        leave = kernel_call(stage_kernel, shape((8, *block), BF16), groups, 20)
        groups.append(swap(leave, *SWAPS[stage]))
    pieces = kernel_call(pair_kernel, shape((16, 4, *tile), BF16), late, 1)
    summed = exchange(pieces, PLANE)
    pieces = kernel_call(plane_kernel, shape((8, 4, *tile), BF16), (summed,), 1)
    summed = exchange(pieces, "z")
    pieces = kernel_call(
        functools.partial(line_kernel, 1.0 / math.sqrt(count)),
        shape((16, 4, *tile), BF16),
        (summed,),
        1,
    )
    mine = exchange(pieces, PLANE)
    mine = mine.reshape(TILES, *tile)
    theirs = swap(mine, "c", 1, 2)
    d_w_qkv, d_w_out, d_gain = kernel_call(
        assemble_kernel,
        (
            shape((WIDTH, TRIPLE), F32),
            shape((WIDTH, WIDTH), F32),
            shape((1, WIDTH), F32),
        ),
        (mine, theirs, gain_row, w_qkv),
        1,
        [pltpu.VMEM((2, TILES, *tile), BF16)],
    )
    d_tokens = kernel_call(
        tokens_kernel,
        shape(local.shape, BF16),
        (local, gain_row, third.reshape(local.shape), *groups, *from_second),
        2,
        [pltpu.VMEM((16, *block), BF16), pltpu.VMEM((4, 8, ROWS, WIDTH), BF16)],
    )
    return (d_tokens[None], d_w_qkv, d_w_out, d_gain.reshape(WIDTH))


def solution(mesh):
    fine = Mesh(mesh.devices.reshape(4, 8, 2, 2, 2), ("y", "z", "xh", "xl", "c"))
    split = P("y", ("z", "xh"), SECOND, None, None)
    count = 4 * 32 * 32 * 32
    return jax.shard_map(
        functools.partial(on_device, count),
        mesh=fine,
        in_specs=(split, split, split, P(), P(), P()),
        out_specs=(split, P(), P(), P()),
        check_vma=False,
    )
```

```python
import functools
import math

import jax
import jax.numpy as jnp
from jax import lax
from jax.experimental import pallas as pl
from jax.experimental.pallas import tpu as pltpu
from jax.sharding import Mesh
from jax.sharding import PartitionSpec as P

HEADS = 8
HEAD = 32
WIDTH = 256
TRIPLE = 3 * WIDTH
EPSILON = 1e-06
FACTOR = 1.0 / math.sqrt(HEAD)
TOKENS = 512
LENGTH = 32
GROUP = 8
PENCILS = 16
ROWS = 16
LANES = 128
TILES = 64
BF16 = jnp.bfloat16
F32 = jnp.float32
VMEM = pl.BlockSpec(memory_space=pltpu.VMEM)
HBM = pl.BlockSpec(memory_space=pltpu.HBM)
PLANE = ("xh", "xl", "y")
FIRST = ("xh", "z")
SECOND = ("xl", "c")


def params(mib):
    return pltpu.CompilerParams(vmem_limit_bytes=mib * 2**20)


def cost(us):
    return pl.CostEstimate(
        flops=int(us * 8e8), bytes_accessed=int(us * 2e6), transcendentals=0
    )


def dot(left, right, left_dim, right_dim):
    return lax.dot_general(
        left, right, (((left_dim,), (right_dim,)), ((), ())), preferred_element_type=F32
    )


def attention(qkv, grad_attn, block, lane, count):
    spans = [slice(i * LENGTH, (i + 1) * LENGTH) for i in range(count)]
    k = [qkv[span, WIDTH : 2 * WIDTH] for span in spans]
    v = [qkv[span, 2 * WIDTH :] for span in spans]
    q_block = [jnp.concatenate([qkv[span, :WIDTH]] * HEADS, axis=0) * block for span in spans]
    g_block = [jnp.concatenate([grad_attn[span]] * HEADS, axis=0) * block for span in spans]
    scores = [dot(k[i], q_block[i], 1, 1) for i in range(count)]
    grad_probs = [dot(v[i], g_block[i], 1, 1) for i in range(count)]
    probs_low = []
    scores_low = []
    for i in range(count):
        top = jnp.max(scores[i], axis=0, keepdims=True)
        powers = jnp.exp((scores[i] - top) * FACTOR)
        probs = powers * (1.0 / jnp.sum(powers, axis=0, keepdims=True))
        inner = jnp.sum(probs * grad_probs[i], axis=0, keepdims=True)
        scores_low.append((probs * (grad_probs[i] - inner)).astype(BF16))
        probs_low.append(probs.astype(BF16))
    grad_v = [dot(probs_low[i], g_block[i], 1, 0) for i in range(count)]
    grad_k = [dot(scores_low[i], q_block[i], 1, 0) * FACTOR for i in range(count)]
    grad_q = [[] for _ in range(count)]
    for half in range(2):
        cols = slice(half * LANES, (half + 1) * LANES)
        for base in range(0, count, 4):
            turned = jnp.concatenate([low[:, cols] for low in scores_low[base : base + 4]], axis=0)
            turned = turned.T
            for i in range(4):
                every = dot(turned[:, spans[i]], k[base + i][:, cols], 1, 0)
                picked = every[96:128]
                for head in (2, 1, 0):
                    picked = jnp.where(
                        lane < HEAD * (head + 1), every[head * HEAD : (head + 1) * HEAD], picked
                    )
                grad_q[base + i].append(picked * FACTOR)
    joined = [
        jnp.concatenate([*grad_q[i], grad_k[i], grad_v[i]], axis=1).astype(BF16)
        for i in range(count)
    ]
    return jnp.concatenate(joined, axis=0)


def axis_grads(tokens, cotangent, gain, w_qkv, w_out, scratch, strided):
    tokens_cols, cot_cols, grad_cols, joined_rows, normed_rows = scratch
    if strided:
        tokens_f, cot_f = tokens.astype(F32), cotangent.astype(F32)
        for col in range(2):
            tokens_cols[col] = tokens_f[:, col * LANES : (col + 1) * LANES]
            cot_cols[col] = cot_f[:, col * LANES : (col + 1) * LANES]
    dims = (WIDTH, WIDTH)
    block = (
        lax.broadcasted_iota(jnp.int32, dims, 0) // HEAD
        == lax.broadcasted_iota(jnp.int32, dims, 1) // HEAD
    )
    block = block.astype(F32).astype(BF16)
    lane = lax.broadcasted_iota(jnp.int32, (LENGTH, LANES), 1)
    for base in range(0, PENCILS, GROUP):
        group = slice(base * LENGTH, (base + GROUP) * LENGTH)
        if strided:
            rows_of = [pl.ds(base + i, LENGTH, stride=PENCILS) for i in range(GROUP)]

            def gathered(ref):
                cols = [
                    jnp.concatenate([ref[col, rows, :] for rows in rows_of], axis=0)
                    for col in range(2)
                ]
                return jnp.concatenate(cols, axis=1)

            tokens_f = gathered(tokens_cols)
            cot = gathered(cot_cols).astype(BF16)
        else:
            rows_of = [pl.ds((base + i) * LENGTH, LENGTH) for i in range(GROUP)]
            tokens_f = tokens[group].astype(F32)
            cot = cotangent[group]
        square = jnp.mean(tokens_f * tokens_f, axis=-1, keepdims=True) + EPSILON
        normed = (tokens_f * lax.rsqrt(square) * gain).astype(BF16)
        normed_rows[group] = normed
        qkv = dot(normed, w_qkv, 1, 0).astype(BF16)
        grad_attn = dot(cot, w_out, 1, 1).astype(BF16)
        joined = attention(qkv, grad_attn, block, lane, GROUP)
        joined_rows[group] = joined
        grad_normed = dot(joined, w_qkv, 1, 1)
        for i, rows in enumerate(rows_of):
            for col in range(2):
                grad_cols[col, rows, :] = grad_normed[spans_of(i), col * LANES : (col + 1) * LANES]
    part_qkv = dot(normed_rows[...], joined_rows[...], 0, 0)
    return jnp.concatenate([grad_cols[0], grad_cols[1]], axis=1), part_qkv


def spans_of(i):
    return slice(i * LENGTH, (i + 1) * LENGTH)


BITS = (1, 4, 8, 2)
SWAPS = (("z", 1, 8), ("z", 4, 8), ("xh", 1, 2), ("z", 2, 8))


def sources_before(stage):
    masks = [0]
    for bit in BITS[:stage]:
        masks += [mask ^ bit for mask in masks]
    return masks


def span_masks(count):
    masks = [0]
    for bit in reversed(BITS[4 - count :]):
        masks += [mask ^ bit for mask in masks]
    return masks


SPANS = [span_masks(count) for count in range(4)]

SCRATCH = [pltpu.VMEM((2, TOKENS, LANES), F32)] * 3 + [
    pltpu.VMEM((TOKENS, TRIPLE), BF16),
    pltpu.VMEM((TOKENS, WIDTH), BF16),
]


def along_second():
    return lax.axis_index("xl") * 2 + lax.axis_index("c")


def along_first():
    return lax.axis_index("xh") * 8 + lax.axis_index("z")


def pieces_kernel(tokens, cotangent, to_first, far, held, sem):
    core, chip = lax.axis_index("c"), lax.axis_index("xl")
    loads = [
        pltpu.make_async_copy(ref, held.at[kind], sem.at[kind])
        for kind, ref in enumerate((tokens, cotangent))
    ]
    for load in loads:
        load.start()
    for kind, load in enumerate(loads):
        load.wait()
        for x in range(2):
            for z in range(2):
                to_first[:, z, kind, x] = held[kind, x, :, z * ROWS : (z + 1) * ROWS, :]
        for other in range(2):
            rows = pl.ds(pl.multiple_of((core ^ other) * ROWS, ROWS), ROWS)
            far[other, kind] = held[kind, 1 - chip, :, rows, :]


def chip_pieces_kernel(tokens, cotangent, near, mate):
    core, chip = lax.axis_index("c"), lax.axis_index("xl")
    for other, out in enumerate((near, mate)):
        rows = pl.ds(pl.multiple_of((core ^ other) * ROWS, ROWS), ROWS)
        for kind, ref in enumerate((tokens, cotangent)):
            out[kind] = ref[chip, :, rows, :]


def third_kernel(
    tokens, cotangent, attn, gain, w_qkv, w_out, normed_out, qkv_out, out_out, *scratch
):
    cot = cotangent[...]
    grad_normed, part_qkv = axis_grads(
        tokens[...], cot, gain[...], w_qkv[...], w_out[...], scratch, False
    )
    normed_out[...] = grad_normed
    qkv_out[...] = part_qkv
    out_out[...] = dot(attn[...], cot, 0, 0)


def pack(total, part_out, halves, own, other):
    for at in range(2 * TILES):
        half, tile = divmod(at, TILES)
        if at < 96:
            row, col = divmod(at, 6)
            halves[half, tile] = total[row * 16 : row * 16 + 16, col * LANES : (col + 1) * LANES]
        elif part_out is None:
            halves[half, tile] = jnp.zeros((16, LANES), F32)
        else:
            row, col = divmod(at - 96, 2)
            halves[half, tile] = part_out[row * 16 : row * 16 + 16, col * LANES : (col + 1) * LANES]
    mine = lax.axis_index("c")
    own[0:TILES] = halves[mine].astype(own.dtype)
    other[...] = halves[1 - mine].astype(BF16)


def second_kernel(*refs):
    pieces, (gain, w_qkv, w_out), parts = refs[:4], refs[4:7], refs[7:9]
    back, packed, scratch, halves = refs[9:13], refs[13:15], refs[15:-1], refs[-1]
    near, mate, far, passed = pieces
    pieces = (near, mate, far.at[0], passed.at[1])
    tokens = jnp.concatenate([piece[0].reshape(-1, WIDTH) for piece in pieces], axis=0)
    cot = jnp.concatenate([piece[1].reshape(-1, WIDTH) for piece in pieces], axis=0)
    grad_normed, part_qkv = axis_grads(
        tokens, cot, gain[...], w_qkv[...], w_out[...], scratch, True
    )
    returned = grad_normed.astype(BF16)
    rows = TOKENS // 4
    for mask, out in enumerate(back):
        out[...] = returned[mask * rows : (mask + 1) * rows].reshape(out.shape)
    third_qkv, part_out = parts
    pack(third_qkv[...] + part_qkv, part_out, halves, *packed)


def first_kernel(pieces, early_own, early_other, gain, w_qkv, w_out, *refs):
    (stay, leave), packed, scratch, rest = refs[:2], refs[2:4], refs[4:-5], refs[-5:]
    returned, halves, held_own, held_other, sem = rest
    held = (held_own, held_other)
    copies = [
        pltpu.make_async_copy(source, target, sem.at[at])
        for at, (source, target) in enumerate(zip((early_own, early_other), held))
    ]
    for copy in copies:
        copy.start()
    tokens = pieces[:, 0].reshape(TOKENS, WIDTH)
    cot = pieces[:, 1].reshape(TOKENS, WIDTH)
    grad_normed, part_qkv = axis_grads(
        tokens, cot, gain[...], w_qkv[...], w_out[...], scratch, True
    )
    returned[...] = grad_normed.astype(BF16).reshape(returned.shape)
    here = along_first()
    for at, mask in enumerate(SPANS[3]):
        stay[at] = returned[here ^ mask]
        leave[at] = returned[here ^ mask ^ BITS[0]]
    pack(part_qkv, None, halves, *packed)
    for copy in copies:
        copy.wait()
    own = packed[0]
    own[...] += held_own[...].astype(F32) + held_other[...].astype(F32)


def stage_kernel(*refs):
    groups, out = refs[:-1], refs[-1]
    left = 16 >> (len(groups) - 1)
    at = 0
    for order, ref in enumerate(groups):
        span = 8 >> max(order - 1, 0)
        for base in range(0, 8, span):
            for block in range(left // 2, left):
                out[at] = ref[base + block]
                at += 1


def pair_kernel(own, received, pieces):
    for peer in range(16):
        tiles = slice(peer * 4, peer * 4 + 4)
        pieces[peer] = (own[tiles] + received[tiles].astype(F32)).astype(BF16)


def plane_kernel(received, pieces):
    total = jnp.sum(received[...].astype(F32), axis=0).astype(BF16)
    for peer in range(8):
        pieces[peer] = total


def line_kernel(scale, received, pieces):
    total = (jnp.sum(received[...].astype(F32), axis=0) * scale).astype(BF16)
    for peer in range(16):
        pieces[peer] = total


def assemble_kernel(mine, theirs, gain, w_qkv, w_qkv_out, w_out_out, gain_out, halves):
    at_core = lax.axis_index("c")
    halves[at_core] = mine[...]
    halves[1 - at_core] = theirs[...]
    for at in range(2 * TILES):
        half, tile = divmod(at, TILES)
        rows = halves[half, tile].astype(F32)
        if at < 96:
            row, col = divmod(at, 6)
            w_qkv_out[row * 16 : row * 16 + 16, col * LANES : (col + 1) * LANES] = rows
        else:
            row, col = divmod(at - 96, 2)
            w_out_out[row * 16 : row * 16 + 16, col * LANES : (col + 1) * LANES] = rows
    products = jnp.zeros((WIDTH, LANES), F32)
    for col in range(6):
        cols = slice(col * LANES, (col + 1) * LANES)
        products = products + w_qkv_out[:, cols] * w_qkv[:, cols].astype(F32)
    ones = jnp.ones((8, LANES), BF16)
    high = products.astype(BF16)
    low = (products - high.astype(F32)).astype(BF16)
    total = dot(ones, high, 1, 1) + dot(ones, low, 1, 1)
    gain_out[...] = total[0:1] / gain[...]


def tokens_kernel(tokens, gain, third, *rest):
    groups, seconds = rest[:5], rest[5:9]
    out, from_first, from_second = rest[9:]
    here = along_first()
    from_first[here] = groups[0][0]
    for stage in range(4):
        span = 8 >> stage
        for at, mask in enumerate(sources_before(stage)):
            from_first[here ^ (mask ^ BITS[stage])] = groups[stage + 1][at * span]
    for mask, ref in enumerate(seconds):
        from_second[along_second() ^ mask] = ref[...]
    for x in range(2):
        for y in range(8):
            tokens_f = tokens[x, y].astype(F32)
            first = jnp.concatenate([from_first[y * 2, x], from_first[y * 2 + 1, x]], axis=0)
            second = jnp.concatenate([from_second[x * 2, y], from_second[x * 2 + 1, y]], axis=0)
            grad_normed = third[x, y] + first.astype(F32) + second.astype(F32)
            square = jnp.mean(tokens_f * tokens_f, axis=-1, keepdims=True) + EPSILON
            inverse = lax.rsqrt(square)
            gained = gain[...] * grad_normed
            inner = jnp.sum(gained * tokens_f, axis=-1, keepdims=True)
            result = gained * inverse - tokens_f * (inner * inverse / (WIDTH * square))
            out[x, y] = result.astype(BF16)


def shape(dims, dtype):
    return jax.ShapeDtypeStruct(dims, dtype)


def kernel_call(body, outs, operands, us, scratch=(), space=VMEM, spaces=None, out_spaces=None):
    return pl.pallas_call(
        body,
        out_shape=outs,
        in_specs=spaces or [space] * len(operands),
        out_specs=out_spaces or jax.tree.map(lambda _: space, outs),
        scratch_shapes=list(scratch),
        compiler_params=params(62 if space is HBM else 48),
        cost_estimate=cost(us),
    )(*operands)


def swap(array, axis, mask, size):
    return lax.ppermute(array, axis, [(i, i ^ mask) for i in range(size)])


def exchange(pieces, axes):
    return lax.all_to_all(pieces, axes, split_axis=0, concat_axis=0, tiled=True)


def on_device(count, tokens, attn, cotangent, gain, w_qkv, w_out):
    gain_row = gain.reshape(1, WIDTH)
    local = tokens[0]
    upstream = cotangent[0]
    flat = (TOKENS, WIDTH)
    tile = (16, LANES)
    quarter = (2, 8, ROWS, WIDTH)
    to_first, far = kernel_call(
        pieces_kernel,
        (shape((8, 2, 2, 2, ROWS, WIDTH), BF16), shape((2, *quarter), BF16)),
        (local, upstream),
        2,
        [pltpu.VMEM((2, *local.shape), BF16), pltpu.SemaphoreType.DMA((2,))],
        space=HBM,
        out_spaces=(VMEM, VMEM),
    )
    at_first = exchange(to_first.reshape(16, 2, 2, ROWS, WIDTH), FIRST)
    far = swap(far, "xl", 1, 2)
    near, mate = kernel_call(
        chip_pieces_kernel, (shape(quarter, BF16),) * 2, (local, upstream), 1
    )
    far, mate = lax.optimization_barrier((far, mate))
    at_second = [near, swap(mate, "c", 1, 2), far, swap(far, "c", 1, 2)]
    third, third_qkv, part_out = kernel_call(
        third_kernel,
        (shape(flat, F32), shape((WIDTH, TRIPLE), F32), shape((WIDTH, WIDTH), F32)),
        (local.reshape(flat), upstream.reshape(flat), attn.reshape(flat), gain_row, w_qkv, w_out),
        5,
        SCRATCH,
    )
    packed = (
        shape((TILES, *tile), BF16),
        shape((TILES, *tile), BF16),
    )
    halves = pltpu.VMEM((2, TILES, *tile), F32)
    *back, own, other = kernel_call(
        second_kernel,
        (shape((8, ROWS, WIDTH), BF16),) * 4 + packed,
        (*at_second, gain_row, w_qkv, w_out, third_qkv, part_out),
        5,
        SCRATCH + [halves],
    )
    from_second = [back[0]] + [swap(back[m], SECOND, m, 4) for m in (1, 2, 3)]
    early = [own, swap(other, "c", 1, 2)]
    block = (2, ROWS, WIDTH)
    stay, leave, own, other = kernel_call(
        first_kernel,
        (
            shape((8, *block), BF16),
            shape((8, *block), BF16),
            shape((TILES, *tile), F32),
            *packed[1:],
        ),
        (at_first, *early, gain_row, w_qkv, w_out),
        5,
        SCRATCH
        + [
            pltpu.VMEM((16, *block), BF16),
            halves,
            *[pltpu.VMEM(part.shape, part.dtype) for part in packed],
            pltpu.SemaphoreType.DMA((2,)),
        ],
        spaces=[VMEM] + [HBM] * 2 + [VMEM] * 3,
    )
    other, from_second = lax.optimization_barrier((other, from_second))
    late = [own, swap(other, "c", 1, 2)]
    groups = [stay, swap(leave, *SWAPS[0])]
    for stage in (1, 2, 3):
        leave = kernel_call(stage_kernel, shape((8, *block), BF16), groups, 20)
        groups.append(swap(leave, *SWAPS[stage]))
    pieces = kernel_call(pair_kernel, shape((16, 4, *tile), BF16), late, 1)
    summed = exchange(pieces, PLANE)
    pieces = kernel_call(plane_kernel, shape((8, 4, *tile), BF16), (summed,), 1)
    summed = exchange(pieces, "z")
    pieces = kernel_call(
        functools.partial(line_kernel, 1.0 / math.sqrt(count)),
        shape((16, 4, *tile), BF16),
        (summed,),
        1,
    )
    mine = exchange(pieces, PLANE)
    mine = mine.reshape(TILES, *tile)
    theirs = swap(mine, "c", 1, 2)
    d_w_qkv, d_w_out, d_gain = kernel_call(
        assemble_kernel,
        (
            shape((WIDTH, TRIPLE), F32),
            shape((WIDTH, WIDTH), F32),
            shape((1, WIDTH), F32),
        ),
        (mine, theirs, gain_row, w_qkv),
        1,
        [pltpu.VMEM((2, TILES, *tile), BF16)],
    )
    d_tokens = kernel_call(
        tokens_kernel,
        shape(local.shape, BF16),
        (local, gain_row, third.reshape(local.shape), *groups, *from_second),
        2,
        [pltpu.VMEM((16, *block), BF16), pltpu.VMEM((4, 8, ROWS, WIDTH), BF16)],
    )
    return (d_tokens[None], d_w_qkv, d_w_out, d_gain.reshape(WIDTH))


def solution(mesh):
    fine = Mesh(mesh.devices.reshape(4, 8, 2, 2, 2), ("y", "z", "xh", "xl", "c"))
    split = P("y", ("z", "xh"), SECOND, None, None)
    count = 4 * 32 * 32 * 32
    return jax.shard_map(
        functools.partial(on_device, count),
        mesh=fine,
        in_specs=(split, split, split, P(), P(), P()),
        out_specs=(split, P(), P(), P()),
        check_vma=False,
    )
```

```python
import functools
import math

import jax
import jax.numpy as jnp
from jax import lax
from jax.experimental import pallas as pl
from jax.experimental.pallas import tpu as pltpu
from jax.sharding import Mesh
from jax.sharding import PartitionSpec as P

HEADS = 8
HEAD = 32
WIDTH = 256
TRIPLE = 3 * WIDTH
EPSILON = 1e-06
FACTOR = 1.0 / math.sqrt(HEAD)
TOKENS = 512
LENGTH = 32
GROUP = 8
PENCILS = 16
ROWS = 16
LANES = 128
TILES = 64
BF16 = jnp.bfloat16
F32 = jnp.float32
VMEM = pl.BlockSpec(memory_space=pltpu.VMEM)
HBM = pl.BlockSpec(memory_space=pltpu.HBM)
PLANE = ("xl", "y", "xh")
FIRST = ("xh", "z")
SECOND = ("xl", "c")


def params(mib):
    return pltpu.CompilerParams(vmem_limit_bytes=mib * 2**20)


def cost(us):
    return pl.CostEstimate(
        flops=int(us * 8e8), bytes_accessed=int(us * 2e6), transcendentals=0
    )


def dot(left, right, left_dim, right_dim):
    return lax.dot_general(
        left, right, (((left_dim,), (right_dim,)), ((), ())), preferred_element_type=F32
    )


def attention(qkv, grad_attn, block, lane, count):
    spans = [slice(i * LENGTH, (i + 1) * LENGTH) for i in range(count)]
    k = [qkv[span, WIDTH : 2 * WIDTH] for span in spans]
    v = [qkv[span, 2 * WIDTH :] for span in spans]
    q_block = [jnp.concatenate([qkv[span, :WIDTH]] * HEADS, axis=0) * block for span in spans]
    g_block = [jnp.concatenate([grad_attn[span]] * HEADS, axis=0) * block for span in spans]
    scores = [dot(k[i], q_block[i], 1, 1) for i in range(count)]
    grad_probs = [dot(v[i], g_block[i], 1, 1) for i in range(count)]
    probs_low = []
    scores_low = []
    for i in range(count):
        top = jnp.max(scores[i], axis=0, keepdims=True)
        powers = jnp.exp((scores[i] - top) * FACTOR)
        probs = powers * (1.0 / jnp.sum(powers, axis=0, keepdims=True))
        inner = jnp.sum(probs * grad_probs[i], axis=0, keepdims=True)
        scores_low.append((probs * (grad_probs[i] - inner)).astype(BF16))
        probs_low.append(probs.astype(BF16))
    grad_v = [dot(probs_low[i], g_block[i], 1, 0) for i in range(count)]
    grad_k = [dot(scores_low[i], q_block[i], 1, 0) * FACTOR for i in range(count)]
    grad_q = [[] for _ in range(count)]
    for half in range(2):
        cols = slice(half * LANES, (half + 1) * LANES)
        for base in range(0, count, 4):
            turned = jnp.concatenate([low[:, cols] for low in scores_low[base : base + 4]], axis=0)
            turned = turned.T
            for i in range(4):
                every = dot(turned[:, spans[i]], k[base + i][:, cols], 1, 0)
                picked = every[96:128]
                for head in (2, 1, 0):
                    picked = jnp.where(
                        lane < HEAD * (head + 1), every[head * HEAD : (head + 1) * HEAD], picked
                    )
                grad_q[base + i].append(picked * FACTOR)
    joined = [
        jnp.concatenate([*grad_q[i], grad_k[i], grad_v[i]], axis=1).astype(BF16)
        for i in range(count)
    ]
    return jnp.concatenate(joined, axis=0)


def axis_grads(tokens, cotangent, gain, w_qkv, w_out, scratch, strided):
    tokens_cols, cot_cols, grad_cols, joined_rows, normed_rows = scratch
    if strided:
        tokens_f, cot_f = tokens.astype(F32), cotangent.astype(F32)
        for col in range(2):
            tokens_cols[col] = tokens_f[:, col * LANES : (col + 1) * LANES]
            cot_cols[col] = cot_f[:, col * LANES : (col + 1) * LANES]
    dims = (WIDTH, WIDTH)
    block = (
        lax.broadcasted_iota(jnp.int32, dims, 0) // HEAD
        == lax.broadcasted_iota(jnp.int32, dims, 1) // HEAD
    )
    block = block.astype(F32).astype(BF16)
    lane = lax.broadcasted_iota(jnp.int32, (LENGTH, LANES), 1)
    for base in range(0, PENCILS, GROUP):
        group = slice(base * LENGTH, (base + GROUP) * LENGTH)
        if strided:
            rows_of = [pl.ds(base + i, LENGTH, stride=PENCILS) for i in range(GROUP)]

            def gathered(ref):
                cols = [
                    jnp.concatenate([ref[col, rows, :] for rows in rows_of], axis=0)
                    for col in range(2)
                ]
                return jnp.concatenate(cols, axis=1)

            tokens_f = gathered(tokens_cols)
            cot = gathered(cot_cols).astype(BF16)
        else:
            rows_of = [pl.ds((base + i) * LENGTH, LENGTH) for i in range(GROUP)]
            tokens_f = tokens[group].astype(F32)
            cot = cotangent[group]
        square = jnp.mean(tokens_f * tokens_f, axis=-1, keepdims=True) + EPSILON
        normed = (tokens_f * lax.rsqrt(square) * gain).astype(BF16)
        normed_rows[group] = normed
        qkv = dot(normed, w_qkv, 1, 0).astype(BF16)
        grad_attn = dot(cot, w_out, 1, 1).astype(BF16)
        joined = attention(qkv, grad_attn, block, lane, GROUP)
        joined_rows[group] = joined
        grad_normed = dot(joined, w_qkv, 1, 1)
        for i, rows in enumerate(rows_of):
            for col in range(2):
                grad_cols[col, rows, :] = grad_normed[spans_of(i), col * LANES : (col + 1) * LANES]
    part_qkv = dot(normed_rows[...], joined_rows[...], 0, 0)
    return jnp.concatenate([grad_cols[0], grad_cols[1]], axis=1), part_qkv


def spans_of(i):
    return slice(i * LENGTH, (i + 1) * LENGTH)


BITS = (1, 4, 8, 2)
SWAPS = (("z", 1, 8), ("z", 4, 8), ("xh", 1, 2), ("z", 2, 8))


def sources_before(stage):
    masks = [0]
    for bit in BITS[:stage]:
        masks += [mask ^ bit for mask in masks]
    return masks


def span_masks(count):
    masks = [0]
    for bit in reversed(BITS[4 - count :]):
        masks += [mask ^ bit for mask in masks]
    return masks


SPANS = [span_masks(count) for count in range(4)]

SCRATCH = [pltpu.VMEM((2, TOKENS, LANES), F32)] * 3 + [
    pltpu.VMEM((TOKENS, TRIPLE), BF16),
    pltpu.VMEM((TOKENS, WIDTH), BF16),
]


def along_second():
    return lax.axis_index("xl") * 2 + lax.axis_index("c")


def along_first():
    return lax.axis_index("xh") * 8 + lax.axis_index("z")


def pieces_kernel(tokens, cotangent, to_first, far, held, sem):
    core, chip = lax.axis_index("c"), lax.axis_index("xl")
    loads = [
        pltpu.make_async_copy(ref, held.at[kind], sem.at[kind])
        for kind, ref in enumerate((tokens, cotangent))
    ]
    for load in loads:
        load.start()
    for kind, load in enumerate(loads):
        load.wait()
        for x in range(2):
            for z in range(2):
                to_first[:, z, kind, x] = held[kind, x, :, z * ROWS : (z + 1) * ROWS, :]
        for other in range(2):
            rows = pl.ds(pl.multiple_of((core ^ other) * ROWS, ROWS), ROWS)
            far[other, kind] = held[kind, 1 - chip, :, rows, :]


def chip_pieces_kernel(tokens, cotangent, near, mate):
    core, chip = lax.axis_index("c"), lax.axis_index("xl")
    for other, out in enumerate((near, mate)):
        rows = pl.ds(pl.multiple_of((core ^ other) * ROWS, ROWS), ROWS)
        for kind, ref in enumerate((tokens, cotangent)):
            out[kind] = ref[chip, :, rows, :]


def third_kernel(
    tokens, cotangent, attn, gain, w_qkv, w_out, normed_out, qkv_out, out_out, *scratch
):
    cot = cotangent[...]
    grad_normed, part_qkv = axis_grads(
        tokens[...], cot, gain[...], w_qkv[...], w_out[...], scratch, False
    )
    normed_out[...] = grad_normed
    qkv_out[...] = part_qkv
    out_out[...] = dot(attn[...], cot, 0, 0)


def pack(total, part_out, halves, own, other):
    for at in range(2 * TILES):
        half, tile = divmod(at, TILES)
        if at < 96:
            row, col = divmod(at, 6)
            halves[half, tile] = total[row * 16 : row * 16 + 16, col * LANES : (col + 1) * LANES]
        elif part_out is None:
            halves[half, tile] = jnp.zeros((16, LANES), F32)
        else:
            row, col = divmod(at - 96, 2)
            halves[half, tile] = part_out[row * 16 : row * 16 + 16, col * LANES : (col + 1) * LANES]
    mine = lax.axis_index("c")
    own[0:TILES] = halves[mine].astype(own.dtype)
    other[...] = halves[1 - mine].astype(BF16)


def second_kernel(*refs):
    pieces, (gain, w_qkv, w_out), parts = refs[:4], refs[4:7], refs[7:9]
    back, packed, scratch, halves = refs[9:13], refs[13:15], refs[15:-1], refs[-1]
    near, mate, far, passed = pieces
    pieces = (near, mate, far.at[0], passed.at[1])
    tokens = jnp.concatenate([piece[0].reshape(-1, WIDTH) for piece in pieces], axis=0)
    cot = jnp.concatenate([piece[1].reshape(-1, WIDTH) for piece in pieces], axis=0)
    grad_normed, part_qkv = axis_grads(
        tokens, cot, gain[...], w_qkv[...], w_out[...], scratch, True
    )
    returned = grad_normed.astype(BF16)
    rows = TOKENS // 4
    for mask, out in enumerate(back):
        out[...] = returned[mask * rows : (mask + 1) * rows].reshape(out.shape)
    third_qkv, part_out = parts
    pack(third_qkv[...] + part_qkv, part_out, halves, *packed)


def early_kernel(own, received, total):
    total[...] = (own[...].astype(F32) + received[...].astype(F32)).astype(BF16)


def first_kernel(pieces, early, gain, w_qkv, w_out, *refs):
    (stay, leave), packed, scratch, rest = refs[:2], refs[2:4], refs[4:-4], refs[-4:]
    returned, halves, held, sem = rest
    load = pltpu.make_async_copy(early, held, sem.at[0])
    load.start()
    tokens = pieces[:, 0].reshape(TOKENS, WIDTH)
    cot = pieces[:, 1].reshape(TOKENS, WIDTH)
    grad_normed, part_qkv = axis_grads(
        tokens, cot, gain[...], w_qkv[...], w_out[...], scratch, True
    )
    returned[...] = grad_normed.astype(BF16).reshape(returned.shape)
    here = along_first()
    for at, mask in enumerate(SPANS[3]):
        stay[at] = returned[here ^ mask]
        leave[at] = returned[here ^ mask ^ BITS[0]]
    pack(part_qkv, None, halves, *packed)
    load.wait()
    own = packed[0]
    own[...] += held[...].astype(F32)


def stage_kernel(*refs):
    groups, out = refs[:-1], refs[-1]
    left = 16 >> (len(groups) - 1)
    at = 0
    for order, ref in enumerate(groups):
        span = 8 >> max(order - 1, 0)
        for base in range(0, 8, span):
            for block in range(left // 2, left):
                out[at] = ref[base + block]
                at += 1


def pair_kernel(own, received, pieces):
    for peer in range(16):
        tiles = slice(peer * 4, peer * 4 + 4)
        pieces[peer] = (own[tiles] + received[tiles].astype(F32)).astype(BF16)


def plane_kernel(received, pieces):
    total = jnp.sum(received[...].astype(F32), axis=0).astype(BF16)
    for peer in range(8):
        pieces[peer] = total


def line_kernel(scale, received, pieces):
    total = (jnp.sum(received[...].astype(F32), axis=0) * scale).astype(BF16)
    for peer in range(16):
        pieces[peer] = total


def assemble_kernel(mine, theirs, gain, w_qkv, w_qkv_out, w_out_out, gain_out, halves):
    at_core = lax.axis_index("c")
    halves[at_core] = mine[...]
    halves[1 - at_core] = theirs[...]
    for at in range(2 * TILES):
        half, tile = divmod(at, TILES)
        rows = halves[half, tile].astype(F32)
        if at < 96:
            row, col = divmod(at, 6)
            w_qkv_out[row * 16 : row * 16 + 16, col * LANES : (col + 1) * LANES] = rows
        else:
            row, col = divmod(at - 96, 2)
            w_out_out[row * 16 : row * 16 + 16, col * LANES : (col + 1) * LANES] = rows
    products = jnp.zeros((WIDTH, LANES), F32)
    for col in range(6):
        cols = slice(col * LANES, (col + 1) * LANES)
        products = products + w_qkv_out[:, cols] * w_qkv[:, cols].astype(F32)
    ones = jnp.ones((8, LANES), BF16)
    high = products.astype(BF16)
    low = (products - high.astype(F32)).astype(BF16)
    total = dot(ones, high, 1, 1) + dot(ones, low, 1, 1)
    gain_out[...] = total[0:1] / gain[...]


def tokens_kernel(tokens, gain, third, *rest):
    groups, seconds = rest[:5], rest[5:9]
    out, from_first, from_second = rest[9:]
    here = along_first()
    from_first[here] = groups[0][0]
    for stage in range(4):
        span = 8 >> stage
        for at, mask in enumerate(sources_before(stage)):
            from_first[here ^ (mask ^ BITS[stage])] = groups[stage + 1][at * span]
    for mask, ref in enumerate(seconds):
        from_second[along_second() ^ mask] = ref[...]
    for x in range(2):
        for y in range(8):
            tokens_f = tokens[x, y].astype(F32)
            first = jnp.concatenate([from_first[y * 2, x], from_first[y * 2 + 1, x]], axis=0)
            second = jnp.concatenate([from_second[x * 2, y], from_second[x * 2 + 1, y]], axis=0)
            grad_normed = third[x, y] + first.astype(F32) + second.astype(F32)
            square = jnp.mean(tokens_f * tokens_f, axis=-1, keepdims=True) + EPSILON
            inverse = lax.rsqrt(square)
            gained = gain[...] * grad_normed
            inner = jnp.sum(gained * tokens_f, axis=-1, keepdims=True)
            result = gained * inverse - tokens_f * (inner * inverse / (WIDTH * square))
            out[x, y] = result.astype(BF16)


def shape(dims, dtype):
    return jax.ShapeDtypeStruct(dims, dtype)


def kernel_call(body, outs, operands, us, scratch=(), space=VMEM, spaces=None, out_spaces=None):
    return pl.pallas_call(
        body,
        out_shape=outs,
        in_specs=spaces or [space] * len(operands),
        out_specs=out_spaces or jax.tree.map(lambda _: space, outs),
        scratch_shapes=list(scratch),
        compiler_params=params(62 if space is HBM else 48),
        cost_estimate=cost(us),
    )(*operands)


def swap(array, axis, mask, size):
    return lax.ppermute(array, axis, [(i, i ^ mask) for i in range(size)])


def exchange(pieces, axes):
    return lax.all_to_all(pieces, axes, split_axis=0, concat_axis=0, tiled=True)


def on_device(count, tokens, attn, cotangent, gain, w_qkv, w_out):
    gain_row = gain.reshape(1, WIDTH)
    local = tokens[0]
    upstream = cotangent[0]
    flat = (TOKENS, WIDTH)
    tile = (16, LANES)
    quarter = (2, 8, ROWS, WIDTH)
    to_first, far = kernel_call(
        pieces_kernel,
        (shape((8, 2, 2, 2, ROWS, WIDTH), BF16), shape((2, *quarter), BF16)),
        (local, upstream),
        2,
        [pltpu.VMEM((2, *local.shape), BF16), pltpu.SemaphoreType.DMA((2,))],
        space=HBM,
        out_spaces=(VMEM, VMEM),
    )
    at_first = exchange(to_first.reshape(16, 2, 2, ROWS, WIDTH), FIRST)
    far = swap(far, "xl", 1, 2)
    near, mate = kernel_call(
        chip_pieces_kernel, (shape(quarter, BF16),) * 2, (local, upstream), 1
    )
    far, mate = lax.optimization_barrier((far, mate))
    at_second = [near, swap(mate, "c", 1, 2), far, swap(far, "c", 1, 2)]
    third, third_qkv, part_out = kernel_call(
        third_kernel,
        (shape(flat, F32), shape((WIDTH, TRIPLE), F32), shape((WIDTH, WIDTH), F32)),
        (local.reshape(flat), upstream.reshape(flat), attn.reshape(flat), gain_row, w_qkv, w_out),
        5,
        SCRATCH,
    )
    packed = (
        shape((TILES, *tile), BF16),
        shape((TILES, *tile), BF16),
    )
    halves = pltpu.VMEM((2, TILES, *tile), F32)
    *back, own, other = kernel_call(
        second_kernel,
        (shape((8, ROWS, WIDTH), BF16),) * 4 + packed,
        (*at_second, gain_row, w_qkv, w_out, third_qkv, part_out),
        5,
        SCRATCH + [halves],
    )
    from_second = [back[0]] + [swap(back[m], SECOND, m, 4) for m in (1, 2, 3)]
    early = kernel_call(
        early_kernel, shape((TILES, *tile), BF16), (own, swap(other, "c", 1, 2)), 1
    )
    block = (2, ROWS, WIDTH)
    stay, leave, own, other = kernel_call(
        first_kernel,
        (
            shape((8, *block), BF16),
            shape((8, *block), BF16),
            shape((TILES, *tile), F32),
            *packed[1:],
        ),
        (at_first, early, gain_row, w_qkv, w_out),
        5,
        SCRATCH
        + [
            pltpu.VMEM((16, *block), BF16),
            halves,
            pltpu.VMEM((TILES, *tile), BF16),
            pltpu.SemaphoreType.DMA((1,)),
        ],
        spaces=[VMEM, HBM] + [VMEM] * 3,
    )
    other, from_second = lax.optimization_barrier((other, from_second))
    late = [own, swap(other, "c", 1, 2)]
    groups = [stay, swap(leave, *SWAPS[0])]
    for stage in (1, 2, 3):
        leave = kernel_call(stage_kernel, shape((8, *block), BF16), groups, 20)
        groups.append(swap(leave, *SWAPS[stage]))
    pieces = kernel_call(pair_kernel, shape((16, 4, *tile), BF16), late, 1)
    summed = exchange(pieces, PLANE)
    pieces = kernel_call(plane_kernel, shape((8, 4, *tile), BF16), (summed,), 1)
    summed = exchange(pieces, "z")
    pieces = kernel_call(
        functools.partial(line_kernel, 1.0 / math.sqrt(count)),
        shape((16, 4, *tile), BF16),
        (summed,),
        1,
    )
    mine = exchange(pieces, PLANE)
    mine = mine.reshape(TILES, *tile)
    theirs = swap(mine, "c", 1, 2)
    d_w_qkv, d_w_out, d_gain = kernel_call(
        assemble_kernel,
        (
            shape((WIDTH, TRIPLE), F32),
            shape((WIDTH, WIDTH), F32),
            shape((1, WIDTH), F32),
        ),
        (mine, theirs, gain_row, w_qkv),
        1,
        [pltpu.VMEM((2, TILES, *tile), BF16)],
    )
    d_tokens = kernel_call(
        tokens_kernel,
        shape(local.shape, BF16),
        (local, gain_row, third.reshape(local.shape), *groups, *from_second),
        2,
        [pltpu.VMEM((16, *block), BF16), pltpu.VMEM((4, 8, ROWS, WIDTH), BF16)],
    )
    return (d_tokens[None], d_w_qkv, d_w_out, d_gain.reshape(WIDTH))


def solution(mesh):
    fine = Mesh(mesh.devices.reshape(4, 8, 2, 2, 2), ("y", "z", "xh", "xl", "c"))
    split = P("y", ("z", "xh"), SECOND, None, None)
    count = 4 * 32 * 32 * 32
    return jax.shard_map(
        functools.partial(on_device, count),
        mesh=fine,
        in_specs=(split, split, split, P(), P(), P()),
        out_specs=(split, P(), P(), P()),
        check_vma=False,
    )
```

```python
import functools
import math

import jax
import jax.numpy as jnp
from jax import lax
from jax.experimental import pallas as pl
from jax.experimental.pallas import tpu as pltpu
from jax.sharding import Mesh
from jax.sharding import PartitionSpec as P

HEADS = 8
HEAD = 32
WIDTH = 256
TRIPLE = 3 * WIDTH
EPSILON = 1e-06
FACTOR = 1.0 / math.sqrt(HEAD)
TOKENS = 512
LENGTH = 32
GROUP = 8
PENCILS = 16
ROWS = 16
LANES = 128
QKV_TILES = 48
TILES = 64
BF16 = jnp.bfloat16
F32 = jnp.float32
VMEM = pl.BlockSpec(memory_space=pltpu.VMEM)
HBM = pl.BlockSpec(memory_space=pltpu.HBM)
PLANE = ("xl", "y", "xh")
FIRST = ("xh", "z")
SECOND = ("xl", "c")


def params(mib):
    return pltpu.CompilerParams(vmem_limit_bytes=mib * 2**20)


def cost(us):
    return pl.CostEstimate(
        flops=int(us * 8e8), bytes_accessed=int(us * 2e6), transcendentals=0
    )


def dot(left, right, left_dim, right_dim):
    return lax.dot_general(
        left, right, (((left_dim,), (right_dim,)), ((), ())), preferred_element_type=F32
    )


def attention(qkv, grad_attn, block, lane, count):
    spans = [slice(i * LENGTH, (i + 1) * LENGTH) for i in range(count)]
    k = [qkv[span, WIDTH : 2 * WIDTH] for span in spans]
    v = [qkv[span, 2 * WIDTH :] for span in spans]
    q_block = [jnp.concatenate([qkv[span, :WIDTH]] * HEADS, axis=0) * block for span in spans]
    g_block = [jnp.concatenate([grad_attn[span]] * HEADS, axis=0) * block for span in spans]
    scores = [dot(k[i], q_block[i], 1, 1) for i in range(count)]
    grad_probs = [dot(v[i], g_block[i], 1, 1) for i in range(count)]
    probs_low = []
    scores_low = []
    for i in range(count):
        top = jnp.max(scores[i], axis=0, keepdims=True)
        powers = jnp.exp((scores[i] - top) * FACTOR)
        probs = powers * (1.0 / jnp.sum(powers, axis=0, keepdims=True))
        inner = jnp.sum(probs * grad_probs[i], axis=0, keepdims=True)
        scores_low.append((probs * (grad_probs[i] - inner)).astype(BF16))
        probs_low.append(probs.astype(BF16))
    grad_v = [dot(probs_low[i], g_block[i], 1, 0) for i in range(count)]
    grad_k = [dot(scores_low[i], q_block[i], 1, 0) * FACTOR for i in range(count)]
    grad_q = [[] for _ in range(count)]
    for half in range(2):
        cols = slice(half * LANES, (half + 1) * LANES)
        for base in range(0, count, 4):
            turned = jnp.concatenate([low[:, cols] for low in scores_low[base : base + 4]], axis=0)
            turned = turned.T
            for i in range(4):
                every = dot(turned[:, spans[i]], k[base + i][:, cols], 1, 0)
                picked = every[96:128]
                for head in (2, 1, 0):
                    picked = jnp.where(
                        lane < HEAD * (head + 1), every[head * HEAD : (head + 1) * HEAD], picked
                    )
                grad_q[base + i].append(picked * FACTOR)
    joined = [
        jnp.concatenate([*grad_q[i], grad_k[i], grad_v[i]], axis=1).astype(BF16)
        for i in range(count)
    ]
    return jnp.concatenate(joined, axis=0)


def axis_grads(tokens, cotangent, gain, w_qkv, w_out, scratch, strided):
    tokens_cols, cot_cols, grad_cols, joined_rows, normed_rows = scratch
    if strided:
        tokens_f, cot_f = tokens.astype(F32), cotangent.astype(F32)
        for col in range(2):
            tokens_cols[col] = tokens_f[:, col * LANES : (col + 1) * LANES]
            cot_cols[col] = cot_f[:, col * LANES : (col + 1) * LANES]
    dims = (WIDTH, WIDTH)
    block = (
        lax.broadcasted_iota(jnp.int32, dims, 0) // HEAD
        == lax.broadcasted_iota(jnp.int32, dims, 1) // HEAD
    )
    block = block.astype(F32).astype(BF16)
    lane = lax.broadcasted_iota(jnp.int32, (LENGTH, LANES), 1)
    for base in range(0, PENCILS, GROUP):
        group = slice(base * LENGTH, (base + GROUP) * LENGTH)
        if strided:
            rows_of = [pl.ds(base + i, LENGTH, stride=PENCILS) for i in range(GROUP)]

            def gathered(ref):
                cols = [
                    jnp.concatenate([ref[col, rows, :] for rows in rows_of], axis=0)
                    for col in range(2)
                ]
                return jnp.concatenate(cols, axis=1)

            tokens_f = gathered(tokens_cols)
            cot = gathered(cot_cols).astype(BF16)
        else:
            rows_of = [pl.ds((base + i) * LENGTH, LENGTH) for i in range(GROUP)]
            tokens_f = tokens[group].astype(F32)
            cot = cotangent[group]
        square = jnp.mean(tokens_f * tokens_f, axis=-1, keepdims=True) + EPSILON
        normed = (tokens_f * lax.rsqrt(square) * gain).astype(BF16)
        normed_rows[group] = normed
        qkv = dot(normed, w_qkv, 1, 0).astype(BF16)
        grad_attn = dot(cot, w_out, 1, 1).astype(BF16)
        joined = attention(qkv, grad_attn, block, lane, GROUP)
        joined_rows[group] = joined
        grad_normed = dot(joined, w_qkv, 1, 1)
        for i, rows in enumerate(rows_of):
            for col in range(2):
                grad_cols[col, rows, :] = grad_normed[spans_of(i), col * LANES : (col + 1) * LANES]
    part_qkv = dot(normed_rows[...], joined_rows[...], 0, 0)
    return jnp.concatenate([grad_cols[0], grad_cols[1]], axis=1), part_qkv


def spans_of(i):
    return slice(i * LENGTH, (i + 1) * LENGTH)


BITS = (1, 4, 8, 2)
SWAPS = (("z", 1, 8), ("z", 4, 8), ("xh", 1, 2), ("z", 2, 8))


def sources_before(stage):
    masks = [0]
    for bit in BITS[:stage]:
        masks += [mask ^ bit for mask in masks]
    return masks


def span_masks(count):
    masks = [0]
    for bit in reversed(BITS[4 - count :]):
        masks += [mask ^ bit for mask in masks]
    return masks


SPANS = [span_masks(count) for count in range(4)]

SCRATCH = [pltpu.VMEM((2, TOKENS, LANES), F32)] * 3 + [
    pltpu.VMEM((TOKENS, TRIPLE), BF16),
    pltpu.VMEM((TOKENS, WIDTH), BF16),
]


def along_second():
    return lax.axis_index("xl") * 2 + lax.axis_index("c")


def along_first():
    return lax.axis_index("xh") * 8 + lax.axis_index("z")


def pieces_kernel(tokens, cotangent, to_first, far, held, sem):
    core, chip = lax.axis_index("c"), lax.axis_index("xl")
    loads = [
        pltpu.make_async_copy(ref, held.at[kind], sem.at[kind])
        for kind, ref in enumerate((tokens, cotangent))
    ]
    for load in loads:
        load.start()
    for kind, load in enumerate(loads):
        load.wait()
        for x in range(2):
            for z in range(2):
                to_first[:, z, kind, x] = held[kind, x, :, z * ROWS : (z + 1) * ROWS, :]
        for other in range(2):
            rows = pl.ds(pl.multiple_of((core ^ other) * ROWS, ROWS), ROWS)
            far[other, kind] = held[kind, 1 - chip, :, rows, :]


def chip_pieces_kernel(tokens, cotangent, near, mate):
    core, chip = lax.axis_index("c"), lax.axis_index("xl")
    for other, out in enumerate((near, mate)):
        rows = pl.ds(pl.multiple_of((core ^ other) * ROWS, ROWS), ROWS)
        for kind, ref in enumerate((tokens, cotangent)):
            out[kind] = ref[chip, :, rows, :]


def third_kernel(
    tokens, cotangent, attn, gain, w_qkv, w_out, normed_out, qkv_out, out_out, *scratch
):
    cot = cotangent[...]
    grad_normed, part_qkv = axis_grads(
        tokens[...], cot, gain[...], w_qkv[...], w_out[...], scratch, False
    )
    normed_out[...] = grad_normed
    qkv_out[...] = part_qkv
    out_out[...] = dot(attn[...], cot, 0, 0)


def place_of(at):
    if at < 96:
        return divmod(at, QKV_TILES)
    half, tile = divmod(at - 96, TILES - QKV_TILES)
    return half, QKV_TILES + tile


def pack(total, part_out, halves, own, other):
    for at in range(2 * TILES):
        half, tile = place_of(at)
        if at < 96:
            row, col = divmod(at, 6)
            halves[half, tile] = total[row * 16 : row * 16 + 16, col * LANES : (col + 1) * LANES]
        elif part_out is None:
            continue
        else:
            row, col = divmod(at - 96, 2)
            halves[half, tile] = part_out[row * 16 : row * 16 + 16, col * LANES : (col + 1) * LANES]
    mine = lax.axis_index("c")
    count = other.shape[0]
    own[0:count] = halves[mine, 0:count].astype(own.dtype)
    other[...] = halves[1 - mine, 0:count].astype(BF16)


def second_kernel(*refs):
    pieces, (gain, w_qkv, w_out), parts = refs[:4], refs[4:7], refs[7:9]
    back, packed, scratch, halves = refs[9:13], refs[13:15], refs[15:-1], refs[-1]
    near, mate, far, passed = pieces
    pieces = (near, mate, far.at[0], passed.at[1])
    tokens = jnp.concatenate([piece[0].reshape(-1, WIDTH) for piece in pieces], axis=0)
    cot = jnp.concatenate([piece[1].reshape(-1, WIDTH) for piece in pieces], axis=0)
    grad_normed, part_qkv = axis_grads(
        tokens, cot, gain[...], w_qkv[...], w_out[...], scratch, True
    )
    returned = grad_normed.astype(BF16)
    rows = TOKENS // 4
    for mask, out in enumerate(back):
        out[...] = returned[mask * rows : (mask + 1) * rows].reshape(out.shape)
    third_qkv, part_out = parts
    pack(third_qkv[...] + part_qkv, part_out, halves, *packed)


def early_kernel(own, received, total):
    total[...] = (own[...].astype(F32) + received[...].astype(F32)).astype(BF16)


def first_kernel(pieces, early, gain, w_qkv, w_out, *refs):
    (stay, leave), packed, scratch, rest = refs[:2], refs[2:4], refs[4:-4], refs[-4:]
    returned, halves, held, sem = rest
    load = pltpu.make_async_copy(early, held, sem.at[0])
    load.start()
    tokens = pieces[:, 0].reshape(TOKENS, WIDTH)
    cot = pieces[:, 1].reshape(TOKENS, WIDTH)
    grad_normed, part_qkv = axis_grads(
        tokens, cot, gain[...], w_qkv[...], w_out[...], scratch, True
    )
    returned[...] = grad_normed.astype(BF16).reshape(returned.shape)
    here = along_first()
    for at, mask in enumerate(SPANS[3]):
        stay[at] = returned[here ^ mask]
        leave[at] = returned[here ^ mask ^ BITS[0]]
    pack(part_qkv, None, halves, *packed)
    load.wait()
    own = packed[0]
    own[0:QKV_TILES] += held[0:QKV_TILES].astype(F32)
    own[QKV_TILES:TILES] = held[QKV_TILES:TILES].astype(F32)


def stage_kernel(*refs):
    groups, out = refs[:-1], refs[-1]
    left = 16 >> (len(groups) - 1)
    at = 0
    for order, ref in enumerate(groups):
        span = 8 >> max(order - 1, 0)
        for base in range(0, 8, span):
            for block in range(left // 2, left):
                out[at] = ref[base + block]
                at += 1


def pair_kernel(own, received, pieces):
    for peer in range(16):
        tiles = slice(peer * 4, peer * 4 + 4)
        total = own[tiles]
        if tiles.stop <= QKV_TILES:
            total = total + received[tiles].astype(F32)
        pieces[peer] = total.astype(BF16)


def plane_kernel(received, pieces):
    total = jnp.sum(received[...].astype(F32), axis=0).astype(BF16)
    for peer in range(8):
        pieces[peer] = total


def line_kernel(scale, received, pieces):
    total = (jnp.sum(received[...].astype(F32), axis=0) * scale).astype(BF16)
    for peer in range(16):
        pieces[peer] = total


def assemble_kernel(mine, theirs, gain, w_qkv, w_qkv_out, w_out_out, gain_out, halves):
    at_core = lax.axis_index("c")
    halves[at_core] = mine[...]
    halves[1 - at_core] = theirs[...]
    for at in range(2 * TILES):
        half, tile = place_of(at)
        rows = halves[half, tile].astype(F32)
        if at < 96:
            row, col = divmod(at, 6)
            w_qkv_out[row * 16 : row * 16 + 16, col * LANES : (col + 1) * LANES] = rows
        else:
            row, col = divmod(at - 96, 2)
            w_out_out[row * 16 : row * 16 + 16, col * LANES : (col + 1) * LANES] = rows
    products = jnp.zeros((WIDTH, LANES), F32)
    for col in range(6):
        cols = slice(col * LANES, (col + 1) * LANES)
        products = products + w_qkv_out[:, cols] * w_qkv[:, cols].astype(F32)
    ones = jnp.ones((8, LANES), BF16)
    high = products.astype(BF16)
    low = (products - high.astype(F32)).astype(BF16)
    total = dot(ones, high, 1, 1) + dot(ones, low, 1, 1)
    gain_out[...] = total[0:1] / gain[...]


def tokens_kernel(tokens, gain, third, *rest):
    groups, seconds = rest[:5], rest[5:9]
    out, from_first, from_second = rest[9:]
    here = along_first()
    from_first[here] = groups[0][0]
    for stage in range(4):
        span = 8 >> stage
        for at, mask in enumerate(sources_before(stage)):
            from_first[here ^ (mask ^ BITS[stage])] = groups[stage + 1][at * span]
    for mask, ref in enumerate(seconds):
        from_second[along_second() ^ mask] = ref[...]
    for x in range(2):
        for y in range(8):
            tokens_f = tokens[x, y].astype(F32)
            first = jnp.concatenate([from_first[y * 2, x], from_first[y * 2 + 1, x]], axis=0)
            second = jnp.concatenate([from_second[x * 2, y], from_second[x * 2 + 1, y]], axis=0)
            grad_normed = third[x, y] + first.astype(F32) + second.astype(F32)
            square = jnp.mean(tokens_f * tokens_f, axis=-1, keepdims=True) + EPSILON
            inverse = lax.rsqrt(square)
            gained = gain[...] * grad_normed
            inner = jnp.sum(gained * tokens_f, axis=-1, keepdims=True)
            result = gained * inverse - tokens_f * (inner * inverse / (WIDTH * square))
            out[x, y] = result.astype(BF16)


def shape(dims, dtype):
    return jax.ShapeDtypeStruct(dims, dtype)


def kernel_call(body, outs, operands, us, scratch=(), space=VMEM, spaces=None, out_spaces=None):
    return pl.pallas_call(
        body,
        out_shape=outs,
        in_specs=spaces or [space] * len(operands),
        out_specs=out_spaces or jax.tree.map(lambda _: space, outs),
        scratch_shapes=list(scratch),
        compiler_params=params(62 if space is HBM else 48),
        cost_estimate=cost(us),
    )(*operands)


def swap(array, axis, mask, size):
    return lax.ppermute(array, axis, [(i, i ^ mask) for i in range(size)])


def exchange(pieces, axes):
    return lax.all_to_all(pieces, axes, split_axis=0, concat_axis=0, tiled=True)


def on_device(count, tokens, attn, cotangent, gain, w_qkv, w_out):
    gain_row = gain.reshape(1, WIDTH)
    local = tokens[0]
    upstream = cotangent[0]
    flat = (TOKENS, WIDTH)
    tile = (16, LANES)
    quarter = (2, 8, ROWS, WIDTH)
    to_first, far = kernel_call(
        pieces_kernel,
        (shape((8, 2, 2, 2, ROWS, WIDTH), BF16), shape((2, *quarter), BF16)),
        (local, upstream),
        2,
        [pltpu.VMEM((2, *local.shape), BF16), pltpu.SemaphoreType.DMA((2,))],
        space=HBM,
        out_spaces=(VMEM, VMEM),
    )
    at_first = exchange(to_first.reshape(16, 2, 2, ROWS, WIDTH), FIRST)
    far = swap(far, "xl", 1, 2)
    near, mate = kernel_call(
        chip_pieces_kernel, (shape(quarter, BF16),) * 2, (local, upstream), 1
    )
    far, mate = lax.optimization_barrier((far, mate))
    at_second = [near, swap(mate, "c", 1, 2), far, swap(far, "c", 1, 2)]
    third, third_qkv, part_out = kernel_call(
        third_kernel,
        (shape(flat, F32), shape((WIDTH, TRIPLE), F32), shape((WIDTH, WIDTH), F32)),
        (local.reshape(flat), upstream.reshape(flat), attn.reshape(flat), gain_row, w_qkv, w_out),
        5,
        SCRATCH,
    )
    packed = (
        shape((TILES, *tile), BF16),
        shape((TILES, *tile), BF16),
    )
    halves = pltpu.VMEM((2, TILES, *tile), F32)
    *back, own, other = kernel_call(
        second_kernel,
        (shape((8, ROWS, WIDTH), BF16),) * 4 + packed,
        (*at_second, gain_row, w_qkv, w_out, third_qkv, part_out),
        5,
        SCRATCH + [halves],
    )
    from_second = [back[0]] + [swap(back[m], SECOND, m, 4) for m in (1, 2, 3)]
    early = kernel_call(
        early_kernel, shape((TILES, *tile), BF16), (own, swap(other, "c", 1, 2)), 1
    )
    block = (2, ROWS, WIDTH)
    stay, leave, own, other = kernel_call(
        first_kernel,
        (
            shape((8, *block), BF16),
            shape((8, *block), BF16),
            shape((TILES, *tile), F32),
            shape((QKV_TILES, *tile), BF16),
        ),
        (at_first, early, gain_row, w_qkv, w_out),
        5,
        SCRATCH
        + [
            pltpu.VMEM((16, *block), BF16),
            halves,
            pltpu.VMEM((TILES, *tile), BF16),
            pltpu.SemaphoreType.DMA((1,)),
        ],
        spaces=[VMEM, HBM] + [VMEM] * 3,
    )
    other, from_second = lax.optimization_barrier((other, from_second))
    late = [own, swap(other, "c", 1, 2)]
    groups = [stay, swap(leave, *SWAPS[0])]
    for stage in (1, 2, 3):
        leave = kernel_call(stage_kernel, shape((8, *block), BF16), groups, 20)
        groups.append(swap(leave, *SWAPS[stage]))
    pieces = kernel_call(pair_kernel, shape((16, 4, *tile), BF16), late, 1)
    summed = exchange(pieces, PLANE)
    pieces = kernel_call(plane_kernel, shape((8, 4, *tile), BF16), (summed,), 1)
    summed = exchange(pieces, "z")
    pieces = kernel_call(
        functools.partial(line_kernel, 1.0 / math.sqrt(count)),
        shape((16, 4, *tile), BF16),
        (summed,),
        1,
    )
    mine = exchange(pieces, PLANE)
    mine = mine.reshape(TILES, *tile)
    theirs = swap(mine, "c", 1, 2)
    d_w_qkv, d_w_out, d_gain = kernel_call(
        assemble_kernel,
        (
            shape((WIDTH, TRIPLE), F32),
            shape((WIDTH, WIDTH), F32),
            shape((1, WIDTH), F32),
        ),
        (mine, theirs, gain_row, w_qkv),
        1,
        [pltpu.VMEM((2, TILES, *tile), BF16)],
    )
    d_tokens = kernel_call(
        tokens_kernel,
        shape(local.shape, BF16),
        (local, gain_row, third.reshape(local.shape), *groups, *from_second),
        2,
        [pltpu.VMEM((16, *block), BF16), pltpu.VMEM((4, 8, ROWS, WIDTH), BF16)],
    )
    return (d_tokens[None], d_w_qkv, d_w_out, d_gain.reshape(WIDTH))


def solution(mesh):
    fine = Mesh(mesh.devices.reshape(4, 8, 2, 2, 2), ("y", "z", "xh", "xl", "c"))
    split = P("y", ("z", "xh"), SECOND, None, None)
    count = 4 * 32 * 32 * 32
    return jax.shard_map(
        functools.partial(on_device, count),
        mesh=fine,
        in_specs=(split, split, split, P(), P(), P()),
        out_specs=(split, P(), P(), P()),
        check_vma=False,
    )
```
